32 devices in a mesh: seq: 16 (over z, y, x), wshard: 2 (over core).
Axes of the slice: x: 2, y: 2, z: 4, core: 2. Of those that a mesh axis runs over, the one named last changes fastest.
Arguments:
- inputs: bfloat16 [2, 4096, 1792], P('wshard', 'seq'), may hold values from -6 to 6
- starts: int32 [2, 16], P('wshard', 'seq'), may hold values from 0 to 1, as said below
- attn_gain: bfloat16 [1792], P(('seq', 'wshard')), may hold values from 0.5 to 1.5
- query_weight: bfloat16 [1792, 1792], P(('seq', 'wshard')), may hold values from -0.125 to 0.125
- key_weight: bfloat16 [1792, 1792], P(('seq', 'wshard')), may hold values from -0.125 to 0.125
- value_weight: bfloat16 [1792, 1792], P(('seq', 'wshard')), may hold values from -0.125 to 0.125
- out_weight: bfloat16 [1792, 1792], P(('seq', 'wshard')), may hold values from -1 to 1
- ffn_gain: bfloat16 [1792], P(('seq', 'wshard')), may hold values from 0.5 to 1.5
- gate_weight: bfloat16 [1792, 4864], P(('seq', 'wshard')), may hold values from -0.125 to 0.125
- up_weight: bfloat16 [1792, 4864], P(('seq', 'wshard')), may hold values from -0.125 to 0.125
- down_weight: bfloat16 [4864, 1792], P(('seq', 'wshard')), may hold values from -0.078125 to 0.078125
- cotangent: bfloat16 [2, 4096, 1792], P('wshard', 'seq'), may hold values from -6 to 6
Outputs:
- layer_out: bfloat16 [2, 4096, 1792], P('wshard', 'seq')
- input_grad: float32 [2, 4096, 1792], P('wshard', 'seq')
- attn_gain_grad: float32 [1792], P(('seq', 'wshard'))
- query_grad: float32 [1792, 1792], P(('seq', 'wshard'))
- key_grad: float32 [1792, 1792], P(('seq', 'wshard'))
- value_grad: float32 [1792, 1792], P(('seq', 'wshard'))
- output_grad: float32 [1792, 1792], P(('seq', 'wshard'))
- ffn_gain_grad: float32 [1792], P(('seq', 'wshard'))
- gate_grad: float32 [1792, 4864], P(('seq', 'wshard'))
- up_grad: float32 [1792, 4864], P(('seq', 'wshard'))
- down_grad: float32 [4864, 1792], P(('seq', 'wshard'))
The draws below stay inside these ranges and needn't reach their ends.
Inputs may be any that keep to these rules, and one draw needn't show every extreme that they name: starts[w, 0] is 1 in every stream; other ones stand only at block numbers that are multiples of 4; in one stream, drawn from the seed, starts[w, 0] is the only 1, so one sequence covers all its blocks.
All inputs are finite; a program needn't handle non-finite values.
Results may differ from the reference program's by a relative error of at most 0.014.
Values may be sent and summed in bfloat16 or wider, within the bound.
No kernel may reach another device: no remote copies, remote signals or barrier semaphores. Data moves between devices by JAX's collectives and lax.ppermute only.
A program may use at most 576 MiB of HBM per device.

```python
import jax
import jax.numpy as jnp
from jax import lax

D = 1792
H = 16
HD = 112
FF = 4864
WINDOW = 64
TOK_DEV = 256
SPAN_CH = 4
STREAMS = 2
STREAM = 4096
N_SEQ = 16


def draw_starts(key, part):
    key = jax.random.fold_in(key, 11)
    pick_key, coin_key = jax.random.split(key)
    whole_row = jax.random.randint(pick_key, (), 0, STREAMS)
    coins = jax.random.randint(coin_key, (STREAMS, N_SEQ), 0, 2)
    place = jnp.arange(N_SEQ)[None, :]
    row_ids = jnp.arange(STREAMS)[:, None]
    opened = jnp.where(place % SPAN_CH == 0, coins, 0)
    opened = jnp.where(place == 0, 1, opened)
    single = jnp.where(place == 0, 1, 0) + 0 * row_ids
    return jnp.where(row_ids == whole_row, single, opened).astype(jnp.int32)


def with_spikes(values, rng, source, target, blocks, factor):
    owner, partner = [(jnp.arange(values.shape[dim]) // (values.shape[dim] // blocks)).reshape([-1 if axis == dim else 1 for axis in range(values.ndim)]) for dim in (source, target)]
    chosen = jax.random.permutation(rng, blocks)[partner]
    strong = (owner == chosen) | (owner == (partner + blocks // 2) % blocks)
    return jnp.where(strong, factor * values, values)


def block_scale(stream_key, dims, cuts, smallest, high):
    factor_of = 1.0
    for dim, parts in cuts:
        draws = jax.random.uniform(jax.random.fold_in(jax.random.fold_in(stream_key, 6), dim), (parts,), jnp.float32, smallest / len(cuts), high / len(cuts))
        factor_of = factor_of * jnp.repeat(jnp.exp(draws), dims[dim] // parts).reshape((-1,) + (1,) * (len(dims) - 1 - dim))
    return factor_of


def centred(stream_key, extent, deviation, reach, cuts=(), held_as=jnp.bfloat16):
    entries = deviation * jax.random.normal(stream_key, extent, jnp.float32)
    if cuts:
        entries = entries * block_scale(stream_key, extent, cuts, -0.22, 0.18)
    return jnp.clip(entries, -reach, reach).astype(held_as)


def heavy_noise(own_key, extent, scale, reach, shards, heavy, kind=jnp.bfloat16):
    drawn = scale * jax.random.normal(own_key, extent, jnp.float32)
    if shards:
        drawn = drawn * block_scale(own_key, extent, shards, -0.22, 0.18)
    return jnp.clip(with_spikes(drawn, jax.random.fold_in(own_key, 3), *heavy), -reach, reach).astype(kind)


def setup_inputs(seed: int = 0) -> dict:
    splits = jax.random.split(jax.random.key(seed), 13)
    inputs = heavy_noise(splits[0], (STREAMS, STREAM, D), 1.0, 6.0, ((0, 2), (1, 16)), (1, 2, 16, 2.0))
    starts = draw_starts(jax.random.fold_in(splits[12], 71), 0)
    attn_gain = jnp.clip(1.0 + 0.1 * jax.random.normal(splits[2], (D,), jnp.float32), 0.5, 1.5).astype(jnp.bfloat16)
    query_weight = centred(splits[3], (D, D), D ** -0.5, 0.125, ((0, 32),))
    key_weight = centred(splits[4], (D, D), D ** -0.5, 0.125, ((0, 32),))
    value_weight = centred(splits[5], (D, D), D ** -0.5, 0.125, ((0, 32),))
    out_weight = centred(splits[6], (D, D), (D // 64) ** -0.5, 1.0, ((0, 32),))
    ffn_gain = jnp.clip(1.0 + 0.1 * jax.random.normal(splits[7], (D,), jnp.float32), 0.5, 1.5).astype(jnp.bfloat16)
    gate_weight = centred(splits[8], (D, FF), D ** -0.5, 0.125, ((0, 32),))
    up_weight = centred(splits[9], (D, FF), D ** -0.5, 0.125, ((0, 32),))
    down_weight = centred(splits[10], (FF, D), FF ** -0.5, 0.078125, ((0, 32),))
    cotangent = centred(splits[11], (STREAMS, STREAM, D), 1.0, 6.0, ((0, 2), (1, 16)))
    return dict(inputs=inputs, starts=starts, attn_gain=attn_gain, query_weight=query_weight, key_weight=key_weight, value_weight=value_weight, out_weight=out_weight, ffn_gain=ffn_gain, gate_weight=gate_weight, up_weight=up_weight, down_weight=down_weight, cotangent=cotangent)


EPS = 1e-06
MASKED = -1e+30

@jax.custom_vjp
def low(v):
    return lax.optimization_barrier(v.astype(jnp.bfloat16)).astype(jnp.float32)

@jax.custom_vjp
def low_back(v):
    return v

def low_keep(v):
    return (low(v), None)

def low_pass(kept, grad):
    return (grad,)

def back_keep(v):
    return (v, None)

def back_low(kept, grad):
    return (low(grad),)
low.defvjp(low_keep, low_pass)
low_back.defvjp(back_keep, back_low)

def highdot(left, right):
    return jnp.dot(left, right, precision=lax.Precision.HIGHEST, preferred_element_type=jnp.float32)

def normalize(values):
    return values * lax.rsqrt(lax.optimization_barrier(jnp.mean(values * values, axis=-1, keepdims=True)) + EPS)

def windows(stream, before, after):
    joined = jnp.concatenate([before, stream, after], axis=0)
    blocks = joined.reshape((-1, WINDOW) + stream.shape[1:])
    return jnp.concatenate([blocks[:-1], blocks[1:]], axis=1)

def attend(query, keys, values, seq_ids):
    length = query.shape[0]
    count = length // WINDOW
    before = jnp.zeros((WINDOW - 1, D), jnp.float32)
    after = jnp.zeros((1, D), jnp.float32)
    key_blocks = windows(keys, before, after).reshape(count, 2 * WINDOW, H, HD)
    value_blocks = windows(values, before, after).reshape(count, 2 * WINDOW, H, HD)
    query_blocks = query.reshape(count, WINDOW, H, HD)
    id_blocks = windows(seq_ids, jnp.full((WINDOW - 1,), -1, jnp.int32), jnp.full((1,), -2, jnp.int32))
    query_ids = seq_ids.reshape(count, WINDOW)
    rowpos = jnp.arange(WINDOW)[:, None]
    colpos = jnp.arange(2 * WINDOW)[None, :]
    band = (colpos >= rowpos) & (colpos <= rowpos + WINDOW - 1)
    valid = band[None, None] & (query_ids[:, None, :, None] == id_blocks[:, None, None, :])
    raw = low_back(jnp.einsum('bqhd,bkhd->bhqk', query_blocks, key_blocks, precision=lax.Precision.HIGHEST))
    scores = jnp.where(valid, raw * HD ** (-0.5), MASKED)
    peak = lax.optimization_barrier(jnp.max(scores, axis=-1, keepdims=True))
    powers = jnp.exp(scores - peak)
    shares = low(powers / lax.optimization_barrier(jnp.sum(powers, axis=-1, keepdims=True)))
    mixed = jnp.einsum('bhqk,bkhd->bqhd', shares, value_blocks, precision=lax.Precision.HIGHEST)
    return mixed.reshape(length, D)

def layer(stream, seq_ids, attn_gain, query_weight, key_weight, value_weight, out_weight, ffn_gain, gate_weight, up_weight, down_weight):
    hidden1 = low(normalize(stream) * attn_gain)
    query = low_back(low(highdot(hidden1, query_weight)))
    keys = low_back(low(highdot(hidden1, key_weight)))
    values = low_back(low(highdot(hidden1, value_weight)))
    mixed = low_back(low(attend(query, keys, values, seq_ids)))
    middle = stream + low_back(highdot(mixed, out_weight))
    hidden2 = low(normalize(middle) * ffn_gain)
    gate = low_back(highdot(hidden2, gate_weight))
    upper = low_back(highdot(hidden2, up_weight))
    inner = low(jax.nn.silu(gate) * upper)
    return middle + low_back(highdot(inner, down_weight))

def reference(inputs, starts, attn_gain, query_weight, key_weight, value_weight, out_weight, ffn_gain, gate_weight, up_weight, down_weight, cotangent):
    seq_ids = jnp.repeat(jnp.cumsum(starts, axis=1).astype(jnp.int32), TOK_DEV, axis=1)
    params = (attn_gain.astype(jnp.float32), query_weight.astype(jnp.float32), key_weight.astype(jnp.float32), value_weight.astype(jnp.float32), out_weight.astype(jnp.float32), ffn_gain.astype(jnp.float32), gate_weight.astype(jnp.float32), up_weight.astype(jnp.float32), down_weight.astype(jnp.float32))

    def forward(streams, attn_g, query_w, key_w, value_w, out_w, ffn_g, gate_w, up_w, down_w):

        def one_stream(stream, ids):
            return layer(stream, ids, attn_g, query_w, key_w, value_w, out_w, ffn_g, gate_w, up_w, down_w)
        return jax.vmap(one_stream)(streams, seq_ids)
    result, pullback = jax.vjp(forward, inputs.astype(jnp.float32), *params)
    grads = pullback(cotangent.astype(jnp.float32))
    return (result.astype(jnp.bfloat16), grads[0], grads[1], grads[2], grads[3], grads[4], grads[5], grads[6], grads[7], grads[8], grads[9])
```

```python
import functools

import jax
import jax.numpy as jnp
from jax import lax
from jax.experimental import pallas as pl
from jax.experimental.pallas import tpu as pltpu
from jax.sharding import Mesh, PartitionSpec as P

H = 16
HD = 112
HP = 128
WINDOW = 64
EPS = 1e-06
MASKED = -1e30
SUB = 128
SPAN = SUB + WINDOW

BF = jnp.bfloat16
F32 = jnp.float32
ALL = ("z", "y", "x", "c")
PLANE = ("y", "x", "c")
SWAP = [(0, 1), (1, 0)]
NT = (((1,), (1,)), ((), ()))
TN = (((0,), (0,)), ((), ()))


def swap(block, axis):
    return lax.ppermute(block, axis, SWAP)


def normalize(values):
    factor = lax.rsqrt(jnp.mean(values * values, axis=-1, keepdims=True) + EPS)
    return (values * factor, factor)


def norm_back(grad_normed, normed_rows, factor):
    return factor * (
        grad_normed - normed_rows * jnp.mean(grad_normed * normed_rows, axis=-1, keepdims=True)
    )


def dot(left, right, dims=(((1,), (0,)), ((), ()))):
    return lax.dot_general(left, right, dims, preferred_element_type=F32)


def plane_gather(own):
    half = own.shape[0] // 2
    from_x = swap(own, "x")
    from_y = swap(own, "y")
    first = swap(from_y[:half], "x")
    second = swap(from_x[half:], "y")
    mine = [own, from_x, from_y, jnp.concatenate([first, second], axis=0)]
    other = [swap(block, "c") for block in mine]
    return jnp.stack([block for pair in zip(mine, other) for block in pair])


def plane_sum(parts):
    half = parts[0][0].shape[0] // 2
    met = [parts[r][0].astype(F32) + swap(parts[r][1], "c").astype(F32) for r in (3, 2, 1, 0)]
    far, along_y, along_x, here = met
    far = far.astype(BF)
    first = swap(far[:half], "x")
    second = swap(far[half:], "y")
    along_y = jnp.concatenate([along_y[:half] + first.astype(F32), along_y[half:]], axis=0)
    along_x = jnp.concatenate([along_x[:half], along_x[half:] + second.astype(F32)], axis=0)
    got_x = swap(along_x.astype(BF), "x")
    got_y = swap(along_y.astype(BF), "y")
    return here + got_x.astype(F32) + got_y.astype(F32)


def ring_gather(block, count):
    route = [(i, (i + 1) % count) for i in range(count)]
    held = [block]
    for _ in range(count - 1):
        held.append(lax.ppermute(held[-1], "z", route))
    me = lax.axis_index("z")
    stacked = jnp.stack(held[::-1])
    return jnp.roll(stacked, me + 1, axis=0)


def shares_of(query, keys, cut, offset):
    raw = lax.dot_general(query, keys, NT, preferred_element_type=F32)
    row = lax.broadcasted_iota(jnp.int32, raw.shape, 0)
    col = lax.broadcasted_iota(jnp.int32, raw.shape, 1)
    valid = (col > row) & (col <= row + WINDOW)
    if offset == 0:
        valid = valid & (col >= cut)
    scores = jnp.where(valid, raw * (HD ** (-0.5)), MASKED)
    peak = jnp.max(scores, axis=-1, keepdims=True)
    powers = jnp.exp(scores - peak)
    return powers / jnp.sum(powers, axis=-1, keepdims=True)


def joined(prev_ref, halo_ref, cur_ref, at_first, lo):
    before = jnp.where(
        at_first, halo_ref[:, lo - 2 * HP : lo - HP], prev_ref[:, lo : lo + HP]
    )
    return jnp.concatenate([before, cur_ref[:, lo : lo + HP]], axis=0)


def attend_kernel(info_ref, cur_ref, prev_ref, halo_ref, flat_ref, kept_ref):
    stream, block = pl.program_id(0), pl.program_id(1)
    at_first = block == 0
    cut = jnp.where(at_first & (info_ref[2 + stream] == 1), WINDOW, 0)
    rows = cur_ref.shape[0]
    for h in range(2):
        keys = joined(prev_ref, halo_ref, cur_ref, at_first, (2 + h) * HP)
        values = joined(prev_ref, halo_ref, cur_ref, at_first, (4 + h) * HP)
        for at in range(0, rows, SUB):
            query = cur_ref[at : at + SUB, h * HP : (h + 1) * HP]
            shares = shares_of(query, keys[at : at + SPAN], cut, at)
            mixed = jnp.dot(
                shares.astype(BF), values[at : at + SPAN], preferred_element_type=F32
            ).astype(BF)
            flat_ref[at : at + SUB, h * HP : (h + 1) * HP] = mixed
            kept_ref[at : at + SUB, h * HP : (h + 1) * HP] = mixed


def attend(qkv, halo, info):
    rows, blocks = qkv.shape[1], qkv.shape[0] // 2
    mine = lambda s, b, info: (2 * (b ^ info[0]) + s, 0, 0)
    before = lambda s, b, info: (2 * (jnp.maximum(b - 1, 0) ^ info[0]) + s, rows // WINDOW - 1, 0)
    spec = pltpu.PrefetchScalarGridSpec(
        num_scalar_prefetch=1,
        grid=(2, blocks),
        in_specs=[
            pl.BlockSpec((None, rows, 6 * HP), mine),
            pl.BlockSpec((None, WINDOW, 6 * HP), before),
            pl.BlockSpec((None, WINDOW, 4 * HP), lambda s, b, info: (s, 0, 0)),
        ],
        out_specs=[
            pl.BlockSpec((None, rows, 2 * HP), lambda s, b, info: (2 * b + (s ^ info[1]), 0, 0)),
            pl.BlockSpec((None, rows, 2 * HP), mine),
        ],
    )
    shape = jax.ShapeDtypeStruct((2 * blocks, rows, 2 * HP), BF)
    return pl.pallas_call(
        attend_kernel,
        grid_spec=spec,
        out_shape=[shape, shape],
        compiler_params=pltpu.CompilerParams(vmem_limit_bytes=32 * 2**20),
    )(info, qkv, qkv, halo)


def attend_back_kernel(
    info_ref, cur_ref, prev_ref, halo_ref, top_ref, out_ref, tail_ref, lead_ref, keep, acc
):
    stream, step = pl.program_id(0), pl.program_id(1)
    blocks = pl.num_programs(1)
    at_first = step == blocks - 1
    cut = jnp.where(at_first & (info_ref[2 + stream] == 1), WINDOW, 0)
    rows = cur_ref.shape[0]

    @pl.when(step == 0)
    def _():
        keep[...] = jnp.zeros_like(keep)

    acc[...] = jnp.zeros_like(acc)
    for h in range(2):
        lo, hi = h * HP, (h + 1) * HP
        keys = joined(prev_ref, halo_ref, cur_ref, at_first, (2 + h) * HP)
        values = joined(prev_ref, halo_ref, cur_ref, at_first, (4 + h) * HP)
        for at in range(0, rows, SUB):
            query = cur_ref[at : at + SUB, lo:hi]
            top = top_ref[at : at + SUB, lo:hi]
            key = keys[at : at + SPAN]
            shares = shares_of(query, key, cut, at)
            grad_shares = lax.dot_general(
                top, values[at : at + SPAN], NT, preferred_element_type=F32
            )
            grad_raw = (
                shares
                * (grad_shares - jnp.sum(shares * grad_shares, axis=-1, keepdims=True))
                * (HD ** (-0.5))
            ).astype(BF)
            out_ref[at : at + SUB, lo:hi] = jnp.dot(
                grad_raw, key, preferred_element_type=F32
            ).astype(BF)
            acc[at : at + SPAN, lo:hi] += lax.dot_general(
                grad_raw, query, TN, preferred_element_type=F32
            )
            acc[at : at + SPAN, 2 * HP + lo : 2 * HP + hi] += lax.dot_general(
                shares.astype(BF), top, TN, preferred_element_type=F32
            )
    last = acc[rows : rows + WINDOW, :] + keep[...]
    out_ref[: rows - WINDOW, 2 * HP :] = acc[WINDOW:rows, :].astype(BF)
    out_ref[rows - WINDOW :, 2 * HP :] = last.astype(BF)
    keep[...] = acc[:WINDOW, :]

    @pl.when(step == 0)
    def _():
        tail_ref[...] = last

    @pl.when(at_first)
    def _():
        lead_ref[...] = acc[:WINDOW, :].astype(BF)


def attend_back(qkv, halo, top, info):
    rows, blocks = qkv.shape[1], qkv.shape[0] // 2
    at = lambda t: blocks - 1 - t
    mine = lambda s, t, info: (2 * (at(t) ^ info[0]) + s, 0, 0)
    before = lambda s, t, info: (
        2 * (jnp.maximum(at(t) - 1, 0) ^ info[0]) + s,
        rows // WINDOW - 1,
        0,
    )
    side = lambda s, t, info: (s, 0, 0)
    spec = pltpu.PrefetchScalarGridSpec(
        num_scalar_prefetch=1,
        grid=(2, blocks),
        in_specs=[
            pl.BlockSpec((None, rows, 6 * HP), mine),
            pl.BlockSpec((None, WINDOW, 6 * HP), before),
            pl.BlockSpec((None, WINDOW, 4 * HP), side),
            pl.BlockSpec(
                (None, rows, 2 * HP), lambda s, t, info: (2 * at(t) + (s ^ info[1]), 0, 0)
            ),
        ],
        out_specs=[
            pl.BlockSpec((None, rows, 6 * HP), mine),
            pl.BlockSpec((None, WINDOW, 4 * HP), side),
            pl.BlockSpec((None, WINDOW, 4 * HP), side),
        ],
        scratch_shapes=[
            pltpu.VMEM((WINDOW, 4 * HP), F32),
            pltpu.VMEM((rows + WINDOW, 4 * HP), F32),
        ],
    )
    return pl.pallas_call(
        attend_back_kernel,
        grid_spec=spec,
        out_shape=[
            jax.ShapeDtypeStruct(qkv.shape, BF),
            jax.ShapeDtypeStruct(halo.shape, F32),
            jax.ShapeDtypeStruct(halo.shape, BF),
        ],
        compiler_params=pltpu.CompilerParams(vmem_limit_bytes=32 * 2**20),
    )(info, qkv, qkv, halo, top)


def padded_heads(block):
    rows = block.shape[0]
    wide = jnp.pad(block.reshape(rows, H, HD), ((0, 0), (0, 0), (0, HP - HD)))
    return wide.reshape(rows, 8, 2 * HP)


def body(
    inputs,
    starts,
    attn_gain,
    query_weight,
    key_weight,
    value_weight,
    out_weight,
    ffn_gain,
    gate_weight,
    up_weight,
    down_weight,
    cotangent,
):
    rows, width = inputs.shape[1:]
    layers = lax.axis_size("z")
    devices = 8 * layers
    share = query_weight.shape[0]
    hidden_units = gate_weight.shape[1]
    units = hidden_units // 8
    part = down_weight.shape[0]
    me_z = lax.axis_index("z")
    me_block = 2 * lax.axis_index("y") + lax.axis_index("x")
    me_core = lax.axis_index("c")

    streams = plane_gather(inputs[0])
    sheet = jnp.concatenate(
        [
            padded_heads(query_weight),
            padded_heads(key_weight),
            padded_heads(value_weight),
            gate_weight.reshape(share, layers, 8, part).swapaxes(1, 2).reshape(share, 8, units),
            up_weight.reshape(share, layers, 8, part).swapaxes(1, 2).reshape(share, 8, units),
        ],
        axis=2,
    ).swapaxes(0, 1)
    sheet = lax.all_to_all(sheet, PLANE, 0, 0, tiled=True).reshape(8 * share, -1)
    small = jnp.concatenate(
        [attn_gain, ffn_gain, starts[0].astype(BF)], axis=0
    )
    small = jnp.pad(small, (0, 128 - small.shape[0]))
    small = lax.all_to_all(jnp.broadcast_to(small, (devices, 128)), ALL, 0, 0, tiled=True)
    gain_attn = small[:, :share].reshape(width)
    gain_ffn = small[:, share : 2 * share].reshape(width)
    opened = lax.dynamic_slice(small, (8 * me_z, 2 * share), (2, 1))[:, 0].astype(jnp.int32)
    opened = jnp.where(me_core == 0, opened, opened[::-1])
    info = jnp.concatenate([jnp.stack([me_block, me_core]).astype(jnp.int32), opened])

    full_out = lax.all_gather(out_weight, ALL, axis=0, tiled=True)
    down = lax.all_gather(down_weight, "z", axis=0, tiled=True)
    qkv_weight = ring_gather(sheet[:, : 6 * HP], layers).reshape(width, 6 * HP)
    gate_up = lax.all_gather(sheet[:, 6 * HP :], "z", axis=0, tiled=True)
    tops = plane_gather(cotangent[0]).reshape(8 * rows, width)

    stream = streams.reshape(8 * rows, width).astype(F32)
    hidden1 = (normalize(stream)[0] * gain_attn).astype(BF)
    qkv = dot(hidden1, qkv_weight).astype(BF).reshape(8, rows, 6 * HP)
    last = 2 * (3 ^ me_block)
    rim = lax.dynamic_slice(
        qkv, (last, rows - WINDOW, 2 * HP), (2, WINDOW, 4 * HP)
    )
    halo = lax.ppermute(rim, "z", [(i, i + 1) for i in range(layers - 1)])
    flat, kept = attend(qkv, halo, info)
    mixed = lax.all_to_all(flat, PLANE, 0, 0, tiled=True)
    mixed = mixed.reshape(8, rows, 2, HP)[..., :HD].transpose(1, 0, 2, 3).reshape(rows, H * HD)
    middle = inputs[0].astype(F32) + dot(mixed, full_out)

    normed2, rscale2 = normalize(middle)
    hidden2 = plane_gather((normed2 * gain_ffn).astype(BF)).reshape(8 * rows, width)
    gate = dot(hidden2, gate_up[:, :units])
    upper = dot(hidden2, gate_up[:, units:])
    sigma = jax.nn.sigmoid(gate)
    activ = gate * sigma
    inner = (activ * upper).astype(BF)
    grad_inner = dot(tops, down, NT)
    grad_upper = (grad_inner * activ).astype(BF)
    grad_gate = (grad_inner * upper * sigma * (1.0 + gate * (1.0 - sigma))).astype(BF)
    parts = []
    for r in range(4):
        at = slice(2 * r * rows, 2 * (r + 1) * rows)
        part_sum = dot(grad_gate[at], gate_up[:, :units], NT) + dot(
            grad_upper[at], gate_up[:, units:], NT
        )
        part_sum = part_sum.astype(BF)
        parts.append((part_sum[:rows], part_sum[rows:]))
    grad_hidden2 = plane_sum(parts)
    down_sum = lax.psum_scatter(
        dot(inner, tops, TN).astype(BF), "z", scatter_dimension=0, tiled=True
    )
    gate_up_sum = lax.psum_scatter(
        jnp.concatenate([dot(hidden2, grad_gate, TN), dot(hidden2, grad_upper, TN)], axis=1).astype(BF),
        "z",
        scatter_dimension=0,
        tiled=True,
    )
    parts = []
    for r in range(4):
        at = slice(2 * r * rows, 2 * (r + 1) * rows)
        part_sum = dot(inner[at], down).astype(BF)
        parts.append((part_sum[:rows], part_sum[rows:]))
    layer_out = (middle + plane_sum(parts)).astype(BF)

    ffn_gain_local = jnp.sum(grad_hidden2 * normed2, axis=0)
    grad_middle = cotangent[0].astype(F32) + norm_back(grad_hidden2 * gain_ffn, normed2, rscale2)
    grad_branch = grad_middle.astype(BF)

    grad_mixed = padded_heads(dot(grad_branch, full_out, NT).astype(BF)).swapaxes(0, 1)
    grad_mixed = lax.all_to_all(grad_mixed, PLANE, 0, 0, tiled=True)
    branches = plane_gather(grad_branch).reshape(8 * rows, width)
    grad_qkv, tail, lead = attend_back(qkv, halo, grad_mixed, info)
    back = lax.ppermute(lead, "z", [(i + 1, i) for i in range(layers - 1)])
    grad_qkv = lax.dynamic_update_slice(
        grad_qkv, (tail + back.astype(F32)).astype(BF), (last, rows - WINDOW, 2 * HP)
    ).reshape(8 * rows, 6 * HP)
    parts = []
    for r in range(4):
        at = slice(2 * r * rows, 2 * (r + 1) * rows)
        part_sum = dot(grad_qkv[at], qkv_weight, NT).astype(BF)
        parts.append((part_sum[:rows], part_sum[rows:]))
    grad_hidden1 = plane_sum(parts)
    attn_sums = jnp.concatenate(
        [dot(hidden1, grad_qkv, TN), dot(branches, kept.reshape(8 * rows, 2 * HP), TN)], axis=1
    ).astype(BF)
    attn_sums = lax.psum_scatter(attn_sums, "z", scatter_dimension=0, tiled=True)
    normed1, rscale1 = normalize(inputs[0].astype(F32))
    attn_gain_local = jnp.sum(grad_hidden1 * normed1, axis=0)
    input_grad = grad_middle + norm_back(grad_hidden1 * gain_attn, normed1, rscale1)

    gate_up_sum = lax.all_to_all(
        gate_up_sum.reshape(8, share, 2 * units), PLANE, 0, 0, tiled=True
    ).astype(F32)
    gate_up_sum = gate_up_sum.reshape(8, share, 2, layers, part).transpose(2, 1, 3, 0, 4)
    gate_grad, up_grad = gate_up_sum.reshape(2, share, hidden_units)
    qkv_sum = lax.all_to_all(
        attn_sums[:, : 6 * HP].reshape(8, share, 6 * HP), PLANE, 0, 0, tiled=True
    ).astype(F32)
    qkv_sum = qkv_sum.reshape(8, share, 3, 2, HP)[..., :HD].transpose(2, 1, 0, 3, 4)
    query_grad, key_grad, value_grad = qkv_sum.reshape(3, share, width)
    out_sum = attn_sums[:, 6 * HP :].reshape(-1, 2, HP)[..., :HD].reshape(-1, layers, share)
    pieces = []
    for j in range(layers):
        route = [
            (8 * z + p, layers * p + (z + j) % layers) for z in range(layers) for p in range(8)
        ]
        piece = lax.dynamic_index_in_dim(out_sum, (me_z + j) % layers, axis=1, keepdims=False)
        pieces.append(lax.ppermute(piece, ALL, route))
    rank = 8 * me_z + 2 * me_block + me_core
    turned = jnp.roll(jnp.stack(pieces[::-1]), rank % layers + 1, axis=0)
    output_grad = turned.reshape(width, share).T.astype(F32)
    gains = jnp.stack([attn_gain_local, ffn_gain_local]).reshape(2, devices, share).swapaxes(0, 1)
    gains = jnp.sum(lax.all_to_all(gains, ALL, 0, 0, tiled=True), axis=0)
    return (
        layer_out[None],
        input_grad[None],
        gains[0],
        query_grad,
        key_grad,
        value_grad,
        output_grad,
        gains[1],
        gate_grad,
        up_grad,
        down_sum.astype(F32),
    )


def solution(mesh):
    blocks = mesh.shape["seq"]
    fine = Mesh(mesh.devices.reshape(blocks // 4, 2, 2, 2), ALL)
    tokens = P("c", ("z", "y", "x"), None)
    weight = P(ALL, None)
    gain = P(ALL)
    in_specs = (
        tokens,
        P("c", ("z", "y", "x")),
        gain,
        weight,
        weight,
        weight,
        weight,
        gain,
        weight,
        weight,
        weight,
        tokens,
    )
    out_specs = (
        tokens,
        tokens,
        gain,
        weight,
        weight,
        weight,
        weight,
        gain,
        weight,
        weight,
        weight,
    )
    return jax.shard_map(body, mesh=fine, in_specs=in_specs, out_specs=out_specs, check_vma=False)
```

```python
import functools

import jax
import jax.numpy as jnp
from jax import lax
from jax.experimental import pallas as pl
from jax.experimental.pallas import tpu as pltpu
from jax.sharding import Mesh, PartitionSpec as P

H = 16
HD = 112
HP = 128
WINDOW = 64
EPS = 1e-06
MASKED = -1e30
SUB = 128
SPAN = SUB + WINDOW

BF = jnp.bfloat16
F32 = jnp.float32
ALL = ("z", "y", "x", "c")
PLANE = ("y", "x", "c")
SWAP = [(0, 1), (1, 0)]
NT = (((1,), (1,)), ((), ()))
TN = (((0,), (0,)), ((), ()))


def swap(block, axis):
    return lax.ppermute(block, axis, SWAP)


def normalize(values):
    factor = lax.rsqrt(jnp.mean(values * values, axis=-1, keepdims=True) + EPS)
    return (values * factor, factor)


def norm_back(grad_normed, normed_rows, factor):
    return factor * (
        grad_normed - normed_rows * jnp.mean(grad_normed * normed_rows, axis=-1, keepdims=True)
    )


def dot(left, right, dims=(((1,), (0,)), ((), ()))):
    return lax.dot_general(left, right, dims, preferred_element_type=F32)


def after(value, *others):
    return lax.optimization_barrier((value, *others))[0]


def plane_gather(own):
    half = own.shape[0] // 2
    from_x = swap(own, "x")
    from_y = swap(own, "y")
    first = swap(from_y[:half], "x")
    second = swap(from_x[half:], "y")
    mine = [own, from_x, from_y, jnp.concatenate([first, second], axis=0)]
    other = [swap(block, "c") for block in mine]
    return [block for pair in zip(mine, other) for block in pair]


def plane_sum(parts):
    half = parts[0][0].shape[0] // 2
    met = [parts[r][0].astype(F32) + swap(parts[r][1], "c").astype(F32) for r in (3, 2, 1, 0)]
    far, along_y, along_x, here = met
    far = far.astype(BF)
    first = swap(far[:half], "x")
    second = swap(far[half:], "y")
    along_y = jnp.concatenate([along_y[:half] + first.astype(F32), along_y[half:]], axis=0)
    along_x = jnp.concatenate([along_x[:half], along_x[half:] + second.astype(F32)], axis=0)
    got_x = swap(along_x.astype(BF), "x")
    got_y = swap(along_y.astype(BF), "y")
    return here, got_x, got_y


def total(terms):
    here, got_x, got_y = terms
    return here + got_x.astype(F32) + got_y.astype(F32)


def placed(pieces):
    count = len(pieces)
    me = lax.axis_index("z")
    whole = jnp.zeros((count, *pieces[0].shape), pieces[0].dtype)
    for k, piece in enumerate(pieces):
        whole = lax.dynamic_update_index_in_dim(whole, piece, (me - k) % count, 0)
    return whole.reshape(-1, *pieces[0].shape[1:])


def ring_gather(block, count):
    route = [(i, (i + 1) % count) for i in range(count)]
    held = [block]
    for _ in range(count - 1):
        held.append(lax.ppermute(held[-1], "z", route))
    return held


def direct_gather(block, count):
    return [block] + [
        lax.ppermute(block, "z", [(i, (i + k) % count) for i in range(count)])
        for k in range(1, count)
    ]


def head_sheet_kernel(query_ref, key_ref, value_ref, out_ref):
    rows = query_ref.shape[0]
    blank = jnp.zeros((rows, HP - HD), BF)
    for i, ref in enumerate((query_ref, key_ref, value_ref)):
        for h in range(H):
            head = jnp.concatenate([ref[:, h * HD : (h + 1) * HD], blank], axis=1)
            lo = (2 * i + h % 2) * HP
            out_ref[h // 2, :, lo : lo + HP] = head


def head_sheet(query, key, value):
    return pl.pallas_call(
        head_sheet_kernel,
        out_shape=jax.ShapeDtypeStruct((8, query.shape[0], 6 * HP), BF),
        compiler_params=pltpu.CompilerParams(vmem_limit_bytes=32 * 2**20),
    )(query, key, value)


def unit_sheet_kernel(layers, part, gate_ref, up_ref, out_ref):
    for w, ref in enumerate((gate_ref, up_ref)):
        for p in range(8):
            pieces = [
                ref[:, (8 * z + p) * part : (8 * z + p + 1) * part] for z in range(layers)
            ]
            lo = w * layers * part
            out_ref[p, :, lo : lo + layers * part] = jnp.concatenate(pieces, axis=1)


def unit_sheet(gate, up, layers, part):
    return pl.pallas_call(
        functools.partial(unit_sheet_kernel, layers, part),
        out_shape=jax.ShapeDtypeStruct((8, gate.shape[0], 2 * layers * part), BF),
        compiler_params=pltpu.CompilerParams(vmem_limit_bytes=32 * 2**20),
    )(gate, up)


def head_owner_kernel(sheet_ref, query_ref, key_ref, value_ref):
    for i, ref in enumerate((query_ref, key_ref, value_ref)):
        for h in range(H):
            lo = (2 * i + h % 2) * HP
            ref[:, h * HD : (h + 1) * HD] = sheet_ref[h // 2, :, lo : lo + HD].astype(F32)


def head_owner(sheet):
    shape = jax.ShapeDtypeStruct((sheet.shape[1], H * HD), F32)
    return pl.pallas_call(
        head_owner_kernel,
        out_shape=[shape, shape, shape],
        compiler_params=pltpu.CompilerParams(vmem_limit_bytes=32 * 2**20),
    )(sheet)


def unit_owner_kernel(layers, part, sheet_ref, gate_ref, up_ref):
    for w, ref in enumerate((gate_ref, up_ref)):
        for z in range(layers):
            lo = (w * layers + z) * part
            pieces = [sheet_ref[p, :, lo : lo + part].astype(F32) for p in range(8)]
            ref[:, 8 * z * part : 8 * (z + 1) * part] = jnp.concatenate(pieces, axis=1)


def unit_owner(sheet, layers, part):
    shape = jax.ShapeDtypeStruct((sheet.shape[1], 8 * layers * part), F32)
    return pl.pallas_call(
        functools.partial(unit_owner_kernel, layers, part),
        out_shape=[shape, shape],
        compiler_params=pltpu.CompilerParams(vmem_limit_bytes=32 * 2**20),
    )(sheet)


def project_kernel(mixed_ref, weight_ref, input_ref, gain_ref, middle_ref, hidden_ref):
    step = pl.program_id(0)

    @pl.when(step == 0)
    def _():
        middle_ref[...] = input_ref[...].astype(F32)

    middle_ref[...] += jnp.dot(mixed_ref[...], weight_ref[...], preferred_element_type=F32)

    @pl.when(step == pl.num_programs(0) - 1)
    def _():
        normed, _ = normalize(middle_ref[...])
        hidden_ref[...] = (normed * gain_ref[...]).astype(BF)


def project(mixed, weight, own, gain):
    count, rows, depth = mixed.shape
    width = own.shape[1]
    whole = lambda p: (0, 0)
    return pl.pallas_call(
        project_kernel,
        grid=(count,),
        in_specs=[
            pl.BlockSpec((None, rows, depth), lambda p: (p, 0, 0)),
            pl.BlockSpec((depth, width), lambda p: (p, 0)),
            pl.BlockSpec((rows, width), whole),
            pl.BlockSpec((1, width), whole),
        ],
        out_specs=[pl.BlockSpec((rows, width), whole), pl.BlockSpec((rows, width), whole)],
        out_shape=[
            jax.ShapeDtypeStruct((rows, width), F32),
            jax.ShapeDtypeStruct((rows, width), BF),
        ],
        compiler_params=pltpu.CompilerParams(vmem_limit_bytes=32 * 2**20),
    )(mixed, weight, own, gain)


def unproject_kernel(
    here_ref, x_ref, y_ref, middle_ref, top_ref, gain_ref, weight_ref, out_ref, grad_ref, branch_ref, gain_grad_ref
):
    @pl.when(pl.program_id(0) == 0)
    def _():
        grad_hidden = here_ref[...] + x_ref[...].astype(F32) + y_ref[...].astype(F32)
        normed, factor = normalize(middle_ref[...])
        gain_grad_ref[...] = jnp.sum(grad_hidden * normed, axis=0, keepdims=True)
        grad = top_ref[...].astype(F32) + norm_back(grad_hidden * gain_ref[...], normed, factor)
        grad_ref[...] = grad
        branch_ref[...] = grad.astype(BF)

    out_ref[...] = lax.dot_general(
        branch_ref[...], weight_ref[...], NT, preferred_element_type=F32
    ).astype(BF)


def unproject(terms, middle, top, gain, weight):
    rows, width = middle.shape
    depth = weight.shape[0] // 8
    full = pl.BlockSpec((rows, width), lambda p: (0, 0))
    line = pl.BlockSpec((1, width), lambda p: (0, 0))
    return pl.pallas_call(
        unproject_kernel,
        grid=(8,),
        in_specs=[full] * 5 + [line, pl.BlockSpec((depth, width), lambda p: (p, 0))],
        out_specs=[pl.BlockSpec((None, rows, depth), lambda p: (p, 0, 0)), full, full, line],
        out_shape=[
            jax.ShapeDtypeStruct((8, rows, depth), BF),
            jax.ShapeDtypeStruct((rows, width), F32),
            jax.ShapeDtypeStruct((rows, width), BF),
            jax.ShapeDtypeStruct((1, width), F32),
        ],
        compiler_params=pltpu.CompilerParams(vmem_limit_bytes=48 * 2**20),
    )(*terms, middle, top, gain, weight)


def ffn_kernel(count, kept, *refs):
    blocks, refs = refs[:count], refs[count:]
    top_ref, gate_up_ref, down_ref, refs = *refs[:3], refs[3 + kept :]
    inner_ref, grads_ref, hidden_ref, back_ref, out_ref = refs
    for j, ref in enumerate(blocks):

        @pl.when(pl.program_id(0) == j)
        def _():
            hidden_ref[...] = ref[...]

    units = down_ref.shape[0]
    both = jnp.dot(hidden_ref[...], gate_up_ref[...], preferred_element_type=F32)
    grad_inner = lax.dot_general(top_ref[...], down_ref[...], NT, preferred_element_type=F32)
    gate, upper = both[:, :units], both[:, units:]
    sigma = jax.nn.sigmoid(gate)
    activ = gate * sigma
    inner = (activ * upper).astype(BF)
    inner_ref[...] = inner
    grad_upper = grad_inner * activ
    grad_gate = grad_inner * upper * sigma * (1.0 + gate * (1.0 - sigma))
    grads = jnp.concatenate([grad_gate, grad_upper], axis=1).astype(BF)
    grads_ref[...] = grads
    back_ref[...] = lax.dot_general(
        grads, gate_up_ref[...], NT, preferred_element_type=F32
    ).astype(BF)
    out_ref[...] = jnp.dot(inner, down_ref[...], preferred_element_type=F32).astype(BF)


def ffn(blocks, tops, gate_up, down, first, carried=()):
    count = len(blocks)
    rows, width = blocks[0].shape
    units = down.shape[0]
    whole = lambda i: (0, 0)
    tile = lambda columns: pl.BlockSpec((rows, columns), lambda i: (i + first, 0))
    part = pl.BlockSpec((None, rows, width), lambda i: (i, 0, 0))
    stacked = lambda columns: jax.ShapeDtypeStruct((8 * rows, columns), BF)
    return pl.pallas_call(
        functools.partial(ffn_kernel, count, len(carried)),
        grid=(count,),
        in_specs=[pl.BlockSpec((rows, width), whole)] * count
        + [
            tile(width),
            pl.BlockSpec((width, 2 * units), whole),
            pl.BlockSpec((units, width), whole),
        ]
        + [pl.BlockSpec(memory_space=pl.ANY)] * len(carried),
        out_specs=[tile(units), tile(2 * units), tile(width), part, part],
        out_shape=[
            stacked(units),
            stacked(2 * units),
            stacked(width),
            jax.ShapeDtypeStruct((count, rows, width), BF),
            jax.ShapeDtypeStruct((count, rows, width), BF),
        ],
        input_output_aliases={count + 3 + i: i for i in range(len(carried))},
        compiler_params=pltpu.CompilerParams(vmem_limit_bytes=56 * 2**20),
    )(*blocks, tops, gate_up, down, *carried)


def outer_kernel(*refs):
    *blocks, right_ref, out_ref = refs
    sums = [
        lax.dot_general(ref[...], right_ref[i], TN, preferred_element_type=F32)
        for i, ref in enumerate(blocks)
    ]
    out_ref[...] = functools.reduce(jnp.add, sums).astype(BF)


def outer(blocks, right):
    rows, width = blocks[0].shape
    count, _, depth = right.shape
    tile = 256
    return pl.pallas_call(
        outer_kernel,
        grid=(width // tile,),
        in_specs=[pl.BlockSpec((rows, tile), lambda i: (0, i))] * count
        + [pl.BlockSpec((count, rows, depth), lambda i: (0, 0, 0))],
        out_specs=pl.BlockSpec((tile, depth), lambda i: (i, 0)),
        out_shape=jax.ShapeDtypeStruct((width, depth), BF),
        compiler_params=pltpu.CompilerParams(vmem_limit_bytes=32 * 2**20),
    )(*blocks, right)


def mend_kernel(info_ref, tail_ref, back_ref, cur_ref, out_ref):
    out_ref[:, : 2 * HP] = cur_ref[:, : 2 * HP]
    out_ref[:, 2 * HP :] = (tail_ref[...] + back_ref[...].astype(F32)).astype(BF)


def mend(info, tail, back, grad_qkv):
    rows, blocks = grad_qkv.shape[1], grad_qkv.shape[0] // 2
    side = pl.BlockSpec((None, WINDOW, 4 * HP), lambda s, info: (s, 0, 0))
    edge = pl.BlockSpec(
        (None, WINDOW, 6 * HP),
        lambda s, info: (2 * ((blocks - 1) ^ info[0]) + s, rows // WINDOW - 1, 0),
    )
    return pl.pallas_call(
        mend_kernel,
        grid_spec=pltpu.PrefetchScalarGridSpec(
            num_scalar_prefetch=1, grid=(2,), in_specs=[side, side, edge], out_specs=edge
        ),
        out_shape=jax.ShapeDtypeStruct(grad_qkv.shape, BF),
        input_output_aliases={3: 0},
    )(info, tail, back, grad_qkv)


def shares_of(query, keys, cut, offset):
    raw = lax.dot_general(query, keys, NT, preferred_element_type=F32)
    row = lax.broadcasted_iota(jnp.int32, raw.shape, 0)
    col = lax.broadcasted_iota(jnp.int32, raw.shape, 1)
    valid = (col > row) & (col <= row + WINDOW)
    if offset == 0:
        valid = valid & (col >= cut)
    scores = jnp.where(valid, raw * (HD ** (-0.5)), MASKED)
    peak = jnp.max(scores, axis=-1, keepdims=True)
    powers = jnp.exp(scores - peak)
    return powers / jnp.sum(powers, axis=-1, keepdims=True)


def joined(prev_ref, halo_ref, cur_ref, at_first, lo):
    before = jnp.where(
        at_first, halo_ref[:, lo - 2 * HP : lo - HP], prev_ref[:, lo : lo + HP]
    )
    return jnp.concatenate([before, cur_ref[:, lo : lo + HP]], axis=0)


def attend_kernel(info_ref, cur_ref, prev_ref, halo_ref, flat_ref, kept_ref):
    stream, block = pl.program_id(0), pl.program_id(1)
    at_first = block == 0
    cut = jnp.where(at_first & (info_ref[2 + stream] == 1), WINDOW, 0)
    rows = cur_ref.shape[0]
    for h in range(2):
        keys = joined(prev_ref, halo_ref, cur_ref, at_first, (2 + h) * HP)
        values = joined(prev_ref, halo_ref, cur_ref, at_first, (4 + h) * HP)
        for at in range(0, rows, SUB):
            query = cur_ref[at : at + SUB, h * HP : (h + 1) * HP]
            shares = shares_of(query, keys[at : at + SPAN], cut, at)
            mixed = jnp.dot(
                shares.astype(BF), values[at : at + SPAN], preferred_element_type=F32
            ).astype(BF)
            flat_ref[at : at + SUB, h * HP : (h + 1) * HP] = mixed
            kept_ref[at : at + SUB, h * HP : (h + 1) * HP] = mixed


def attend(qkv, halo, info):
    rows, blocks = qkv.shape[1], qkv.shape[0] // 2
    mine = lambda s, b, info: (2 * (b ^ info[0]) + s, 0, 0)
    before = lambda s, b, info: (2 * (jnp.maximum(b - 1, 0) ^ info[0]) + s, rows // WINDOW - 1, 0)
    spec = pltpu.PrefetchScalarGridSpec(
        num_scalar_prefetch=1,
        grid=(2, blocks),
        in_specs=[
            pl.BlockSpec((None, rows, 6 * HP), mine),
            pl.BlockSpec((None, WINDOW, 6 * HP), before),
            pl.BlockSpec((None, WINDOW, 4 * HP), lambda s, b, info: (s, 0, 0)),
        ],
        out_specs=[
            pl.BlockSpec((None, rows, 2 * HP), lambda s, b, info: (2 * b + (s ^ info[1]), 0, 0)),
            pl.BlockSpec((None, rows, 2 * HP), mine),
        ],
    )
    shape = jax.ShapeDtypeStruct((2 * blocks, rows, 2 * HP), BF)
    return pl.pallas_call(
        attend_kernel,
        grid_spec=spec,
        out_shape=[shape, shape],
        compiler_params=pltpu.CompilerParams(vmem_limit_bytes=32 * 2**20),
    )(info, qkv, qkv, halo)


def attend_back_kernel(
    info_ref, cur_ref, prev_ref, halo_ref, top_ref, out_ref, tail_ref, lead_ref, keep, acc
):
    stream, step = pl.program_id(0), pl.program_id(1)
    blocks = pl.num_programs(1)
    at_first = step == blocks - 1
    cut = jnp.where(at_first & (info_ref[2 + stream] == 1), WINDOW, 0)
    rows = cur_ref.shape[0]

    @pl.when(step == 0)
    def _():
        keep[...] = jnp.zeros_like(keep)

    acc[...] = jnp.zeros_like(acc)
    for h in range(2):
        lo, hi = h * HP, (h + 1) * HP
        keys = joined(prev_ref, halo_ref, cur_ref, at_first, (2 + h) * HP)
        values = joined(prev_ref, halo_ref, cur_ref, at_first, (4 + h) * HP)
        for at in range(0, rows, SUB):
            query = cur_ref[at : at + SUB, lo:hi]
            top = top_ref[at : at + SUB, lo:hi]
            key = keys[at : at + SPAN]
            shares = shares_of(query, key, cut, at)
            grad_shares = lax.dot_general(
                top, values[at : at + SPAN], NT, preferred_element_type=F32
            )
            grad_raw = (
                shares
                * (grad_shares - jnp.sum(shares * grad_shares, axis=-1, keepdims=True))
                * (HD ** (-0.5))
            ).astype(BF)
            out_ref[at : at + SUB, lo:hi] = jnp.dot(
                grad_raw, key, preferred_element_type=F32
            ).astype(BF)
            acc[at : at + SPAN, lo:hi] += lax.dot_general(
                grad_raw, query, TN, preferred_element_type=F32
            )
            acc[at : at + SPAN, 2 * HP + lo : 2 * HP + hi] += lax.dot_general(
                shares.astype(BF), top, TN, preferred_element_type=F32
            )
    last = acc[rows : rows + WINDOW, :] + keep[...]
    out_ref[: rows - WINDOW, 2 * HP :] = acc[WINDOW:rows, :].astype(BF)
    out_ref[rows - WINDOW :, 2 * HP :] = last.astype(BF)
    keep[...] = acc[:WINDOW, :]

    @pl.when(step == 0)
    def _():
        tail_ref[...] = last

    @pl.when(at_first)
    def _():
        lead_ref[...] = acc[:WINDOW, :].astype(BF)


def attend_back(qkv, halo, top, info):
    rows, blocks = qkv.shape[1], qkv.shape[0] // 2
    at = lambda t: blocks - 1 - t
    mine = lambda s, t, info: (2 * (at(t) ^ info[0]) + s, 0, 0)
    before = lambda s, t, info: (
        2 * (jnp.maximum(at(t) - 1, 0) ^ info[0]) + s,
        rows // WINDOW - 1,
        0,
    )
    side = lambda s, t, info: (s, 0, 0)
    spec = pltpu.PrefetchScalarGridSpec(
        num_scalar_prefetch=1,
        grid=(2, blocks),
        in_specs=[
            pl.BlockSpec((None, rows, 6 * HP), mine),
            pl.BlockSpec((None, WINDOW, 6 * HP), before),
            pl.BlockSpec((None, WINDOW, 4 * HP), side),
            pl.BlockSpec(
                (None, rows, 2 * HP), lambda s, t, info: (2 * at(t) + (s ^ info[1]), 0, 0)
            ),
        ],
        out_specs=[
            pl.BlockSpec((None, rows, 6 * HP), mine),
            pl.BlockSpec((None, WINDOW, 4 * HP), side),
            pl.BlockSpec((None, WINDOW, 4 * HP), side),
        ],
        scratch_shapes=[
            pltpu.VMEM((WINDOW, 4 * HP), F32),
            pltpu.VMEM((rows + WINDOW, 4 * HP), F32),
        ],
    )
    return pl.pallas_call(
        attend_back_kernel,
        grid_spec=spec,
        out_shape=[
            jax.ShapeDtypeStruct(qkv.shape, BF),
            jax.ShapeDtypeStruct(halo.shape, F32),
            jax.ShapeDtypeStruct(halo.shape, BF),
        ],
        compiler_params=pltpu.CompilerParams(vmem_limit_bytes=32 * 2**20),
    )(info, qkv, qkv, halo, top)


def body(
    inputs,
    starts,
    attn_gain,
    query_weight,
    key_weight,
    value_weight,
    out_weight,
    ffn_gain,
    gate_weight,
    up_weight,
    down_weight,
    cotangent,
):
    rows, width = inputs.shape[1:]
    layers = lax.axis_size("z")
    devices = 8 * layers
    share = query_weight.shape[0]
    hidden_units = gate_weight.shape[1]
    units = hidden_units // 8
    part = down_weight.shape[0]
    me_z = lax.axis_index("z")
    me_block = 2 * lax.axis_index("y") + lax.axis_index("x")
    me_core = lax.axis_index("c")

    own = inputs[0]
    top = cotangent[0]
    streams = plane_gather(own)
    heads = head_sheet(query_weight, key_weight, value_weight)
    heads = lax.all_to_all(heads, PLANE, 0, 0, tiled=True).reshape(8 * share, 6 * HP)
    qkv_pieces = ring_gather(heads, layers)
    qkv_weight = placed(qkv_pieces)
    small = jnp.concatenate([attn_gain, ffn_gain, starts[0].astype(BF)], axis=0)
    small = jnp.pad(small, (0, 128 - small.shape[0]))
    small = after(jnp.broadcast_to(small, (devices, 128)), heads)
    small = lax.all_to_all(small, ALL, 0, 0, tiled=True)
    gain_attn = small[:, :share].reshape(1, width).astype(F32)
    gain_ffn = small[:, share : 2 * share].reshape(1, width).astype(F32)
    opened = lax.dynamic_slice(small, (8 * me_z, 2 * share), (2, 1))[:, 0].astype(jnp.int32)
    opened = jnp.where(me_core == 0, opened, opened[::-1])
    info = jnp.concatenate([jnp.stack([me_block, me_core]).astype(jnp.int32), opened])
    sheet = after(unit_sheet(gate_weight, up_weight, layers, part), small)
    sheet = lax.all_to_all(sheet, PLANE, 0, 0, tiled=True).reshape(8 * share, 2 * units)

    full_out = lax.all_gather(out_weight, ALL, axis=0, tiled=True)
    full_out = jnp.pad(full_out.reshape(H, HD, width), ((0, 0), (0, HP - HD), (0, 0)))
    full_out = full_out.reshape(H * HP, width)
    gate_up = lax.all_gather(sheet, "z", axis=0, tiled=True)
    down = placed(direct_gather(after(down_weight, qkv_pieces[-1]), layers))
    tops = plane_gather(after(top, streams[6]))
    tops = jnp.concatenate(tops[:4] + tops[6:] + tops[4:6], axis=0)

    stream = jnp.concatenate(streams, axis=0).astype(F32)
    hidden1 = (normalize(stream)[0] * gain_attn).astype(BF)
    qkv = dot(hidden1, qkv_weight).astype(BF).reshape(8, rows, 6 * HP)
    last = 2 * (3 ^ me_block)
    rim = lax.dynamic_slice(qkv, (last, rows - WINDOW, 2 * HP), (2, WINDOW, 4 * HP))
    halo = lax.ppermute(rim, "z", [(i, i + 1) for i in range(layers - 1)])
    flat, kept = attend(qkv, halo, info)
    mixed = lax.all_to_all(flat, PLANE, 0, 0, tiled=True)
    middle, hidden2 = project(mixed, full_out, own, gain_ffn)

    hidden2 = plane_gather(hidden2)
    *carried, back_near, out_near = ffn(hidden2[:4], tops, gate_up, down, 0)
    inner, grads, hidden2, back_far, out_far = ffn(
        hidden2[6:] + hidden2[4:6], tops, gate_up, down, 4, carried
    )
    pairs = lambda near, far: [
        (near[0], near[1]), (near[2], near[3]), (far[2], far[3]), (far[0], far[1])
    ]
    terms = plane_sum(pairs(back_near, back_far))
    down_sum = lax.psum_scatter(
        dot(inner, tops, TN).astype(BF), "z", scatter_dimension=0, tiled=True
    )
    gate_up_sum = lax.psum_scatter(
        dot(hidden2, grads, TN).astype(BF), "z", scatter_dimension=0, tiled=True
    )

    grad_mixed, grad_middle, grad_branch, ffn_gain_local = unproject(
        terms, middle, top, gain_ffn, full_out
    )
    grad_mixed = lax.all_to_all(grad_mixed, PLANE, 0, 0, tiled=True)
    branches = plane_gather(after(grad_branch, grad_mixed))
    out_near, out_far, _ = lax.optimization_barrier((out_near, out_far, branches[6]))
    out_terms = plane_sum(pairs(out_near, out_far))
    layer_out = (middle + total(out_terms)).astype(BF)
    grad_qkv, tail, lead = attend_back(qkv, halo, grad_mixed, info)
    back = lax.ppermute(lead, "z", [(i + 1, i) for i in range(layers - 1)])
    grad_qkv = mend(info, tail, back, grad_qkv).reshape(8 * rows, 6 * HP)
    parts = []
    for r in range(4):
        at = slice(2 * r * rows, 2 * (r + 1) * rows)
        part_sum = dot(grad_qkv[at], qkv_weight, NT).astype(BF)
        parts.append((part_sum[:rows], part_sum[rows:]))
    grad_hidden1 = total(plane_sum(parts))
    out_sum = lax.psum_scatter(outer(branches, kept), "z", scatter_dimension=0, tiled=True)
    qkv_sum = lax.psum_scatter(
        dot(hidden1, grad_qkv, TN).astype(BF), "z", scatter_dimension=0, tiled=True
    )
    normed1, rscale1 = normalize(own.astype(F32))
    attn_gain_local = jnp.sum(grad_hidden1 * normed1, axis=0)
    input_grad = grad_middle + norm_back(grad_hidden1 * gain_attn, normed1, rscale1)

    gate_up_sum = lax.all_to_all(
        gate_up_sum.reshape(8, share, 2 * units), PLANE, 0, 0, tiled=True
    )
    gate_grad, up_grad = unit_owner(gate_up_sum, layers, part)
    qkv_sum = lax.all_to_all(qkv_sum.reshape(8, share, 6 * HP), PLANE, 0, 0, tiled=True)
    query_grad, key_grad, value_grad = head_owner(qkv_sum)
    out_sum = out_sum.reshape(-1, 2, HP)[..., :HD].reshape(-1, layers, share)
    pieces = []
    for j in range(layers):
        route = [
            (8 * z + p, layers * p + (z + j) % layers) for z in range(layers) for p in range(8)
        ]
        piece = lax.dynamic_index_in_dim(out_sum, (me_z + j) % layers, axis=1, keepdims=False)
        pieces.append(lax.ppermute(piece, ALL, route))
    rank = 8 * me_z + 2 * me_block + me_core
    turned = jnp.roll(jnp.stack(pieces[::-1]), rank % layers + 1, axis=0)
    output_grad = turned.reshape(width, share).T.astype(F32)
    gains = jnp.stack([attn_gain_local, ffn_gain_local[0]]).reshape(2, devices, share).swapaxes(0, 1)
    gains = jnp.sum(lax.all_to_all(gains, ALL, 0, 0, tiled=True), axis=0)
    return (
        layer_out[None],
        input_grad[None],
        gains[0],
        query_grad,
        key_grad,
        value_grad,
        output_grad,
        gains[1],
        gate_grad,
        up_grad,
        down_sum.astype(F32),
    )


def solution(mesh):
    blocks = mesh.shape["seq"]
    fine = Mesh(mesh.devices.reshape(blocks // 4, 2, 2, 2), ALL)
    tokens = P("c", ("z", "y", "x"), None)
    weight = P(ALL, None)
    gain = P(ALL)
    in_specs = (
        tokens,
        P("c", ("z", "y", "x")),
        gain,
        weight,
        weight,
        weight,
        weight,
        gain,
        weight,
        weight,
        weight,
        tokens,
    )
    out_specs = (
        tokens,
        tokens,
        gain,
        weight,
        weight,
        weight,
        weight,
        gain,
        weight,
        weight,
        weight,
    )
    return jax.shard_map(body, mesh=fine, in_specs=in_specs, out_specs=out_specs, check_vma=False)
```

```python
import functools

import jax
import jax.numpy as jnp
from jax import lax
from jax.experimental import pallas as pl
from jax.experimental.pallas import tpu as pltpu
from jax.sharding import Mesh, PartitionSpec as P

H = 16
HD = 112
HP = 128
WINDOW = 64
EPS = 1e-06
MASKED = -1e30
SUB = 128
SPAN = 256

BF = jnp.bfloat16
F32 = jnp.float32
ALL = ("z", "y", "x", "c")
PLANE = ("y", "x", "c")
SWAP = [(0, 1), (1, 0)]
NT = (((1,), (1,)), ((), ()))
TN = (((0,), (0,)), ((), ()))
NN = (((1,), (0,)), ((), ()))


def cost(us):
    return pl.CostEstimate(flops=int(us * 1.1e9), bytes_accessed=int(us * 3.5e6), transcendentals=0)


def swap(block, axis):
    return lax.ppermute(block, axis, SWAP)


def normalize(values):
    factor = lax.rsqrt(jnp.mean(values * values, axis=-1, keepdims=True) + EPS)
    return (values * factor, factor)


def norm_back(grad_normed, normed_rows, factor):
    return factor * (
        grad_normed - normed_rows * jnp.mean(grad_normed * normed_rows, axis=-1, keepdims=True)
    )


def dot(left, right, dims=NN):
    return lax.dot_general(left, right, dims, preferred_element_type=F32)


ANY = pl.BlockSpec(memory_space=pl.ANY)


VMEM = pl.BlockSpec(memory_space=pltpu.VMEM)
SMEM = pl.BlockSpec(memory_space=pltpu.SMEM)


def held_kernel(source_ref, *refs):
    refs[-1][...] = source_ref[...]


def held(value, *others):
    return pl.pallas_call(
        held_kernel,
        in_specs=[VMEM] + [ANY] * len(others),
        out_specs=VMEM,
        out_shape=jax.ShapeDtypeStruct(value.shape, value.dtype),
        cost_estimate=cost(2),
        compiler_params=pltpu.CompilerParams(vmem_limit_bytes=32 * 2**20),
    )(value, *others)


def stack_kernel(count, *refs):
    for k in range(count):
        refs[-1][k] = refs[k][...]


def stack(pieces, *others):
    count = len(pieces)
    return pl.pallas_call(
        functools.partial(stack_kernel, count),
        in_specs=[VMEM] * count + [ANY] * len(others),
        out_specs=VMEM,
        out_shape=jax.ShapeDtypeStruct((count, *pieces[0].shape), pieces[0].dtype),
        cost_estimate=cost(2),
        compiler_params=pltpu.CompilerParams(vmem_limit_bytes=32 * 2**20),
    )(*pieces, *others)


def neighbours(own):
    return swap(own, "x"), swap(own, "y")


def join_kernel(first_ref, second_ref, *refs):
    half = first_ref.shape[0]
    refs[-1][:half] = first_ref[...]
    refs[-1][half:] = second_ref[...]


def join(first, second, *others):
    shape = (2 * first.shape[0], *first.shape[1:])
    return pl.pallas_call(
        join_kernel,
        in_specs=[VMEM] * 2 + [ANY] * len(others),
        out_specs=VMEM,
        out_shape=jax.ShapeDtypeStruct(shape, first.dtype),
        cost_estimate=cost(2),
        compiler_params=pltpu.CompilerParams(vmem_limit_bytes=32 * 2**20),
    )(first, second, *others)


def halves_kernel(x_ref, y_ref, *refs):
    half = x_ref.shape[0] // 2
    refs[-2][...] = y_ref[:half]
    refs[-1][...] = x_ref[half:]


def halves(from_x, from_y, *others):
    shape = jax.ShapeDtypeStruct((from_x.shape[0] // 2, *from_x.shape[1:]), from_x.dtype)
    return pl.pallas_call(
        halves_kernel,
        in_specs=[VMEM] * 2 + [ANY] * len(others),
        out_specs=[VMEM] * 2,
        out_shape=[shape, shape],
        cost_estimate=cost(2),
        compiler_params=pltpu.CompilerParams(vmem_limit_bytes=32 * 2**20),
    )(from_x, from_y, *others)


def diagonal(from_x, from_y, *others):
    first, second = halves(from_x, from_y, *others)
    return swap(first, "x"), swap(second, "y")


def both_cores(blocks):
    return [block for mine in blocks for block in (mine, swap(mine, "c"))]


def add_kernel(mine_ref, other_ref, *refs):
    refs[-1][...] = (mine_ref[...].astype(F32) + other_ref[...].astype(F32)).astype(BF)


def add(mine, other, *others):
    return pl.pallas_call(
        add_kernel,
        in_specs=[VMEM] * 2 + [ANY] * len(others),
        out_specs=VMEM,
        out_shape=jax.ShapeDtypeStruct(mine.shape, BF),
        cost_estimate=cost(2),
        compiler_params=pltpu.CompilerParams(vmem_limit_bytes=32 * 2**20),
    )(mine, other, *others)


def plane_sum(parts, *others):
    half = parts[0][0].shape[0] // 2
    other = {r: swap(parts[r][1], "c") for r in (3, 2, 1, 0)}
    far = add(parts[3][0], other[3], *others)
    first = swap(far[:half], "x")
    second = swap(far[half:], "y")
    along_y, along_x, here = (parts[r][0].astype(F32) + other[r].astype(F32) for r in (2, 1, 0))
    along_y = jnp.concatenate([along_y[:half] + first.astype(F32), along_y[half:]], axis=0).astype(BF)
    along_x = jnp.concatenate([along_x[:half], along_x[half:] + second.astype(F32)], axis=0).astype(BF)
    return (here, swap(along_x, "x"), swap(along_y, "y")), (along_x, along_y), far


def total(terms):
    here, got_x, got_y = terms
    return here + got_x.astype(F32) + got_y.astype(F32)


def direct_gather(block, count):
    return [block] + [
        lax.ppermute(block, "z", [(i, (i + k) % count) for i in range(count)])
        for k in range(1, count)
    ]


def padded(share):
    return share * HP // HD


def head_sheet_kernel(starts_ref, query_ref, key_ref, value_ref, gains_ref, out_ref):
    rows = query_ref.shape[0]
    spare = padded(rows) - rows
    same = lax.broadcasted_iota(jnp.int32, (rows, rows), 0) == lax.broadcasted_iota(
        jnp.int32, (rows, rows), 1
    )
    extra = [
        jnp.sum(
            jnp.where(same, jnp.broadcast_to(gains_ref[i : i + 1, :], (rows, rows)), 0.0),
            axis=1,
            keepdims=True,
        )
        for i in range(2)
    ]
    extra = extra + [jnp.full((rows, 1), starts_ref[0, 0], jnp.int32).astype(F32)]
    extra = jnp.concatenate(extra + [jnp.zeros((rows, HP - HD - 3), F32)], axis=1).astype(BF)
    for i, ref in enumerate((query_ref, key_ref, value_ref)):
        for h in range(H):
            pieces = []
            for a in range(HD // rows):
                pieces.append(ref[:, h * HD + a * rows : h * HD + (a + 1) * rows])
                if i == 0 and h % 2 == 0:
                    pieces.append(extra[:, a * spare : (a + 1) * spare])
                else:
                    pieces.append(jnp.zeros((rows, spare), BF))
            lo = (2 * i + h % 2) * HP
            out_ref[h // 2, :, lo : lo + HP] = jnp.concatenate(pieces, axis=1)


def head_sheet(query, key, value, gains, starts):
    whole = pl.BlockSpec(memory_space=pltpu.VMEM)
    return pl.pallas_call(
        head_sheet_kernel,
        in_specs=[pl.BlockSpec(memory_space=pltpu.SMEM)] + [whole] * 4,
        out_specs=whole,
        out_shape=jax.ShapeDtypeStruct((8, query.shape[0], 6 * HP), BF),
        cost_estimate=cost(2),
        compiler_params=pltpu.CompilerParams(vmem_limit_bytes=32 * 2**20),
    )(starts, query, key, value, gains)


def extra_column(j, share):
    spare = padded(share) - share
    return j // spare * padded(share) + share + j % spare


def attn_sheet_kernel(heads_ref, out_weight_ref, *refs):
    sheet_ref = refs[-1]
    count, rows, columns = heads_ref.shape
    size, tile = padded(rows), sheet_ref.shape[1] - columns
    heads = [heads_ref[p].astype(F32) for p in range(count)]
    sheet_ref[:, :columns] = jnp.concatenate(heads, axis=0).astype(BF)
    blank = jnp.zeros((size - rows, tile), F32)
    blocks = []
    for i in range(out_weight_ref.shape[1] // tile):
        blocks += [out_weight_ref[:, i * tile : (i + 1) * tile].astype(F32), blank]
    sheet_ref[:, columns:] = jnp.concatenate(blocks, axis=0).astype(BF)


def attn_sheet(heads, out_weight, *others):
    count, rows, columns = heads.shape
    return pl.pallas_call(
        attn_sheet_kernel,
        in_specs=[VMEM] * 2 + [ANY] * len(others),
        out_shape=jax.ShapeDtypeStruct((count * rows, columns + 256), BF),
        cost_estimate=cost(2),
        compiler_params=pltpu.CompilerParams(vmem_limit_bytes=32 * 2**20),
    )(heads, out_weight, *others)


def out_sheet_kernel(info_ref, *refs):
    *blocks, out_ref = refs
    layers, size, width = out_ref.shape
    tile = blocks[0].shape[1]
    count = width // tile
    for r, block in enumerate(blocks):

        @pl.when(pl.program_id(0) == r)
        def _():
            for z in range(layers):
                for i in range(count):
                    at = (z * count + i) * size
                    out_ref[z, :, i * tile : (i + 1) * tile] = block[at : at + size, :]


def out_sheet(blocks, info, layers):
    depth, tile = blocks[0].shape
    size, width = 2 * HP // layers, depth * tile * 8 // (16 * HP)
    place = lambda r, info: (0, 2 * ((r // 2) ^ info[0]) + ((r % 2) ^ info[1]), 0, 0)
    out = pl.pallas_call(
        out_sheet_kernel,
        grid_spec=pltpu.PrefetchScalarGridSpec(
            num_scalar_prefetch=1,
            grid=(8,),
            in_specs=[pl.BlockSpec((depth, tile), lambda r, info: (0, 0))] * 8,
            out_specs=pl.BlockSpec((layers, None, size, width), place),
        ),
        out_shape=pltpu.HBM((layers, 8, size, width), BF),
        cost_estimate=cost(6),
        compiler_params=pltpu.CompilerParams(vmem_limit_bytes=32 * 2**20),
    )(info, *blocks)
    return out.reshape(-1, width)


def unit_sheet_kernel(layers, part, gate_ref, up_ref, *refs):
    out_ref = refs[-1]
    units = out_ref.shape[2] // 2
    blank = jnp.zeros((gate_ref.shape[0], units // layers - part), BF)
    for w, ref in enumerate((gate_ref, up_ref)):
        for p in range(8):
            pieces = []
            for z in range(layers):
                pieces.append(ref[:, (8 * z + p) * part : (8 * z + p + 1) * part])
                pieces.append(blank)
            out_ref[p, :, w * units : (w + 1) * units] = jnp.concatenate(pieces, axis=1)


def unit_sheet(gate, up, layers, part, units, *others):
    return pl.pallas_call(
        functools.partial(unit_sheet_kernel, layers, part),
        in_specs=[pl.BlockSpec(memory_space=pltpu.VMEM)] * 2 + [ANY] * len(others),
        out_shape=jax.ShapeDtypeStruct((8, gate.shape[0], 2 * units), BF),
        cost_estimate=cost(2),
        compiler_params=pltpu.CompilerParams(vmem_limit_bytes=32 * 2**20),
    )(gate, up, *others)


def gain_row(products, gain):
    rows = products.shape[0]
    same = lax.broadcasted_iota(jnp.int32, (rows, rows), 0) == lax.broadcasted_iota(
        jnp.int32, (rows, rows), 1
    )
    row = jnp.sum(jnp.where(same, jnp.broadcast_to(products, (rows, rows)), 0.0), axis=0, keepdims=True)
    return row / gain


def head_owner_kernel(sheet_ref, *refs):
    weights, gain_ref, (*grads, gain_grad_ref) = refs[:3], refs[3], refs[4:]
    rows = weights[0].shape[0]
    products = jnp.zeros((rows, 1), F32)
    for i, ref in enumerate(grads):
        pieces = []
        for h in range(H):
            lo = (h % 2) * HP
            pieces += [
                sheet_ref[h // 2, i, :, lo + a * padded(rows) : lo + a * padded(rows) + rows]
                for a in range(HD // rows)
            ]
        grad = jnp.concatenate(pieces, axis=1).astype(F32)
        ref[...] = grad
        products += jnp.sum(grad * weights[i][...].astype(F32), axis=1, keepdims=True)
    gain_grad_ref[...] = gain_row(products, gain_ref[...])


def head_owner(sheet, weights, gain):
    share, width = weights[0].shape
    shape = jax.ShapeDtypeStruct((share, width), F32)
    return pl.pallas_call(
        head_owner_kernel,
        out_shape=[shape, shape, shape, jax.ShapeDtypeStruct((1, share), F32)],
        cost_estimate=cost(3),
        compiler_params=pltpu.CompilerParams(vmem_limit_bytes=32 * 2**20),
    )(sheet, *weights, gain)


def unit_owner_kernel(layers, part, sheet_ref, *refs):
    weights, gain_ref, (*grads, gain_grad_ref) = refs[:2], refs[2], refs[3:]
    _, columns, rows, tile = sheet_ref.shape
    units = columns * tile // 2
    owned = [
        jnp.concatenate([sheet_ref[p, b] for b in range(columns)], axis=1).astype(F32)
        for p in range(8)
    ]
    products = jnp.zeros((rows, 1), F32)
    for w, ref in enumerate(grads):
        for z in range(layers):
            lo = w * units + z * (units // layers)
            at = slice(8 * z * part, 8 * (z + 1) * part)
            grad = jnp.concatenate([value[:, lo : lo + part] for value in owned], axis=1)
            ref[:, at] = grad
            products += jnp.sum(grad * weights[w][:, at].astype(F32), axis=1, keepdims=True)
    gain_grad_ref[...] = gain_row(products, gain_ref[...])


def unit_owner(sheet, weights, gain, layers, part):
    share, columns = weights[0].shape
    shape = jax.ShapeDtypeStruct((share, columns), F32)
    return pl.pallas_call(
        functools.partial(unit_owner_kernel, layers, part),
        out_shape=[shape, shape, jax.ShapeDtypeStruct((1, share), F32)],
        cost_estimate=cost(3),
        compiler_params=pltpu.CompilerParams(vmem_limit_bytes=32 * 2**20),
    )(sheet, *weights, gain)


def enter_kernel(share, stream_ref, factor_ref, weight_ref, *refs):
    hidden_ref, qkv_ref, gains_ref = refs[-3:]

    @pl.when(pl.program_id(0) == 0)
    def _():
        row = lax.broadcasted_iota(jnp.int32, (8, HP), 0)
        col = lax.broadcasted_iota(jnp.int32, (8, HP), 1)
        pick = (row == 0) & (col == extra_column(0, share))
        pick = pick | ((row == 1) & (col == extra_column(1, share)))
        pick = pick.astype(F32).astype(BF)
        gains_ref[...] = dot(pick, weight_ref[:, :HP], NT)

    normed = stream_ref[...].astype(F32) * factor_ref[...]
    hidden = (normed * gains_ref[0:1, :]).astype(BF)
    hidden_ref[...] = hidden
    qkv_ref[...] = dot(hidden, weight_ref[...]).astype(BF)


def enter(stream, factor, weight, rows, share, *others):
    tokens, width = stream.shape
    whole = lambda i: (0, 0)
    tile = lambda columns: pl.BlockSpec((rows, columns), lambda i: (i, 0))
    return pl.pallas_call(
        functools.partial(enter_kernel, share),
        grid=(tokens // rows,),
        in_specs=[tile(width), tile(1), pl.BlockSpec((width, 6 * HP), whole)] + [ANY] * len(others),
        out_specs=[tile(width), tile(6 * HP), pl.BlockSpec((8, width), whole)],
        out_shape=[
            pltpu.HBM((tokens, width), BF),
            pltpu.HBM((tokens, 6 * HP), BF),
            jax.ShapeDtypeStruct((8, width), F32),
        ],
        cost_estimate=cost(12),
        compiler_params=pltpu.CompilerParams(vmem_limit_bytes=32 * 2**20),
    )(stream, factor, weight, *others)


def project_kernel(mixed_ref, weight_ref, input_ref, gain_ref, *refs):
    middle_ref, hidden_ref = refs[-2:]
    step = pl.program_id(0)

    @pl.when(step == 0)
    def _():
        middle_ref[...] = input_ref[...].astype(F32)

    middle_ref[...] += jnp.dot(mixed_ref[...], weight_ref[...], preferred_element_type=F32)

    @pl.when(step == pl.num_programs(0) - 1)
    def _():
        normed, _ = normalize(middle_ref[...])
        hidden_ref[...] = (normed * gain_ref[...]).astype(BF)


def project(mixed, weight, own, gain, *others):
    count, rows, depth = mixed.shape
    width = own.shape[1]
    whole = lambda p: (0, 0)
    return pl.pallas_call(
        project_kernel,
        grid=(count,),
        in_specs=[
            pl.BlockSpec((None, rows, depth), lambda p: (p, 0, 0)),
            pl.BlockSpec((depth, width), lambda p: (p, 0)),
            pl.BlockSpec((rows, width), whole),
            pl.BlockSpec((1, width), whole),
        ]
        + [ANY] * len(others),
        out_specs=[pl.BlockSpec((rows, width), whole), pl.BlockSpec((rows, width), whole)],
        out_shape=[
            jax.ShapeDtypeStruct((rows, width), F32),
            jax.ShapeDtypeStruct((rows, width), BF),
        ],
        cost_estimate=cost(7),
        compiler_params=pltpu.CompilerParams(vmem_limit_bytes=32 * 2**20),
    )(mixed, weight, own, gain, *others)


def unproject_kernel(
    here_ref, x_ref, y_ref, middle_ref, top_ref, gain_ref, weight_ref, *refs
):
    out_ref, grad_ref, branch_ref = refs[-3:]

    @pl.when(pl.program_id(0) == 0)
    def _():
        grad_hidden = here_ref[...] + x_ref[...].astype(F32) + y_ref[...].astype(F32)
        normed, factor = normalize(middle_ref[...])
        grad = top_ref[...].astype(F32) + norm_back(grad_hidden * gain_ref[...], normed, factor)
        grad_ref[...] = grad
        branch_ref[...] = grad.astype(BF)

    out_ref[...] = lax.dot_general(
        branch_ref[...], weight_ref[...], NT, preferred_element_type=F32
    ).astype(BF)


def unproject(terms, middle, top, gain, weight, *others):
    rows, width = middle.shape
    depth = weight.shape[0] // 8
    full = pl.BlockSpec((rows, width), lambda p: (0, 0))
    line = pl.BlockSpec((1, width), lambda p: (0, 0))
    return pl.pallas_call(
        unproject_kernel,
        grid=(8,),
        in_specs=[full] * 5
        + [line, pl.BlockSpec((depth, width), lambda p: (p, 0))]
        + [ANY] * len(others),
        out_specs=[pl.BlockSpec((None, rows, depth), lambda p: (p, 0, 0)), full, full],
        out_shape=[
            jax.ShapeDtypeStruct((8, rows, depth), BF),
            jax.ShapeDtypeStruct((rows, width), F32),
            jax.ShapeDtypeStruct((rows, width), BF),
        ],
        cost_estimate=cost(12),
        compiler_params=pltpu.CompilerParams(vmem_limit_bytes=48 * 2**20),
    )(*terms, middle, top, gain, weight, *others)


def ffn_kernel(count, kept, *refs):
    blocks, tops, refs = refs[:count], refs[count : 2 * count], refs[2 * count :]
    gate_up_ref, down_ref, refs = refs[0], refs[1], refs[2 + kept :]
    inner_ref, grads_ref, hidden_ref, top_ref = refs[:4]
    backs, (held_hidden, held_top, held_back, sems) = refs[4 : 4 + count], refs[4 + count :]
    rows = blocks[0].shape[0]
    step = pl.program_id(0)
    bring = [
        [
            pltpu.make_async_copy(source, place.at[j], sems.at[k, j])
            for j, source in enumerate(sources)
        ]
        for k, (sources, place) in enumerate(((blocks, held_hidden), (tops, held_top)))
    ]
    send = [
        pltpu.make_async_copy(
            held_back.at[j // 2, pl.ds(j % 2 * rows, rows)], backs[j], sems.at[2, j]
        )
        for j in range(count)
    ]

    @pl.when(step == 0)
    def _():
        for j in range(count):
            bring[0][j].start()
            bring[1][j].start()

    for j in range(0, count, 2):

        @pl.when(step == j // 2)
        def _():
            for k in range(2):
                bring[k][j].wait()
                bring[k][j + 1].wait()

    for half in range(2):
        at = slice(half * rows, (half + 1) * rows)
        hidden_ref[at, :] = held_hidden[2 * step + half]
        top_ref[at, :] = held_top[2 * step + half]
    units = down_ref.shape[0]
    both = dot(hidden_ref[...], gate_up_ref[...])
    grad_inner = dot(top_ref[...], down_ref[...], NT)
    gate, upper = both[:, :units], both[:, units:]
    sigma = jax.nn.sigmoid(gate)
    activ = gate * sigma
    inner_ref[...] = (activ * upper).astype(BF)
    grads_ref[:, units:] = (grad_inner * activ).astype(BF)
    grad_gate = grad_inner * upper * sigma * (1.0 + gate * (1.0 - sigma))
    grads_ref[:, :units] = grad_gate.astype(BF)
    held_back[step] = dot(grads_ref[...], gate_up_ref[...], NT).astype(BF)
    for j in range(0, count, 2):

        @pl.when(step == j // 2)
        def _():
            send[j].start()
            send[j + 1].start()

    @pl.when(step == count // 2 - 1)
    def _():
        for copy in send:
            copy.wait()


def ffn(blocks, tops, gate_up, down, first, carried=(), others=()):
    count = len(blocks)
    rows, width = blocks[0].shape
    units = down.shape[0]
    whole = lambda i: (0, 0)
    tile = lambda columns: pl.BlockSpec((2 * rows, columns), lambda i: (i + first, 0))
    once = lambda shape: pl.BlockSpec(shape, whole, pipeline_mode=pl.Buffered(1))
    stacked = lambda columns: jax.ShapeDtypeStruct((8 * rows, columns), BF)
    out = pl.pallas_call(
        functools.partial(ffn_kernel, count, len(carried) + len(others)),
        grid=(count // 2,),
        in_specs=[ANY] * (2 * count)
        + [once((width, 2 * units)), once((units, width))]
        + [ANY] * (len(carried) + len(others)),
        out_specs=[tile(units), tile(2 * units), tile(width), tile(width)] + [ANY] * count,
        out_shape=[stacked(units), stacked(2 * units), stacked(width), stacked(width)]
        + [jax.ShapeDtypeStruct((rows, width), BF)] * count,
        scratch_shapes=[
            pltpu.VMEM((count, rows, width), BF),
            pltpu.VMEM((count, rows, width), BF),
            pltpu.VMEM((count // 2, 2 * rows, width), BF),
            pltpu.SemaphoreType.DMA((3, count)),
        ],
        input_output_aliases={2 * count + 2 + i: i for i in range(len(carried))},
        cost_estimate=cost(4 * count + 2),
        compiler_params=pltpu.CompilerParams(vmem_limit_bytes=60 * 2**20),
    )(*blocks, *tops, gate_up, down, *carried, *others)
    return out[:4], out[4:]


def split_kernel(order, dims, left_ref, right_ref, *refs):
    rows = left_ref.shape[0] // 2
    both = dot(left_ref[...], right_ref[...], dims)
    outs = refs[-2 * len(order) :]
    both = both.astype(BF)
    for i in range(len(order)):

        @pl.when(pl.program_id(0) == i)
        def _():
            outs[2 * i][...] = both[:rows]
            outs[2 * i + 1][...] = both[rows:]


def split(left, right, dims, order, rows, others=()):
    width = right.shape[1 - dims[0][1][0]]

    def place(i):
        at = order[0]
        for n, r in enumerate(order):
            at = jnp.where(i == n, r, at)
        return at, 0

    used = (width, left.shape[1]) if dims == NT else (left.shape[1], width)
    out = pl.pallas_call(
        functools.partial(split_kernel, order, dims),
        grid=(len(order),),
        in_specs=[
            pl.BlockSpec((2 * rows, left.shape[1]), place),
            pl.BlockSpec(used, lambda i: (0, 0)),
        ]
        + [ANY] * len(others),
        out_specs=[pl.BlockSpec((rows, width), lambda i: (0, 0))] * (2 * len(order)),
        out_shape=[jax.ShapeDtypeStruct((rows, width), BF)] * (2 * len(order)),
        cost_estimate=cost(3 * len(order) + 2),
        compiler_params=pltpu.CompilerParams(vmem_limit_bytes=56 * 2**20),
    )(left, right, *others)
    return [tuple(out[2 * order.index(r) :][:2]) for r in range(len(order))]


def down_sums_kernel(inner_ref, top_ref, *refs):
    out_ref = refs[-1]
    count, size, _ = out_ref.shape
    found = dot(inner_ref[...], top_ref[...], TN).astype(BF)
    for z in range(count):
        out_ref[z] = found[z * size : (z + 1) * size]


def unit_sums_kernel(hidden_ref, grads_ref, *refs):
    out_ref = refs[-1]
    count, size, tile = out_ref.shape
    columns = grads_ref.shape[1] // tile
    depth = size // columns
    found = dot(hidden_ref[...], grads_ref[...], TN).astype(BF)
    for z in range(count):
        for b in range(columns):
            out_ref[z, b * depth : (b + 1) * depth, :] = found[
                z * depth : (z + 1) * depth, b * tile : (b + 1) * tile
            ]


def unit_sums(hidden, grads, layers, below, *others):
    tokens, width = hidden.shape
    tile = 256
    above = grads.shape[1] // tile * width // layers
    return pl.pallas_call(
        unit_sums_kernel,
        grid=(2,),
        in_specs=[
            pl.BlockSpec((tokens, width // 2), lambda i: (0, i)),
            pl.BlockSpec(grads.shape, lambda i: (0, 0)),
        ]
        + [ANY] * len(others),
        out_specs=pl.BlockSpec((layers // 2, above, tile), lambda i: (i, 0, 0)),
        out_shape=jax.ShapeDtypeStruct((layers, above + below, tile), BF),
        cost_estimate=cost(14),
        compiler_params=pltpu.CompilerParams(vmem_limit_bytes=56 * 2**20),
    )(hidden, grads, *others)


def down_sums(inner, tops, carried, *others):
    tokens, units = inner.shape
    width = tops.shape[1]
    layers, length, tile = carried.shape
    size = units // layers
    above = length - width // tile * size
    return pl.pallas_call(
        down_sums_kernel,
        grid=(width // tile,),
        in_specs=[
            pl.BlockSpec((tokens, units), lambda i: (0, 0)),
            pl.BlockSpec((tokens, tile), lambda i: (0, i)),
        ]
        + [ANY] * (1 + len(others)),
        out_specs=pl.BlockSpec((layers, size, tile), lambda i: (0, above // size + i, 0)),
        out_shape=jax.ShapeDtypeStruct(carried.shape, BF),
        input_output_aliases={2: 0},
        cost_estimate=cost(10),
        compiler_params=pltpu.CompilerParams(vmem_limit_bytes=56 * 2**20),
    )(inner, tops, carried, *others)


def part_sheet_kernel(sum_ref, *refs):
    heads_ref, out_ref = refs[-2:]
    owners, blocks, share, _ = heads_ref.shape
    depth = owners * share
    for b in range(blocks):
        block = sum_ref[b * depth : (b + 1) * depth].astype(F32)
        for p in range(owners):
            heads_ref[p, b] = block[p * share : (p + 1) * share].astype(BF)
    out_ref[...] = sum_ref[blocks * depth :]


def part_sheet(total_sum, share, *others):
    rows, tile = total_sum.shape
    blocks = 6 * HP // tile
    return pl.pallas_call(
        part_sheet_kernel,
        in_specs=[VMEM] + [ANY] * len(others),
        out_specs=[VMEM, VMEM],
        out_shape=[
            jax.ShapeDtypeStruct((8, blocks, share, tile), BF),
            jax.ShapeDtypeStruct((rows - blocks * 8 * share, tile), BF),
        ],
        cost_estimate=cost(2),
        compiler_params=pltpu.CompilerParams(vmem_limit_bytes=32 * 2**20),
    )(total_sum, *others)


def out_owner_kernel(piece_ref, out_ref):
    share, width = out_ref.shape
    size, tile = padded(share), piece_ref.shape[1]
    for i in range(width // tile):
        block = piece_ref[i * size : (i + 1) * size].astype(F32)
        out_ref[:, i * tile : (i + 1) * tile] = block[:share]


def out_owner(piece, share, width):
    return pl.pallas_call(
        out_owner_kernel,
        out_shape=jax.ShapeDtypeStruct((share, width), F32),
        cost_estimate=cost(2),
        compiler_params=pltpu.CompilerParams(vmem_limit_bytes=32 * 2**20),
    )(piece)


def out_sums_kernel(count, *refs):
    blocks, kept_ref, out_ref = refs[:count], refs[count], refs[-1]
    layers, size, _ = out_ref.shape
    found = [dot(kept_ref[i], ref[...], TN) for i, ref in enumerate(blocks)]
    found = functools.reduce(jnp.add, found).astype(BF)
    for z in range(layers):
        out_ref[z] = found[z * size : (z + 1) * size]


def head_sums_kernel(hidden_ref, grads_ref, rim_ref, lead_ref, *refs):
    out_ref = refs[-1]
    count, size, tile = out_ref.shape
    columns = grads_ref.shape[1] // tile
    depth = size // columns
    found = dot(hidden_ref[...], grads_ref[...], TN)
    more = dot(rim_ref[...], lead_ref[...], TN)
    skip = found.shape[1] - more.shape[1]
    found = jnp.concatenate([found[:, :skip], found[:, skip:] + more], axis=1).astype(BF)
    for z in range(count):
        for b in range(columns):
            out_ref[z, b * depth : (b + 1) * depth, :] = found[
                z * depth : (z + 1) * depth, b * tile : (b + 1) * tile
            ]


def head_sums(hidden, grad, rim, lead, layers, rows, *others):
    tokens, width = hidden.shape
    tile = 256
    above = grad.shape[1] // tile * width // layers
    whole = lambda i: (0, 0)
    return pl.pallas_call(
        head_sums_kernel,
        grid=(2,),
        in_specs=[
            pl.BlockSpec((tokens, width // 2), lambda i: (0, i)),
            pl.BlockSpec(grad.shape, whole),
            pl.BlockSpec((rim.shape[0], width // 2), lambda i: (0, i)),
            pl.BlockSpec(lead.shape, whole),
        ]
        + [ANY] * len(others),
        out_specs=pl.BlockSpec((layers // 2, above, tile), lambda i: (i, 0, 0)),
        out_shape=jax.ShapeDtypeStruct((layers, above + rows, tile), BF),
        cost_estimate=cost(11),
        compiler_params=pltpu.CompilerParams(vmem_limit_bytes=56 * 2**20),
    )(hidden, grad, rim, lead, *others)


def out_sums(blocks, kept, carried, *others):
    rows, width = blocks[0].shape
    count, _, depth = kept.shape
    layers, length, tile = carried.shape
    size = depth // layers
    above = length - width // tile * size
    return pl.pallas_call(
        functools.partial(out_sums_kernel, count),
        grid=(width // tile,),
        in_specs=[pl.BlockSpec((rows, tile), lambda i: (0, i))] * count
        + [pl.BlockSpec((count, rows, depth), lambda i: (0, 0, 0))]
        + [ANY] * (1 + len(others)),
        out_specs=pl.BlockSpec((layers, size, tile), lambda i: (0, above // size + i, 0)),
        out_shape=jax.ShapeDtypeStruct(carried.shape, BF),
        input_output_aliases={count + 1: 0},
        cost_estimate=cost(6),
        compiler_params=pltpu.CompilerParams(vmem_limit_bytes=32 * 2**20),
    )(*blocks, kept, carried, *others)


def leave_kernel(here_ref, x_ref, y_ref, own_ref, grad_ref, gain_ref, *refs):
    grad_hidden = here_ref[...] + x_ref[...].astype(F32) + y_ref[...].astype(F32)
    normed, factor = normalize(own_ref[...].astype(F32))
    refs[-1][...] = grad_ref[...] + norm_back(grad_hidden * gain_ref[...], normed, factor)


def leave(terms, own, grad_middle, gain, *others):
    return pl.pallas_call(
        leave_kernel,
        in_specs=[VMEM] * 6 + [ANY] * len(others),
        out_specs=VMEM,
        out_shape=jax.ShapeDtypeStruct(own.shape, F32),
        cost_estimate=cost(6),
        compiler_params=pltpu.CompilerParams(vmem_limit_bytes=32 * 2**20),
    )(*terms, own, grad_middle, gain, *others)


def mend_kernel(info_ref, tail_ref, back_ref, cur_ref, *refs):
    out_ref = refs[-1]
    out_ref[:, : 2 * HP] = cur_ref[:, : 2 * HP]
    out_ref[:, 2 * HP :] = (tail_ref[...] + back_ref[...].astype(F32)).astype(BF)


def mend(info, tail, back, grad_qkv, *others):
    rows, blocks = grad_qkv.shape[1], grad_qkv.shape[0] // 2
    side = pl.BlockSpec((None, WINDOW, 4 * HP), lambda s, info: (s, 0, 0))
    edge = pl.BlockSpec(
        (None, WINDOW, 6 * HP),
        lambda s, info: (2 * ((blocks - 1) ^ info[0]) + s, rows // WINDOW - 1, 0),
    )
    return pl.pallas_call(
        mend_kernel,
        grid_spec=pltpu.PrefetchScalarGridSpec(
            num_scalar_prefetch=1,
            grid=(2,),
            in_specs=[side, side, edge] + [ANY] * len(others),
            out_specs=edge,
        ),
        out_shape=jax.ShapeDtypeStruct(grad_qkv.shape, BF),
        cost_estimate=cost(2),
        input_output_aliases={3: 0},
    )(info, tail, back, grad_qkv, *others)


def first_key(at, rows):
    return min(at, rows + WINDOW - SPAN)


def shares_of(raws, cut, rows):
    row = lax.broadcasted_iota(jnp.int32, (SUB, SPAN), 0)
    col = lax.broadcasted_iota(jnp.int32, (SUB, SPAN), 1)
    seen = {}
    for at in range(0, rows, SUB):
        shift = at - first_key(at, rows)
        valid = (col > row + shift) & (col <= row + (shift + WINDOW))
        seen[at] = valid & (col >= cut) if at == 0 else valid
    scores = [jnp.where(seen[at], raw, MASKED) for at, raw in raws]
    peaks = [jnp.max(score, axis=-1, keepdims=True) for score in scores]
    powers = [jnp.exp((s - p) * (HD ** (-0.5))) for s, p in zip(scores, peaks)]
    totals = [jnp.sum(power, axis=-1, keepdims=True) for power in powers]
    return [power * (1.0 / total) for power, total in zip(powers, totals)]


def joined(prev_ref, halo_ref, cur_ref, at_first, lo):
    before = jnp.where(
        at_first, halo_ref[:, lo - 2 * HP : lo - HP], prev_ref[:, lo : lo + HP]
    )
    return jnp.concatenate([before, cur_ref[:, lo : lo + HP]], axis=0)


def tiles_of(rows):
    return [(h, at, first_key(at, rows)) for h in range(2) for at in range(0, rows, SUB)]


def attend_kernel(info_ref, cur_ref, prev_ref, halo_ref, *refs):
    flat_ref, kept_ref = refs[-2:]
    stream, block = pl.program_id(0), pl.program_id(1)
    at_first = block == 0
    cut = jnp.where(at_first & (info_ref[2 + stream] == 1), WINDOW, 0)
    rows = cur_ref.shape[0]
    tiles = tiles_of(rows)
    keys = [joined(prev_ref, halo_ref, cur_ref, at_first, (2 + h) * HP) for h in range(2)]
    values = [joined(prev_ref, halo_ref, cur_ref, at_first, (4 + h) * HP) for h in range(2)]
    raws = [
        (at, dot(cur_ref[at : at + SUB, h * HP : (h + 1) * HP], keys[h][lo : lo + SPAN], NT))
        for h, at, lo in tiles
    ]
    shares = [share.astype(BF) for share in shares_of(raws, cut, rows)]
    mixes = [dot(share, values[h][lo : lo + SPAN]) for share, (h, at, lo) in zip(shares, tiles)]
    for mixed, (h, at, lo) in zip(mixes, tiles):
        mixed = mixed.astype(BF)
        flat_ref[at : at + SUB, h * HP : (h + 1) * HP] = mixed
        kept_ref[at : at + SUB, h * HP : (h + 1) * HP] = mixed


def attend(qkv, halo, info, *others):
    rows, blocks = qkv.shape[1], qkv.shape[0] // 2
    mine = lambda s, b, info: (2 * (b ^ info[0]) + s, 0, 0)
    before = lambda s, b, info: (2 * (jnp.maximum(b - 1, 0) ^ info[0]) + s, rows // WINDOW - 1, 0)
    spec = pltpu.PrefetchScalarGridSpec(
        num_scalar_prefetch=1,
        grid=(2, blocks),
        in_specs=[
            pl.BlockSpec((None, rows, 6 * HP), mine),
            pl.BlockSpec((None, WINDOW, 6 * HP), before),
            pl.BlockSpec((None, WINDOW, 4 * HP), lambda s, b, info: (s, 0, 0)),
        ]
        + [ANY] * len(others),
        out_specs=[
            pl.BlockSpec((None, rows, 2 * HP), lambda s, b, info: (2 * b + (s ^ info[1]), 0, 0)),
            pl.BlockSpec((None, rows, 2 * HP), mine),
        ],
    )
    shape = jax.ShapeDtypeStruct((2 * blocks, rows, 2 * HP), BF)
    return pl.pallas_call(
        attend_kernel,
        grid_spec=spec,
        out_shape=[shape, pltpu.HBM(shape.shape, shape.dtype)],
        cost_estimate=cost(8),
        compiler_params=pltpu.CompilerParams(vmem_limit_bytes=32 * 2**20),
    )(info, qkv, qkv, halo, *others)


def attend_back_kernel(
    info_ref, cur_ref, prev_ref, halo_ref, top_ref, *refs
):
    out_ref, tail_ref, lead_ref, keep, acc = refs[-5:]
    stream, step = pl.program_id(0), pl.program_id(1)
    blocks = pl.num_programs(1)
    at_first = step == blocks - 1
    cut = jnp.where(at_first & (info_ref[2 + stream] == 1), WINDOW, 0)
    rows = cur_ref.shape[0]

    @pl.when(step == 0)
    def _():
        keep[...] = jnp.zeros_like(keep)

    acc[...] = jnp.zeros_like(acc)
    tiles = tiles_of(rows)
    keys = [joined(prev_ref, halo_ref, cur_ref, at_first, (2 + h) * HP) for h in range(2)]
    values = [joined(prev_ref, halo_ref, cur_ref, at_first, (4 + h) * HP) for h in range(2)]
    queries = [cur_ref[at : at + SUB, h * HP : (h + 1) * HP] for h, at, lo in tiles]
    tops = [top_ref[at : at + SUB, h * HP : (h + 1) * HP] for h, at, lo in tiles]
    raws = [
        (at, dot(query, keys[h][lo : lo + SPAN], NT)) for query, (h, at, lo) in zip(queries, tiles)
    ]
    grads = [dot(top, values[h][lo : lo + SPAN], NT) for top, (h, at, lo) in zip(tops, tiles)]
    shares = shares_of(raws, cut, rows)
    spent = [
        jnp.sum(share * grad, axis=-1, keepdims=True) for share, grad in zip(shares, grads)
    ]
    grads = [
        (share * ((grad - sum_) * (HD ** (-0.5)))).astype(BF)
        for share, grad, sum_ in zip(shares, grads, spent)
    ]
    shares = [share.astype(BF) for share in shares]
    for share, grad, query, top, (h, at, lo) in zip(shares, grads, queries, tops, tiles):
        left, right = h * HP, (h + 1) * HP
        out_ref[at : at + SUB, left:right] = dot(grad, keys[h][lo : lo + SPAN]).astype(BF)
        acc[lo : lo + SPAN, left:right] += dot(grad, query, TN)
        acc[lo : lo + SPAN, 2 * HP + left : 2 * HP + right] += dot(share, top, TN)
    last = acc[rows : rows + WINDOW, :] + keep[...]
    out_ref[: rows - WINDOW, 2 * HP :] = acc[WINDOW:rows, :].astype(BF)
    out_ref[rows - WINDOW :, 2 * HP :] = last.astype(BF)
    keep[...] = acc[:WINDOW, :]

    @pl.when(step == 0)
    def _():
        tail_ref[...] = last

    @pl.when(at_first)
    def _():
        lead_ref[...] = acc[:WINDOW, :].astype(BF)


def attend_back(qkv, halo, top, info, *others):
    rows, blocks = qkv.shape[1], qkv.shape[0] // 2
    at = lambda t: blocks - 1 - t
    mine = lambda s, t, info: (2 * (at(t) ^ info[0]) + s, 0, 0)
    before = lambda s, t, info: (
        2 * (jnp.maximum(at(t) - 1, 0) ^ info[0]) + s,
        rows // WINDOW - 1,
        0,
    )
    side = lambda s, t, info: (s, 0, 0)
    spec = pltpu.PrefetchScalarGridSpec(
        num_scalar_prefetch=1,
        grid=(2, blocks),
        in_specs=[
            pl.BlockSpec((None, rows, 6 * HP), mine),
            pl.BlockSpec((None, WINDOW, 6 * HP), before),
            pl.BlockSpec((None, WINDOW, 4 * HP), side),
            pl.BlockSpec(
                (None, rows, 2 * HP), lambda s, t, info: (2 * at(t) + (s ^ info[1]), 0, 0)
            ),
        ]
        + [ANY] * len(others),
        out_specs=[
            pl.BlockSpec((None, rows, 6 * HP), mine),
            pl.BlockSpec((None, WINDOW, 4 * HP), side),
            pl.BlockSpec((None, WINDOW, 4 * HP), side),
        ],
        scratch_shapes=[
            pltpu.VMEM((WINDOW, 4 * HP), F32),
            pltpu.VMEM((rows + WINDOW, 4 * HP), F32),
        ],
    )
    return pl.pallas_call(
        attend_back_kernel,
        grid_spec=spec,
        out_shape=[
            jax.ShapeDtypeStruct(qkv.shape, BF),
            jax.ShapeDtypeStruct(halo.shape, F32),
            jax.ShapeDtypeStruct(halo.shape, BF),
        ],
        cost_estimate=cost(17),
        compiler_params=pltpu.CompilerParams(vmem_limit_bytes=32 * 2**20),
    )(info, qkv, qkv, halo, top, *others)


def body(
    inputs,
    starts,
    attn_gain,
    query_weight,
    key_weight,
    value_weight,
    out_weight,
    ffn_gain,
    gate_weight,
    up_weight,
    down_weight,
    cotangent,
):
    rows, width = inputs.shape[1:]
    layers = lax.axis_size("z")
    devices = 8 * layers
    share = query_weight.shape[0]
    part = down_weight.shape[0]
    units = -(-part // 16) * 16 * layers
    me_z = lax.axis_index("z")
    me_block = 2 * lax.axis_index("y") + lax.axis_index("x")
    me_core = lax.axis_index("c")

    own = inputs[0]
    top = cotangent[0]
    own_gains = jnp.stack([attn_gain, ffn_gain]).astype(F32)
    heads = head_sheet(query_weight, key_weight, value_weight, own_gains, starts)
    down = jnp.pad(down_weight, ((0, units // layers - part), (0, 0)))
    down = lax.all_gather(down, "z", axis=0, tiled=True)
    heads = lax.all_to_all(heads, PLANE, 0, 0, tiled=True)
    opened = heads[:2, 0, extra_column(2, share)].astype(jnp.int32)
    opened = jnp.where(me_core == 0, opened, opened[::-1])
    info = jnp.concatenate([jnp.stack([me_block, me_core]), opened, me_z[None]]).astype(jnp.int32)
    from_x, from_y = neighbours(held(own, heads))
    far = join(*diagonal(from_x, from_y))
    streams = both_cores([own, from_x, from_y, far])
    attn_weight = attn_sheet(heads, out_weight, down, from_x, from_y)
    attn_weight = lax.all_gather(attn_weight, "z", axis=0, tiled=True)
    stream = jnp.concatenate(streams, axis=0)
    factor = normalize(stream.astype(F32))[1]
    sheet = unit_sheet(gate_weight, up_weight, layers, part, units, heads)
    sheet = lax.all_to_all(sheet, PLANE, 0, 0, tiled=True).reshape(8 * share, 2 * units)
    gate_up = lax.all_gather(sheet, "z", axis=0, tiled=True)
    from_x, from_y = neighbours(held(top, streams[6]))
    first, second = halves(from_x, from_y)
    tops = [top, from_x, from_y]
    far_top = swap(first, "x"), swap(second, "y")

    hidden1, qkv, gains = enter(stream, factor, attn_weight, rows, share, first)
    gain_attn, gain_ffn = gains[0:1], gains[1:2]
    qkv = qkv.reshape(8, rows, 6 * HP)
    last = 2 * (3 ^ me_block)
    rim = lax.dynamic_slice(qkv, (last, rows - WINDOW, 2 * HP), (2, WINDOW, 4 * HP))
    halo = lax.ppermute(rim, "z", [(i, i + 1) for i in range(layers - 1)])
    own_out = attn_weight[:, 6 * HP :]
    from_x, from_y = neighbours(own_out)
    far = diagonal(from_x, from_y, halo)
    flat, kept = attend(qkv, halo, info)
    full_out = both_cores([own_out, from_x, from_y, join(*far, flat)])
    full_out = out_sheet(full_out, info, layers)
    tops = both_cores(tops + [join(*far_top, flat)])
    rim = lax.dynamic_slice(
        hidden1.reshape(8, rows, width), (last, rows - WINDOW, 0), (2, WINDOW, width)
    )
    rim = lax.ppermute(rim, "z", [(i, i + 1) for i in range(layers - 1)])
    mixed = lax.all_to_all(flat, PLANE, 0, 0, tiled=True)
    middle, hidden2 = project(mixed, full_out, own, gain_ffn, tops[6])

    from_x, from_y = neighbours(hidden2)
    far = diagonal(from_x, from_y)
    carried, near = ffn(
        both_cores([hidden2, from_x, from_y]), tops[:6], gate_up, down, 0
    )
    far = join(*far, carried[0])
    (inner, grads, hidden2, tops), far = ffn(
        both_cores([far]), tops[6:], gate_up, down, 3, carried
    )
    terms, sent, far = plane_sum([near[:2], near[2:4], near[4:], far])
    ffn_part = unit_sums(hidden2, grads, layers, width // 256 * units // layers, far, rim)
    ffn_part = down_sums(inner, tops, ffn_part, *sent)
    out_parts = split(inner, down, NN, (3, 2, 1, 0), rows, [ffn_part])
    ffn_sum = lax.psum_scatter(ffn_part, "z", scatter_dimension=0, tiled=True)[0]

    grad_mixed, grad_middle, grad_branch = unproject(
        terms, middle, top, gain_ffn, full_out, out_parts[3][0]
    )

    grad_mixed = lax.all_to_all(grad_mixed, PLANE, 0, 0, tiled=True)
    from_x, from_y = neighbours(grad_branch)
    grad_qkv, tail, lead = attend_back(qkv, halo, grad_mixed, info)
    back = lax.ppermute(lead, "z", [(i + 1, i) for i in range(layers - 1)])
    out_terms, sent, _ = plane_sum(out_parts, tail)
    attn_part = head_sums(
        hidden1,
        grad_qkv.reshape(8 * rows, 6 * HP),
        rim.reshape(2 * WINDOW, width),
        lead.reshape(2 * WINDOW, 4 * HP),
        layers,
        8 * share,
    )
    branches = join(*diagonal(from_x, from_y, attn_part))
    branches = both_cores([grad_branch, from_x, from_y, branches])
    grad_qkv = mend(info, tail, back, grad_qkv, attn_part).reshape(8 * rows, 6 * HP)
    attn_part = out_sums(branches, kept, attn_part, grad_qkv, *sent)
    attn_sum = lax.psum_scatter(attn_part, "z", scatter_dimension=0, tiled=True)[0]
    layer_out = (middle + total(out_terms)).astype(BF)
    above = 2 * units // 256 * 8 * share
    gate_up_sum = ffn_sum[:above].reshape(-1, 8, share, 256).swapaxes(0, 1)
    gate_up_sum = lax.all_to_all(gate_up_sum, PLANE, 0, 0, tiled=True)
    gate_grad, up_grad, ffn_gain_grad = unit_owner(
        gate_up_sum, (gate_weight, up_weight), own_gains[1:2], layers, part
    )
    down_grad = ffn_sum[above:].reshape(width // 256, -1, 256).swapaxes(0, 1)
    down_grad = down_grad[:part].reshape(part, width).astype(F32)
    parts = split(grad_qkv, attn_weight, NT, (3, 2, 1, 0), rows, [attn_part])
    terms, _, _ = plane_sum(parts, *out_terms[1:])
    input_grad = leave(terms, own, grad_middle, gain_attn, gate_grad)

    qkv_sum, out_sum = part_sheet(attn_sum, share, input_grad, layer_out)
    qkv_sum = lax.all_to_all(qkv_sum, PLANE, 0, 0, tiled=True)
    query_grad, key_grad, value_grad, attn_gain_grad = head_owner(
        qkv_sum, (query_weight, key_weight, value_weight), own_gains[0:1]
    )
    route = [(8 * z + p, layers * p + z) for z in range(layers) for p in range(8)]
    output_grad = out_owner(lax.ppermute(out_sum, ALL, route), share, width)
    return (
        layer_out[None],
        input_grad[None],
        attn_gain_grad[0],
        query_grad,
        key_grad,
        value_grad,
        output_grad,
        ffn_gain_grad[0],
        gate_grad,
        up_grad,
        down_grad,
    )


def solution(mesh):
    blocks = mesh.shape["seq"]
    fine = Mesh(mesh.devices.reshape(blocks // 4, 2, 2, 2), ALL)
    tokens = P("c", ("z", "y", "x"), None)
    weight = P(ALL, None)
    gain = P(ALL)
    in_specs = (
        tokens,
        P("c", ("z", "y", "x")),
        gain,
        weight,
        weight,
        weight,
        weight,
        gain,
        weight,
        weight,
        weight,
        tokens,
    )
    out_specs = (
        tokens,
        tokens,
        gain,
        weight,
        weight,
        weight,
        weight,
        gain,
        weight,
        weight,
        weight,
    )
    return jax.shard_map(body, mesh=fine, in_specs=in_specs, out_specs=out_specs, check_vma=False)
```

```python
import functools

import jax
import jax.numpy as jnp
from jax import lax
from jax.experimental import pallas as pl
from jax.experimental.pallas import tpu as pltpu
from jax.sharding import Mesh, PartitionSpec as P

H = 16
HD = 112
HP = 128
WINDOW = 64
EPS = 1e-06
MASKED = -1e30
SUB = 128
SPAN = 256

BF = jnp.bfloat16
F32 = jnp.float32
ALL = ("z", "y", "x", "c")
PLANE = ("y", "x", "c")
SWAP = [(0, 1), (1, 0)]
NT = (((1,), (1,)), ((), ()))
TN = (((0,), (0,)), ((), ()))
NN = (((1,), (0,)), ((), ()))


def cost(us):
    return pl.CostEstimate(flops=int(us * 1.1e9), bytes_accessed=int(us * 3.5e6), transcendentals=0)


def swap(block, axis):
    return lax.ppermute(block, axis, SWAP)


def normalize(values):
    factor = lax.rsqrt(jnp.mean(values * values, axis=-1, keepdims=True) + EPS)
    return (values * factor, factor)


def norm_back(grad_normed, normed_rows, factor):
    return factor * (
        grad_normed - normed_rows * jnp.mean(grad_normed * normed_rows, axis=-1, keepdims=True)
    )


def dot(left, right, dims=NN):
    return lax.dot_general(left, right, dims, preferred_element_type=F32)


ANY = pl.BlockSpec(memory_space=pl.ANY)


VMEM = pl.BlockSpec(memory_space=pltpu.VMEM)
SMEM = pl.BlockSpec(memory_space=pltpu.SMEM)


def held_kernel(source_ref, *refs):
    refs[-1][...] = source_ref[...]


def held(value, *others):
    return pl.pallas_call(
        held_kernel,
        in_specs=[VMEM] + [ANY] * len(others),
        out_specs=VMEM,
        out_shape=jax.ShapeDtypeStruct(value.shape, value.dtype),
        cost_estimate=cost(2),
        compiler_params=pltpu.CompilerParams(vmem_limit_bytes=32 * 2**20),
    )(value, *others)


def stack_kernel(count, *refs):
    for k in range(count):
        refs[-1][k] = refs[k][...]


def stack(pieces, *others):
    count = len(pieces)
    return pl.pallas_call(
        functools.partial(stack_kernel, count),
        in_specs=[VMEM] * count + [ANY] * len(others),
        out_specs=VMEM,
        out_shape=jax.ShapeDtypeStruct((count, *pieces[0].shape), pieces[0].dtype),
        cost_estimate=cost(2),
        compiler_params=pltpu.CompilerParams(vmem_limit_bytes=32 * 2**20),
    )(*pieces, *others)


def neighbours(own):
    return swap(own, "x"), swap(own, "y")


def across(own):
    return lax.ppermute(own, ("y", "x"), [(i, i ^ 3) for i in range(4)])


def join_kernel(first_ref, second_ref, *refs):
    half = first_ref.shape[0]
    refs[-1][:half] = first_ref[...]
    refs[-1][half:] = second_ref[...]


def join(first, second, *others):
    shape = (2 * first.shape[0], *first.shape[1:])
    return pl.pallas_call(
        join_kernel,
        in_specs=[VMEM] * 2 + [ANY] * len(others),
        out_specs=VMEM,
        out_shape=jax.ShapeDtypeStruct(shape, first.dtype),
        cost_estimate=cost(2),
        compiler_params=pltpu.CompilerParams(vmem_limit_bytes=32 * 2**20),
    )(first, second, *others)


def halves_kernel(x_ref, y_ref, *refs):
    half = x_ref.shape[0] // 2
    refs[-2][...] = y_ref[:half]
    refs[-1][...] = x_ref[half:]


def halves(from_x, from_y, *others):
    shape = jax.ShapeDtypeStruct((from_x.shape[0] // 2, *from_x.shape[1:]), from_x.dtype)
    return pl.pallas_call(
        halves_kernel,
        in_specs=[VMEM] * 2 + [ANY] * len(others),
        out_specs=[VMEM] * 2,
        out_shape=[shape, shape],
        cost_estimate=cost(2),
        compiler_params=pltpu.CompilerParams(vmem_limit_bytes=32 * 2**20),
    )(from_x, from_y, *others)


def diagonal(from_x, from_y, *others):
    first, second = halves(from_x, from_y, *others)
    return swap(first, "x"), swap(second, "y")


def both_cores(blocks):
    return [block for mine in blocks for block in (mine, swap(mine, "c"))]


def add_kernel(mine_ref, other_ref, *refs):
    refs[-1][...] = (mine_ref[...].astype(F32) + other_ref[...].astype(F32)).astype(BF)


def add(mine, other, *others):
    return pl.pallas_call(
        add_kernel,
        in_specs=[VMEM] * 2 + [ANY] * len(others),
        out_specs=VMEM,
        out_shape=jax.ShapeDtypeStruct(mine.shape, BF),
        cost_estimate=cost(2),
        compiler_params=pltpu.CompilerParams(vmem_limit_bytes=32 * 2**20),
    )(mine, other, *others)


def plane_sum(parts, *others):
    half = parts[0][0].shape[0] // 2
    other = {r: swap(parts[r][1], "c") for r in (3, 2, 1, 0)}
    far = add(parts[3][0], other[3], *others)
    first = swap(far[:half], "x")
    second = swap(far[half:], "y")
    along_y, along_x, here = (parts[r][0].astype(F32) + other[r].astype(F32) for r in (2, 1, 0))
    along_y = jnp.concatenate([along_y[:half] + first.astype(F32), along_y[half:]], axis=0).astype(BF)
    along_x = jnp.concatenate([along_x[:half], along_x[half:] + second.astype(F32)], axis=0).astype(BF)
    return (here, swap(along_x, "x"), swap(along_y, "y")), (along_x, along_y), far


def total(terms):
    here, got_x, got_y = terms
    return here + got_x.astype(F32) + got_y.astype(F32)


def direct_gather(block, count):
    return [block] + [
        lax.ppermute(block, "z", [(i, (i + k) % count) for i in range(count)])
        for k in range(1, count)
    ]


def padded(share):
    return share * HP // HD


def head_sheet_kernel(starts_ref, query_ref, key_ref, value_ref, gains_ref, out_ref):
    rows = query_ref.shape[0]
    spare = padded(rows) - rows
    same = lax.broadcasted_iota(jnp.int32, (rows, rows), 0) == lax.broadcasted_iota(
        jnp.int32, (rows, rows), 1
    )
    extra = [
        jnp.sum(
            jnp.where(same, jnp.broadcast_to(gains_ref[i : i + 1, :], (rows, rows)), 0.0),
            axis=1,
            keepdims=True,
        )
        for i in range(2)
    ]
    extra = extra + [jnp.full((rows, 1), starts_ref[0, 0], jnp.int32).astype(F32)]
    extra = jnp.concatenate(extra + [jnp.zeros((rows, HP - HD - 3), F32)], axis=1).astype(BF)
    for i, ref in enumerate((query_ref, key_ref, value_ref)):
        for h in range(H):
            pieces = []
            for a in range(HD // rows):
                pieces.append(ref[:, h * HD + a * rows : h * HD + (a + 1) * rows])
                if i == 0 and h % 2 == 0:
                    pieces.append(extra[:, a * spare : (a + 1) * spare])
                else:
                    pieces.append(jnp.zeros((rows, spare), BF))
            lo = (2 * i + h % 2) * HP
            out_ref[h // 2, :, lo : lo + HP] = jnp.concatenate(pieces, axis=1)


def head_sheet(query, key, value, gains, starts):
    whole = pl.BlockSpec(memory_space=pltpu.VMEM)
    return pl.pallas_call(
        head_sheet_kernel,
        in_specs=[pl.BlockSpec(memory_space=pltpu.SMEM)] + [whole] * 4,
        out_specs=whole,
        out_shape=jax.ShapeDtypeStruct((8, query.shape[0], 6 * HP), BF),
        cost_estimate=cost(2),
        compiler_params=pltpu.CompilerParams(vmem_limit_bytes=32 * 2**20),
    )(starts, query, key, value, gains)


def extra_column(j, share):
    spare = padded(share) - share
    return j // spare * padded(share) + share + j % spare


def attn_sheet_kernel(heads_ref, out_weight_ref, *refs):
    sheet_ref = refs[-1]
    count, rows, columns = heads_ref.shape
    size, tile = padded(rows), sheet_ref.shape[1] - columns
    heads = [heads_ref[p].astype(F32) for p in range(count)]
    sheet_ref[:, :columns] = jnp.concatenate(heads, axis=0).astype(BF)
    blank = jnp.zeros((size - rows, tile), F32)
    blocks = []
    for i in range(out_weight_ref.shape[1] // tile):
        blocks += [out_weight_ref[:, i * tile : (i + 1) * tile].astype(F32), blank]
    sheet_ref[:, columns:] = jnp.concatenate(blocks, axis=0).astype(BF)


def attn_sheet(heads, out_weight, *others):
    count, rows, columns = heads.shape
    return pl.pallas_call(
        attn_sheet_kernel,
        in_specs=[VMEM] * 2 + [ANY] * len(others),
        out_shape=jax.ShapeDtypeStruct((count * rows, columns + 256), BF),
        cost_estimate=cost(2),
        compiler_params=pltpu.CompilerParams(vmem_limit_bytes=32 * 2**20),
    )(heads, out_weight, *others)


def out_sheet_kernel(info_ref, *refs):
    *blocks, out_ref = refs
    layers, size, width = out_ref.shape
    tile = blocks[0].shape[1]
    count = width // tile
    for r, block in enumerate(blocks):

        @pl.when(pl.program_id(0) == r)
        def _():
            for z in range(layers):
                for i in range(count):
                    at = (z * count + i) * size
                    out_ref[z, :, i * tile : (i + 1) * tile] = block[at : at + size, :]


def out_sheet(blocks, info, layers):
    depth, tile = blocks[0].shape
    size, width = 2 * HP // layers, depth * tile * 8 // (16 * HP)
    place = lambda r, info: (0, 2 * ((r // 2) ^ info[0]) + ((r % 2) ^ info[1]), 0, 0)
    out = pl.pallas_call(
        out_sheet_kernel,
        grid_spec=pltpu.PrefetchScalarGridSpec(
            num_scalar_prefetch=1,
            grid=(8,),
            in_specs=[pl.BlockSpec((depth, tile), lambda r, info: (0, 0))] * 8,
            out_specs=pl.BlockSpec((layers, None, size, width), place),
        ),
        out_shape=pltpu.HBM((layers, 8, size, width), BF),
        cost_estimate=cost(6),
        compiler_params=pltpu.CompilerParams(vmem_limit_bytes=32 * 2**20),
    )(info, *blocks)
    return out.reshape(-1, width)


def unit_sheet_kernel(layers, part, gate_ref, up_ref, *refs):
    out_ref = refs[-1]
    units = out_ref.shape[2] // 2
    blank = jnp.zeros((gate_ref.shape[0], units // layers - part), BF)
    for w, ref in enumerate((gate_ref, up_ref)):
        for p in range(8):
            pieces = []
            for z in range(layers):
                pieces.append(ref[:, (8 * z + p) * part : (8 * z + p + 1) * part])
                pieces.append(blank)
            out_ref[p, :, w * units : (w + 1) * units] = jnp.concatenate(pieces, axis=1)


def unit_sheet(gate, up, layers, part, units, *others):
    return pl.pallas_call(
        functools.partial(unit_sheet_kernel, layers, part),
        in_specs=[pl.BlockSpec(memory_space=pltpu.VMEM)] * 2 + [ANY] * len(others),
        out_shape=jax.ShapeDtypeStruct((8, gate.shape[0], 2 * units), BF),
        cost_estimate=cost(2),
        compiler_params=pltpu.CompilerParams(vmem_limit_bytes=32 * 2**20),
    )(gate, up, *others)


def gain_row(products, gain):
    rows = products.shape[0]
    same = lax.broadcasted_iota(jnp.int32, (rows, rows), 0) == lax.broadcasted_iota(
        jnp.int32, (rows, rows), 1
    )
    row = jnp.sum(jnp.where(same, jnp.broadcast_to(products, (rows, rows)), 0.0), axis=0, keepdims=True)
    return row / gain


def head_owner_kernel(sheet_ref, *refs):
    weights, gain_ref, (*grads, gain_grad_ref) = refs[:3], refs[3], refs[4:]
    rows = weights[0].shape[0]
    products = jnp.zeros((rows, 1), F32)
    for i, ref in enumerate(grads):
        pieces = []
        for h in range(H):
            lo = (h % 2) * HP
            pieces += [
                sheet_ref[h // 2, i, :, lo + a * padded(rows) : lo + a * padded(rows) + rows]
                for a in range(HD // rows)
            ]
        grad = jnp.concatenate(pieces, axis=1).astype(F32)
        ref[...] = grad
        products += jnp.sum(grad * weights[i][...].astype(F32), axis=1, keepdims=True)
    gain_grad_ref[...] = gain_row(products, gain_ref[...])


def head_owner(sheet, weights, gain):
    share, width = weights[0].shape
    shape = jax.ShapeDtypeStruct((share, width), F32)
    return pl.pallas_call(
        head_owner_kernel,
        out_shape=[shape, shape, shape, jax.ShapeDtypeStruct((1, share), F32)],
        cost_estimate=cost(3),
        compiler_params=pltpu.CompilerParams(vmem_limit_bytes=32 * 2**20),
    )(sheet, *weights, gain)


def unit_owner_kernel(layers, part, sheet_ref, *refs):
    weights, gain_ref, (*grads, gain_grad_ref) = refs[:2], refs[2], refs[3:]
    _, columns, rows, tile = sheet_ref.shape
    units = columns * tile // 2
    owned = [
        jnp.concatenate([sheet_ref[p, b] for b in range(columns)], axis=1).astype(F32)
        for p in range(8)
    ]
    products = jnp.zeros((rows, 1), F32)
    for w, ref in enumerate(grads):
        for z in range(layers):
            lo = w * units + z * (units // layers)
            at = slice(8 * z * part, 8 * (z + 1) * part)
            grad = jnp.concatenate([value[:, lo : lo + part] for value in owned], axis=1)
            ref[:, at] = grad
            products += jnp.sum(grad * weights[w][:, at].astype(F32), axis=1, keepdims=True)
    gain_grad_ref[...] = gain_row(products, gain_ref[...])


def unit_owner(sheet, weights, gain, layers, part):
    share, columns = weights[0].shape
    shape = jax.ShapeDtypeStruct((share, columns), F32)
    return pl.pallas_call(
        functools.partial(unit_owner_kernel, layers, part),
        out_shape=[shape, shape, jax.ShapeDtypeStruct((1, share), F32)],
        cost_estimate=cost(3),
        compiler_params=pltpu.CompilerParams(vmem_limit_bytes=32 * 2**20),
    )(sheet, *weights, gain)


def enter_kernel(share, stream_ref, factor_ref, weight_ref, *refs):
    hidden_ref, qkv_ref, gains_ref = refs[-3:]

    @pl.when(pl.program_id(0) == 0)
    def _():
        row = lax.broadcasted_iota(jnp.int32, (8, HP), 0)
        col = lax.broadcasted_iota(jnp.int32, (8, HP), 1)
        pick = (row == 0) & (col == extra_column(0, share))
        pick = pick | ((row == 1) & (col == extra_column(1, share)))
        pick = pick.astype(F32).astype(BF)
        gains_ref[...] = dot(pick, weight_ref[:, :HP], NT)

    normed = stream_ref[...].astype(F32) * factor_ref[...]
    hidden = (normed * gains_ref[0:1, :]).astype(BF)
    hidden_ref[...] = hidden
    qkv_ref[...] = dot(hidden, weight_ref[...]).astype(BF)


def enter(stream, factor, weight, rows, share, *others):
    tokens, width = stream.shape
    whole = lambda i: (0, 0)
    tile = lambda columns: pl.BlockSpec((rows, columns), lambda i: (i, 0))
    return pl.pallas_call(
        functools.partial(enter_kernel, share),
        grid=(tokens // rows,),
        in_specs=[tile(width), tile(1), pl.BlockSpec((width, 6 * HP), whole)] + [ANY] * len(others),
        out_specs=[tile(width), tile(6 * HP), pl.BlockSpec((8, width), whole)],
        out_shape=[
            pltpu.HBM((tokens, width), BF),
            pltpu.HBM((tokens, 6 * HP), BF),
            jax.ShapeDtypeStruct((8, width), F32),
        ],
        cost_estimate=cost(12),
        compiler_params=pltpu.CompilerParams(vmem_limit_bytes=32 * 2**20),
    )(stream, factor, weight, *others)


def project_kernel(mixed_ref, weight_ref, input_ref, gain_ref, *refs):
    middle_ref, hidden_ref = refs[-2:]
    step = pl.program_id(0)

    @pl.when(step == 0)
    def _():
        middle_ref[...] = input_ref[...].astype(F32)

    middle_ref[...] += jnp.dot(mixed_ref[...], weight_ref[...], preferred_element_type=F32)

    @pl.when(step == pl.num_programs(0) - 1)
    def _():
        normed, _ = normalize(middle_ref[...])
        hidden_ref[...] = (normed * gain_ref[...]).astype(BF)


def project(mixed, weight, own, gain, *others):
    count, rows, depth = mixed.shape
    width = own.shape[1]
    whole = lambda p: (0, 0)
    return pl.pallas_call(
        project_kernel,
        grid=(count,),
        in_specs=[
            pl.BlockSpec((None, rows, depth), lambda p: (p, 0, 0)),
            pl.BlockSpec((depth, width), lambda p: (p, 0)),
            pl.BlockSpec((rows, width), whole),
            pl.BlockSpec((1, width), whole),
        ]
        + [ANY] * len(others),
        out_specs=[pl.BlockSpec((rows, width), whole), pl.BlockSpec((rows, width), whole)],
        out_shape=[
            jax.ShapeDtypeStruct((rows, width), F32),
            jax.ShapeDtypeStruct((rows, width), BF),
        ],
        cost_estimate=cost(7),
        compiler_params=pltpu.CompilerParams(vmem_limit_bytes=32 * 2**20),
    )(mixed, weight, own, gain, *others)


def unproject_kernel(
    here_ref, x_ref, y_ref, middle_ref, top_ref, gain_ref, weight_ref, *refs
):
    out_ref, grad_ref, branch_ref = refs[-3:]

    @pl.when(pl.program_id(0) == 0)
    def _():
        grad_hidden = here_ref[...] + x_ref[...].astype(F32) + y_ref[...].astype(F32)
        normed, factor = normalize(middle_ref[...])
        grad = top_ref[...].astype(F32) + norm_back(grad_hidden * gain_ref[...], normed, factor)
        grad_ref[...] = grad
        branch_ref[...] = grad.astype(BF)

    out_ref[...] = lax.dot_general(
        branch_ref[...], weight_ref[...], NT, preferred_element_type=F32
    ).astype(BF)


def unproject(terms, middle, top, gain, weight, *others):
    rows, width = middle.shape
    depth = weight.shape[0] // 8
    full = pl.BlockSpec((rows, width), lambda p: (0, 0))
    line = pl.BlockSpec((1, width), lambda p: (0, 0))
    return pl.pallas_call(
        unproject_kernel,
        grid=(8,),
        in_specs=[full] * 5
        + [line, pl.BlockSpec((depth, width), lambda p: (p, 0))]
        + [ANY] * len(others),
        out_specs=[pl.BlockSpec((None, rows, depth), lambda p: (p, 0, 0)), full, full],
        out_shape=[
            jax.ShapeDtypeStruct((8, rows, depth), BF),
            jax.ShapeDtypeStruct((rows, width), F32),
            jax.ShapeDtypeStruct((rows, width), BF),
        ],
        cost_estimate=cost(12),
        compiler_params=pltpu.CompilerParams(vmem_limit_bytes=48 * 2**20),
    )(*terms, middle, top, gain, weight, *others)


def ffn_kernel(count, kept, *refs):
    blocks, tops, refs = refs[:count], refs[count : 2 * count], refs[2 * count :]
    gate_up_ref, down_ref, refs = refs[0], refs[1], refs[2 + kept :]
    inner_ref, grads_ref, hidden_ref, top_ref = refs[:4]
    backs, (held_hidden, held_top, held_back, sems) = refs[4 : 4 + count], refs[4 + count :]
    rows = blocks[0].shape[0]
    step = pl.program_id(0)
    bring = [
        [
            pltpu.make_async_copy(source, place.at[j], sems.at[k, j])
            for j, source in enumerate(sources)
        ]
        for k, (sources, place) in enumerate(((blocks, held_hidden), (tops, held_top)))
    ]
    send = [
        pltpu.make_async_copy(
            held_back.at[j // 2, pl.ds(j % 2 * rows, rows)], backs[j], sems.at[2, j]
        )
        for j in range(count)
    ]

    @pl.when(step == 0)
    def _():
        for j in range(count):
            bring[0][j].start()
            bring[1][j].start()

    for j in range(0, count, 2):

        @pl.when(step == j // 2)
        def _():
            for k in range(2):
                bring[k][j].wait()
                bring[k][j + 1].wait()

    for half in range(2):
        at = slice(half * rows, (half + 1) * rows)
        hidden_ref[at, :] = held_hidden[2 * step + half]
        top_ref[at, :] = held_top[2 * step + half]
    units = down_ref.shape[0]
    both = dot(hidden_ref[...], gate_up_ref[...])
    grad_inner = dot(top_ref[...], down_ref[...], NT)
    gate, upper = both[:, :units], both[:, units:]
    sigma = jax.nn.sigmoid(gate)
    activ = gate * sigma
    inner_ref[...] = (activ * upper).astype(BF)
    grads_ref[:, units:] = (grad_inner * activ).astype(BF)
    grad_gate = grad_inner * upper * sigma * (1.0 + gate * (1.0 - sigma))
    grads_ref[:, :units] = grad_gate.astype(BF)
    held_back[step] = dot(grads_ref[...], gate_up_ref[...], NT).astype(BF)
    for j in range(0, count, 2):

        @pl.when(step == j // 2)
        def _():
            send[j].start()
            send[j + 1].start()

    @pl.when(step == count // 2 - 1)
    def _():
        for copy in send:
            copy.wait()


def ffn(blocks, tops, gate_up, down, first, carried=(), others=()):
    count = len(blocks)
    rows, width = blocks[0].shape
    units = down.shape[0]
    whole = lambda i: (0, 0)
    tile = lambda columns: pl.BlockSpec((2 * rows, columns), lambda i: (i + first, 0))
    once = lambda shape: pl.BlockSpec(shape, whole, pipeline_mode=pl.Buffered(1))
    stacked = lambda columns: jax.ShapeDtypeStruct((8 * rows, columns), BF)
    out = pl.pallas_call(
        functools.partial(ffn_kernel, count, len(carried) + len(others)),
        grid=(count // 2,),
        in_specs=[ANY] * (2 * count)
        + [once((width, 2 * units)), once((units, width))]
        + [ANY] * (len(carried) + len(others)),
        out_specs=[tile(units), tile(2 * units), tile(width), tile(width)] + [ANY] * count,
        out_shape=[stacked(units), stacked(2 * units), stacked(width), stacked(width)]
        + [jax.ShapeDtypeStruct((rows, width), BF)] * count,
        scratch_shapes=[
            pltpu.VMEM((count, rows, width), BF),
            pltpu.VMEM((count, rows, width), BF),
            pltpu.VMEM((count // 2, 2 * rows, width), BF),
            pltpu.SemaphoreType.DMA((3, count)),
        ],
        input_output_aliases={2 * count + 2 + i: i for i in range(len(carried))},
        cost_estimate=cost(4 * count + 2),
        compiler_params=pltpu.CompilerParams(vmem_limit_bytes=60 * 2**20),
    )(*blocks, *tops, gate_up, down, *carried, *others)
    return out[:4], out[4:]


def split_kernel(order, dims, left_ref, right_ref, *refs):
    rows = left_ref.shape[0] // 2
    both = dot(left_ref[...], right_ref[...], dims)
    outs = refs[-2 * len(order) :]
    both = both.astype(BF)
    for i in range(len(order)):

        @pl.when(pl.program_id(0) == i)
        def _():
            outs[2 * i][...] = both[:rows]
            outs[2 * i + 1][...] = both[rows:]


def split(left, right, dims, order, rows, others=()):
    width = right.shape[1 - dims[0][1][0]]

    def place(i):
        at = order[0]
        for n, r in enumerate(order):
            at = jnp.where(i == n, r, at)
        return at, 0

    used = (width, left.shape[1]) if dims == NT else (left.shape[1], width)
    out = pl.pallas_call(
        functools.partial(split_kernel, order, dims),
        grid=(len(order),),
        in_specs=[
            pl.BlockSpec((2 * rows, left.shape[1]), place),
            pl.BlockSpec(used, lambda i: (0, 0)),
        ]
        + [ANY] * len(others),
        out_specs=[pl.BlockSpec((rows, width), lambda i: (0, 0))] * (2 * len(order)),
        out_shape=[jax.ShapeDtypeStruct((rows, width), BF)] * (2 * len(order)),
        cost_estimate=cost(3 * len(order) + 2),
        compiler_params=pltpu.CompilerParams(vmem_limit_bytes=56 * 2**20),
    )(left, right, *others)
    return [tuple(out[2 * order.index(r) :][:2]) for r in range(len(order))]


def down_sums_kernel(inner_ref, top_ref, *refs):
    out_ref = refs[-1]
    count, size, _ = out_ref.shape
    found = dot(inner_ref[...], top_ref[...], TN).astype(BF)
    for z in range(count):
        out_ref[z] = found[z * size : (z + 1) * size]


def unit_sums_kernel(hidden_ref, grads_ref, *refs):
    out_ref = refs[-1]
    count, size, tile = out_ref.shape
    columns = grads_ref.shape[1] // tile
    depth = size // columns
    found = dot(hidden_ref[...], grads_ref[...], TN).astype(BF)
    for z in range(count):
        for b in range(columns):
            out_ref[z, b * depth : (b + 1) * depth, :] = found[
                z * depth : (z + 1) * depth, b * tile : (b + 1) * tile
            ]


def unit_sums(hidden, grads, layers, below, *others):
    tokens, width = hidden.shape
    tile = 256
    above = grads.shape[1] // tile * width // layers
    return pl.pallas_call(
        unit_sums_kernel,
        grid=(2,),
        in_specs=[
            pl.BlockSpec((tokens, width // 2), lambda i: (0, i)),
            pl.BlockSpec(grads.shape, lambda i: (0, 0)),
        ]
        + [ANY] * len(others),
        out_specs=pl.BlockSpec((layers // 2, above, tile), lambda i: (i, 0, 0)),
        out_shape=jax.ShapeDtypeStruct((layers, above + below, tile), BF),
        cost_estimate=cost(14),
        compiler_params=pltpu.CompilerParams(vmem_limit_bytes=56 * 2**20),
    )(hidden, grads, *others)


def down_sums(inner, tops, carried, *others):
    tokens, units = inner.shape
    width = tops.shape[1]
    layers, length, tile = carried.shape
    size = units // layers
    above = length - width // tile * size
    return pl.pallas_call(
        down_sums_kernel,
        grid=(width // tile,),
        in_specs=[
            pl.BlockSpec((tokens, units), lambda i: (0, 0)),
            pl.BlockSpec((tokens, tile), lambda i: (0, i)),
        ]
        + [ANY] * (1 + len(others)),
        out_specs=pl.BlockSpec((layers, size, tile), lambda i: (0, above // size + i, 0)),
        out_shape=jax.ShapeDtypeStruct(carried.shape, BF),
        input_output_aliases={2: 0},
        cost_estimate=cost(10),
        compiler_params=pltpu.CompilerParams(vmem_limit_bytes=56 * 2**20),
    )(inner, tops, carried, *others)


def part_sheet_kernel(sum_ref, *refs):
    heads_ref, out_ref = refs[-2:]
    owners, blocks, share, _ = heads_ref.shape
    depth = owners * share
    for b in range(blocks):
        block = sum_ref[b * depth : (b + 1) * depth].astype(F32)
        for p in range(owners):
            heads_ref[p, b] = block[p * share : (p + 1) * share].astype(BF)
    out_ref[...] = sum_ref[blocks * depth :]


def part_sheet(total_sum, share, *others):
    rows, tile = total_sum.shape
    blocks = 6 * HP // tile
    return pl.pallas_call(
        part_sheet_kernel,
        in_specs=[VMEM] + [ANY] * len(others),
        out_specs=[VMEM, VMEM],
        out_shape=[
            jax.ShapeDtypeStruct((8, blocks, share, tile), BF),
            jax.ShapeDtypeStruct((rows - blocks * 8 * share, tile), BF),
        ],
        cost_estimate=cost(2),
        compiler_params=pltpu.CompilerParams(vmem_limit_bytes=32 * 2**20),
    )(total_sum, *others)


def out_owner_kernel(piece_ref, out_ref):
    share, width = out_ref.shape
    size, tile = padded(share), piece_ref.shape[1]
    for i in range(width // tile):
        block = piece_ref[i * size : (i + 1) * size].astype(F32)
        out_ref[:, i * tile : (i + 1) * tile] = block[:share]


def out_owner(piece, share, width):
    return pl.pallas_call(
        out_owner_kernel,
        out_shape=jax.ShapeDtypeStruct((share, width), F32),
        cost_estimate=cost(2),
        compiler_params=pltpu.CompilerParams(vmem_limit_bytes=32 * 2**20),
    )(piece)


def out_sums_kernel(count, *refs):
    blocks, kept_ref, out_ref = refs[:count], refs[count], refs[-1]
    layers, size, _ = out_ref.shape
    found = [dot(kept_ref[i], ref[...], TN) for i, ref in enumerate(blocks)]
    found = functools.reduce(jnp.add, found).astype(BF)
    for z in range(layers):
        out_ref[z] = found[z * size : (z + 1) * size]


def head_sums_kernel(hidden_ref, grads_ref, rim_ref, lead_ref, *refs):
    out_ref = refs[-1]
    count, size, tile = out_ref.shape
    columns = grads_ref.shape[1] // tile
    depth = size // columns
    found = dot(hidden_ref[...], grads_ref[...], TN)
    more = dot(rim_ref[...], lead_ref[...], TN)
    skip = found.shape[1] - more.shape[1]
    found = jnp.concatenate([found[:, :skip], found[:, skip:] + more], axis=1).astype(BF)
    for z in range(count):
        for b in range(columns):
            out_ref[z, b * depth : (b + 1) * depth, :] = found[
                z * depth : (z + 1) * depth, b * tile : (b + 1) * tile
            ]


def head_sums(hidden, grad, rim, lead, layers, rows, *others):
    tokens, width = hidden.shape
    tile = 256
    above = grad.shape[1] // tile * width // layers
    whole = lambda i: (0, 0)
    return pl.pallas_call(
        head_sums_kernel,
        grid=(2,),
        in_specs=[
            pl.BlockSpec((tokens, width // 2), lambda i: (0, i)),
            pl.BlockSpec(grad.shape, whole),
            pl.BlockSpec((rim.shape[0], width // 2), lambda i: (0, i)),
            pl.BlockSpec(lead.shape, whole),
        ]
        + [ANY] * len(others),
        out_specs=pl.BlockSpec((layers // 2, above, tile), lambda i: (i, 0, 0)),
        out_shape=jax.ShapeDtypeStruct((layers, above + rows, tile), BF),
        cost_estimate=cost(11),
        compiler_params=pltpu.CompilerParams(vmem_limit_bytes=56 * 2**20),
    )(hidden, grad, rim, lead, *others)


def out_sums(blocks, kept, carried, *others):
    rows, width = blocks[0].shape
    count, _, depth = kept.shape
    layers, length, tile = carried.shape
    size = depth // layers
    above = length - width // tile * size
    return pl.pallas_call(
        functools.partial(out_sums_kernel, count),
        grid=(width // tile,),
        in_specs=[pl.BlockSpec((rows, tile), lambda i: (0, i))] * count
        + [pl.BlockSpec((count, rows, depth), lambda i: (0, 0, 0))]
        + [ANY] * (1 + len(others)),
        out_specs=pl.BlockSpec((layers, size, tile), lambda i: (0, above // size + i, 0)),
        out_shape=jax.ShapeDtypeStruct(carried.shape, BF),
        input_output_aliases={count + 1: 0},
        cost_estimate=cost(6),
        compiler_params=pltpu.CompilerParams(vmem_limit_bytes=32 * 2**20),
    )(*blocks, kept, carried, *others)


def leave_kernel(here_ref, x_ref, y_ref, own_ref, grad_ref, gain_ref, *refs):
    grad_hidden = here_ref[...] + x_ref[...].astype(F32) + y_ref[...].astype(F32)
    normed, factor = normalize(own_ref[...].astype(F32))
    refs[-1][...] = grad_ref[...] + norm_back(grad_hidden * gain_ref[...], normed, factor)


def leave(terms, own, grad_middle, gain, *others):
    return pl.pallas_call(
        leave_kernel,
        in_specs=[VMEM] * 6 + [ANY] * len(others),
        out_specs=VMEM,
        out_shape=jax.ShapeDtypeStruct(own.shape, F32),
        cost_estimate=cost(6),
        compiler_params=pltpu.CompilerParams(vmem_limit_bytes=32 * 2**20),
    )(*terms, own, grad_middle, gain, *others)


def mend_kernel(info_ref, tail_ref, back_ref, cur_ref, *refs):
    out_ref = refs[-1]
    out_ref[:, : 2 * HP] = cur_ref[:, : 2 * HP]
    out_ref[:, 2 * HP :] = (tail_ref[...] + back_ref[...].astype(F32)).astype(BF)


def mend(info, tail, back, grad_qkv, *others):
    rows, blocks = grad_qkv.shape[1], grad_qkv.shape[0] // 2
    side = pl.BlockSpec((None, WINDOW, 4 * HP), lambda s, info: (s, 0, 0))
    edge = pl.BlockSpec(
        (None, WINDOW, 6 * HP),
        lambda s, info: (2 * ((blocks - 1) ^ info[0]) + s, rows // WINDOW - 1, 0),
    )
    return pl.pallas_call(
        mend_kernel,
        grid_spec=pltpu.PrefetchScalarGridSpec(
            num_scalar_prefetch=1,
            grid=(2,),
            in_specs=[side, side, edge] + [ANY] * len(others),
            out_specs=edge,
        ),
        out_shape=jax.ShapeDtypeStruct(grad_qkv.shape, BF),
        cost_estimate=cost(2),
        input_output_aliases={3: 0},
    )(info, tail, back, grad_qkv, *others)


def first_key(at, rows):
    return min(at, rows + WINDOW - SPAN)


def shares_of(raws, cut, rows):
    row = lax.broadcasted_iota(jnp.int32, (SUB, SPAN), 0)
    col = lax.broadcasted_iota(jnp.int32, (SUB, SPAN), 1)
    seen = {}
    for at in range(0, rows, SUB):
        shift = at - first_key(at, rows)
        valid = (col > row + shift) & (col <= row + (shift + WINDOW))
        seen[at] = valid & (col >= cut) if at == 0 else valid
    scores = [jnp.where(seen[at], raw, MASKED) for at, raw in raws]
    peaks = [jnp.max(score, axis=-1, keepdims=True) for score in scores]
    powers = [jnp.exp((s - p) * (HD ** (-0.5))) for s, p in zip(scores, peaks)]
    totals = [jnp.sum(power, axis=-1, keepdims=True) for power in powers]
    return [power * (1.0 / total) for power, total in zip(powers, totals)]


def joined(prev_ref, halo_ref, cur_ref, at_first, lo):
    before = jnp.where(
        at_first, halo_ref[:, lo - 2 * HP : lo - HP], prev_ref[:, lo : lo + HP]
    )
    return jnp.concatenate([before, cur_ref[:, lo : lo + HP]], axis=0)


def tiles_of(rows):
    return [(h, at, first_key(at, rows)) for h in range(2) for at in range(0, rows, SUB)]


def attend_kernel(info_ref, cur_ref, prev_ref, halo_ref, *refs):
    flat_ref, kept_ref = refs[-2:]
    stream, block = pl.program_id(0), pl.program_id(1)
    at_first = block == 0
    cut = jnp.where(at_first & (info_ref[2 + stream] == 1), WINDOW, 0)
    rows = cur_ref.shape[0]
    tiles = tiles_of(rows)
    keys = [joined(prev_ref, halo_ref, cur_ref, at_first, (2 + h) * HP) for h in range(2)]
    values = [joined(prev_ref, halo_ref, cur_ref, at_first, (4 + h) * HP) for h in range(2)]
    raws = [
        (at, dot(cur_ref[at : at + SUB, h * HP : (h + 1) * HP], keys[h][lo : lo + SPAN], NT))
        for h, at, lo in tiles
    ]
    shares = [share.astype(BF) for share in shares_of(raws, cut, rows)]
    mixes = [dot(share, values[h][lo : lo + SPAN]) for share, (h, at, lo) in zip(shares, tiles)]
    for mixed, (h, at, lo) in zip(mixes, tiles):
        mixed = mixed.astype(BF)
        flat_ref[at : at + SUB, h * HP : (h + 1) * HP] = mixed
        kept_ref[at : at + SUB, h * HP : (h + 1) * HP] = mixed


def attend(qkv, halo, info, *others):
    rows, blocks = qkv.shape[1], qkv.shape[0] // 2
    mine = lambda s, b, info: (2 * (b ^ info[0]) + s, 0, 0)
    before = lambda s, b, info: (2 * (jnp.maximum(b - 1, 0) ^ info[0]) + s, rows // WINDOW - 1, 0)
    spec = pltpu.PrefetchScalarGridSpec(
        num_scalar_prefetch=1,
        grid=(2, blocks),
        in_specs=[
            pl.BlockSpec((None, rows, 6 * HP), mine),
            pl.BlockSpec((None, WINDOW, 6 * HP), before),
            pl.BlockSpec((None, WINDOW, 4 * HP), lambda s, b, info: (s, 0, 0)),
        ]
        + [ANY] * len(others),
        out_specs=[
            pl.BlockSpec((None, rows, 2 * HP), lambda s, b, info: (2 * b + (s ^ info[1]), 0, 0)),
            pl.BlockSpec((None, rows, 2 * HP), mine),
        ],
    )
    shape = jax.ShapeDtypeStruct((2 * blocks, rows, 2 * HP), BF)
    return pl.pallas_call(
        attend_kernel,
        grid_spec=spec,
        out_shape=[shape, pltpu.HBM(shape.shape, shape.dtype)],
        cost_estimate=cost(8),
        compiler_params=pltpu.CompilerParams(vmem_limit_bytes=32 * 2**20),
    )(info, qkv, qkv, halo, *others)


def attend_back_kernel(
    info_ref, cur_ref, prev_ref, halo_ref, top_ref, *refs
):
    out_ref, tail_ref, lead_ref, keep, acc = refs[-5:]
    stream, step = pl.program_id(0), pl.program_id(1)
    blocks = pl.num_programs(1)
    at_first = step == blocks - 1
    cut = jnp.where(at_first & (info_ref[2 + stream] == 1), WINDOW, 0)
    rows = cur_ref.shape[0]

    @pl.when(step == 0)
    def _():
        keep[...] = jnp.zeros_like(keep)

    acc[...] = jnp.zeros_like(acc)
    tiles = tiles_of(rows)
    keys = [joined(prev_ref, halo_ref, cur_ref, at_first, (2 + h) * HP) for h in range(2)]
    values = [joined(prev_ref, halo_ref, cur_ref, at_first, (4 + h) * HP) for h in range(2)]
    queries = [cur_ref[at : at + SUB, h * HP : (h + 1) * HP] for h, at, lo in tiles]
    tops = [top_ref[at : at + SUB, h * HP : (h + 1) * HP] for h, at, lo in tiles]
    raws = [
        (at, dot(query, keys[h][lo : lo + SPAN], NT)) for query, (h, at, lo) in zip(queries, tiles)
    ]
    grads = [dot(top, values[h][lo : lo + SPAN], NT) for top, (h, at, lo) in zip(tops, tiles)]
    shares = shares_of(raws, cut, rows)
    spent = [
        jnp.sum(share * grad, axis=-1, keepdims=True) for share, grad in zip(shares, grads)
    ]
    grads = [
        (share * ((grad - sum_) * (HD ** (-0.5)))).astype(BF)
        for share, grad, sum_ in zip(shares, grads, spent)
    ]
    shares = [share.astype(BF) for share in shares]
    for share, grad, query, top, (h, at, lo) in zip(shares, grads, queries, tops, tiles):
        left, right = h * HP, (h + 1) * HP
        out_ref[at : at + SUB, left:right] = dot(grad, keys[h][lo : lo + SPAN]).astype(BF)
        acc[lo : lo + SPAN, left:right] += dot(grad, query, TN)
        acc[lo : lo + SPAN, 2 * HP + left : 2 * HP + right] += dot(share, top, TN)
    last = acc[rows : rows + WINDOW, :] + keep[...]
    out_ref[: rows - WINDOW, 2 * HP :] = acc[WINDOW:rows, :].astype(BF)
    out_ref[rows - WINDOW :, 2 * HP :] = last.astype(BF)
    keep[...] = acc[:WINDOW, :]

    @pl.when(step == 0)
    def _():
        tail_ref[...] = last

    @pl.when(at_first)
    def _():
        lead_ref[...] = acc[:WINDOW, :].astype(BF)


def attend_back(qkv, halo, top, info, *others):
    rows, blocks = qkv.shape[1], qkv.shape[0] // 2
    at = lambda t: blocks - 1 - t
    mine = lambda s, t, info: (2 * (at(t) ^ info[0]) + s, 0, 0)
    before = lambda s, t, info: (
        2 * (jnp.maximum(at(t) - 1, 0) ^ info[0]) + s,
        rows // WINDOW - 1,
        0,
    )
    side = lambda s, t, info: (s, 0, 0)
    spec = pltpu.PrefetchScalarGridSpec(
        num_scalar_prefetch=1,
        grid=(2, blocks),
        in_specs=[
            pl.BlockSpec((None, rows, 6 * HP), mine),
            pl.BlockSpec((None, WINDOW, 6 * HP), before),
            pl.BlockSpec((None, WINDOW, 4 * HP), side),
            pl.BlockSpec(
                (None, rows, 2 * HP), lambda s, t, info: (2 * at(t) + (s ^ info[1]), 0, 0)
            ),
        ]
        + [ANY] * len(others),
        out_specs=[
            pl.BlockSpec((None, rows, 6 * HP), mine),
            pl.BlockSpec((None, WINDOW, 4 * HP), side),
            pl.BlockSpec((None, WINDOW, 4 * HP), side),
        ],
        scratch_shapes=[
            pltpu.VMEM((WINDOW, 4 * HP), F32),
            pltpu.VMEM((rows + WINDOW, 4 * HP), F32),
        ],
    )
    return pl.pallas_call(
        attend_back_kernel,
        grid_spec=spec,
        out_shape=[
            jax.ShapeDtypeStruct(qkv.shape, BF),
            jax.ShapeDtypeStruct(halo.shape, F32),
            jax.ShapeDtypeStruct(halo.shape, BF),
        ],
        cost_estimate=cost(17),
        compiler_params=pltpu.CompilerParams(vmem_limit_bytes=32 * 2**20),
    )(info, qkv, qkv, halo, top, *others)


def body(
    inputs,
    starts,
    attn_gain,
    query_weight,
    key_weight,
    value_weight,
    out_weight,
    ffn_gain,
    gate_weight,
    up_weight,
    down_weight,
    cotangent,
):
    rows, width = inputs.shape[1:]
    layers = lax.axis_size("z")
    devices = 8 * layers
    share = query_weight.shape[0]
    part = down_weight.shape[0]
    units = -(-part // 16) * 16 * layers
    me_z = lax.axis_index("z")
    me_block = 2 * lax.axis_index("y") + lax.axis_index("x")
    me_core = lax.axis_index("c")

    own = inputs[0]
    top = cotangent[0]
    own_gains = jnp.stack([attn_gain, ffn_gain]).astype(F32)
    heads = head_sheet(query_weight, key_weight, value_weight, own_gains, starts)
    down = jnp.pad(down_weight, ((0, units // layers - part), (0, 0)))
    down = lax.all_gather(down, "z", axis=0, tiled=True)
    heads = lax.all_to_all(heads, PLANE, 0, 0, tiled=True)
    opened = heads[:2, 0, extra_column(2, share)].astype(jnp.int32)
    opened = jnp.where(me_core == 0, opened, opened[::-1])
    info = jnp.concatenate([jnp.stack([me_block, me_core]), opened, me_z[None]]).astype(jnp.int32)
    ready = held(own, heads)
    from_x, from_y = neighbours(ready)
    streams = both_cores([own, from_x, from_y, across(ready)])
    top_ready = held(top, from_x, from_y)
    attn_weight = attn_sheet(heads, out_weight, down, from_x, from_y)
    attn_weight = lax.all_gather(attn_weight, "z", axis=0, tiled=True)
    stream = jnp.concatenate(streams, axis=0)
    factor = normalize(stream.astype(F32))[1]
    sheet = unit_sheet(gate_weight, up_weight, layers, part, units, heads)
    sheet = lax.all_to_all(sheet, PLANE, 0, 0, tiled=True).reshape(8 * share, 2 * units)
    gate_up = lax.all_gather(sheet, "z", axis=0, tiled=True)
    tops = both_cores([top, *neighbours(top_ready), across(top_ready)])

    hidden1, qkv, gains = enter(stream, factor, attn_weight, rows, share, *tops[2::2])
    gain_attn, gain_ffn = gains[0:1], gains[1:2]
    qkv = qkv.reshape(8, rows, 6 * HP)
    last = 2 * (3 ^ me_block)
    rim = lax.dynamic_slice(qkv, (last, rows - WINDOW, 2 * HP), (2, WINDOW, 4 * HP))
    halo = lax.ppermute(rim, "z", [(i, i + 1) for i in range(layers - 1)])
    own_out = attn_weight[:, 6 * HP :]
    from_x, from_y = neighbours(own_out)
    far = diagonal(from_x, from_y, halo)
    flat, kept = attend(qkv, halo, info)
    full_out = both_cores([own_out, from_x, from_y, join(*far, flat)])
    full_out = out_sheet(full_out, info, layers)
    rim = lax.dynamic_slice(
        hidden1.reshape(8, rows, width), (last, rows - WINDOW, 0), (2, WINDOW, width)
    )
    rim = lax.ppermute(rim, "z", [(i, i + 1) for i in range(layers - 1)])
    mixed = lax.all_to_all(flat, PLANE, 0, 0, tiled=True)
    middle, hidden2 = project(mixed, full_out, own, gain_ffn)

    from_x, from_y = neighbours(hidden2)
    far = diagonal(from_x, from_y)
    carried, near = ffn(
        both_cores([hidden2, from_x, from_y]), tops[:6], gate_up, down, 0
    )
    far = join(*far, carried[0])
    (inner, grads, hidden2, tops), far = ffn(
        both_cores([far]), tops[6:], gate_up, down, 3, carried
    )
    terms, sent, far = plane_sum([near[:2], near[2:4], near[4:], far])
    ffn_part = unit_sums(hidden2, grads, layers, width // 256 * units // layers, far, rim)
    ffn_part = down_sums(inner, tops, ffn_part, *sent)
    out_parts = split(inner, down, NN, (3, 2, 1, 0), rows, [ffn_part])
    ffn_sum = lax.psum_scatter(ffn_part, "z", scatter_dimension=0, tiled=True)[0]

    grad_mixed, grad_middle, grad_branch = unproject(
        terms, middle, top, gain_ffn, full_out, out_parts[3][0]
    )

    grad_mixed = lax.all_to_all(grad_mixed, PLANE, 0, 0, tiled=True)
    from_x, from_y = neighbours(grad_branch)
    grad_qkv, tail, lead = attend_back(qkv, halo, grad_mixed, info)
    back = lax.ppermute(lead, "z", [(i + 1, i) for i in range(layers - 1)])
    out_terms, sent, _ = plane_sum(out_parts, tail)
    attn_part = head_sums(
        hidden1,
        grad_qkv.reshape(8 * rows, 6 * HP),
        rim.reshape(2 * WINDOW, width),
        lead.reshape(2 * WINDOW, 4 * HP),
        layers,
        8 * share,
    )
    branches = join(*diagonal(from_x, from_y, attn_part))
    branches = both_cores([grad_branch, from_x, from_y, branches])
    grad_qkv = mend(info, tail, back, grad_qkv, attn_part).reshape(8 * rows, 6 * HP)
    attn_part = out_sums(branches, kept, attn_part, grad_qkv, *sent)
    attn_sum = lax.psum_scatter(attn_part, "z", scatter_dimension=0, tiled=True)[0]
    layer_out = (middle + total(out_terms)).astype(BF)
    above = 2 * units // 256 * 8 * share
    gate_up_sum = ffn_sum[:above].reshape(-1, 8, share, 256).swapaxes(0, 1)
    gate_up_sum = lax.all_to_all(gate_up_sum, PLANE, 0, 0, tiled=True)
    gate_grad, up_grad, ffn_gain_grad = unit_owner(
        gate_up_sum, (gate_weight, up_weight), own_gains[1:2], layers, part
    )
    down_grad = ffn_sum[above:].reshape(width // 256, -1, 256).swapaxes(0, 1)
    down_grad = down_grad[:part].reshape(part, width).astype(F32)
    parts = split(grad_qkv, attn_weight, NT, (3, 2, 1, 0), rows, [attn_part])
    terms, _, _ = plane_sum(parts, *out_terms[1:])
    input_grad = leave(terms, own, grad_middle, gain_attn, gate_grad)

    qkv_sum, out_sum = part_sheet(attn_sum, share, input_grad, layer_out)
    qkv_sum = lax.all_to_all(qkv_sum, PLANE, 0, 0, tiled=True)
    query_grad, key_grad, value_grad, attn_gain_grad = head_owner(
        qkv_sum, (query_weight, key_weight, value_weight), own_gains[0:1]
    )
    route = [(8 * z + p, layers * p + z) for z in range(layers) for p in range(8)]
    output_grad = out_owner(lax.ppermute(out_sum, ALL, route), share, width)
    return (
        layer_out[None],
        input_grad[None],
        attn_gain_grad[0],
        query_grad,
        key_grad,
        value_grad,
        output_grad,
        ffn_gain_grad[0],
        gate_grad,
        up_grad,
        down_grad,
    )


def solution(mesh):
    blocks = mesh.shape["seq"]
    fine = Mesh(mesh.devices.reshape(blocks // 4, 2, 2, 2), ALL)
    tokens = P("c", ("z", "y", "x"), None)
    weight = P(ALL, None)
    gain = P(ALL)
    in_specs = (
        tokens,
        P("c", ("z", "y", "x")),
        gain,
        weight,
        weight,
        weight,
        weight,
        gain,
        weight,
        weight,
        weight,
        tokens,
    )
    out_specs = (
        tokens,
        tokens,
        gain,
        weight,
        weight,
        weight,
        weight,
        gain,
        weight,
        weight,
        weight,
    )
    return jax.shard_map(body, mesh=fine, in_specs=in_specs, out_specs=out_specs, check_vma=False)
```

```python
import functools

import jax
import jax.numpy as jnp
from jax import lax
from jax.experimental import pallas as pl
from jax.experimental.pallas import tpu as pltpu
from jax.sharding import Mesh, PartitionSpec as P

H = 16
HD = 112
HP = 128
WINDOW = 64
EPS = 1e-06
MASKED = -1e30
SUB = 128
SPAN = 256

BF = jnp.bfloat16
F32 = jnp.float32
ALL = ("z", "y", "x", "c")
PLANE = ("y", "x", "c")
SWAP = [(0, 1), (1, 0)]
NT = (((1,), (1,)), ((), ()))
TN = (((0,), (0,)), ((), ()))
NN = (((1,), (0,)), ((), ()))


def cost(us):
    return pl.CostEstimate(flops=int(us * 1.1e9), bytes_accessed=int(us * 3.5e6), transcendentals=0)


def swap(block, axis):
    return lax.ppermute(block, axis, SWAP)


def normalize(values):
    factor = lax.rsqrt(jnp.mean(values * values, axis=-1, keepdims=True) + EPS)
    return (values * factor, factor)


def norm_back(grad_normed, normed_rows, factor):
    return factor * (
        grad_normed - normed_rows * jnp.mean(grad_normed * normed_rows, axis=-1, keepdims=True)
    )


def dot(left, right, dims=NN):
    return lax.dot_general(left, right, dims, preferred_element_type=F32)


ANY = pl.BlockSpec(memory_space=pl.ANY)


VMEM = pl.BlockSpec(memory_space=pltpu.VMEM)
SMEM = pl.BlockSpec(memory_space=pltpu.SMEM)


def held_kernel(source_ref, *refs):
    refs[-1][...] = source_ref[...]


def held(value, *others):
    return pl.pallas_call(
        held_kernel,
        in_specs=[VMEM] + [ANY] * len(others),
        out_specs=VMEM,
        out_shape=jax.ShapeDtypeStruct(value.shape, value.dtype),
        cost_estimate=cost(2),
        compiler_params=pltpu.CompilerParams(vmem_limit_bytes=32 * 2**20),
    )(value, *others)


def stack_kernel(count, *refs):
    for k in range(count):
        refs[-1][k] = refs[k][...]


def stack(pieces, *others):
    count = len(pieces)
    return pl.pallas_call(
        functools.partial(stack_kernel, count),
        in_specs=[VMEM] * count + [ANY] * len(others),
        out_specs=VMEM,
        out_shape=jax.ShapeDtypeStruct((count, *pieces[0].shape), pieces[0].dtype),
        cost_estimate=cost(2),
        compiler_params=pltpu.CompilerParams(vmem_limit_bytes=32 * 2**20),
    )(*pieces, *others)


def neighbours(own):
    return swap(own, "x"), swap(own, "y")


def across(own):
    return lax.ppermute(own, ("y", "x"), [(i, i ^ 3) for i in range(4)])


def join_kernel(first_ref, second_ref, *refs):
    half = first_ref.shape[0]
    refs[-1][:half] = first_ref[...]
    refs[-1][half:] = second_ref[...]


def join(first, second, *others):
    shape = (2 * first.shape[0], *first.shape[1:])
    return pl.pallas_call(
        join_kernel,
        in_specs=[VMEM] * 2 + [ANY] * len(others),
        out_specs=VMEM,
        out_shape=jax.ShapeDtypeStruct(shape, first.dtype),
        cost_estimate=cost(2),
        compiler_params=pltpu.CompilerParams(vmem_limit_bytes=32 * 2**20),
    )(first, second, *others)


def halves_kernel(x_ref, y_ref, *refs):
    half = x_ref.shape[0] // 2
    refs[-2][...] = y_ref[:half]
    refs[-1][...] = x_ref[half:]


def halves(from_x, from_y, *others):
    shape = jax.ShapeDtypeStruct((from_x.shape[0] // 2, *from_x.shape[1:]), from_x.dtype)
    return pl.pallas_call(
        halves_kernel,
        in_specs=[VMEM] * 2 + [ANY] * len(others),
        out_specs=[VMEM] * 2,
        out_shape=[shape, shape],
        cost_estimate=cost(2),
        compiler_params=pltpu.CompilerParams(vmem_limit_bytes=32 * 2**20),
    )(from_x, from_y, *others)


def diagonal(from_x, from_y, *others):
    first, second = halves(from_x, from_y, *others)
    return swap(first, "x"), swap(second, "y")


def both_cores(blocks):
    return [block for mine in blocks for block in (mine, swap(mine, "c"))]


def add_kernel(mine_ref, other_ref, *refs):
    refs[-1][...] = (mine_ref[...].astype(F32) + other_ref[...].astype(F32)).astype(BF)


def add(mine, other, *others):
    return pl.pallas_call(
        add_kernel,
        in_specs=[VMEM] * 2 + [ANY] * len(others),
        out_specs=VMEM,
        out_shape=jax.ShapeDtypeStruct(mine.shape, BF),
        cost_estimate=cost(2),
        compiler_params=pltpu.CompilerParams(vmem_limit_bytes=32 * 2**20),
    )(mine, other, *others)


def plane_sum(parts, *others):
    half = parts[0][0].shape[0] // 2
    other = {r: swap(parts[r][1], "c") for r in (3, 2, 1, 0)}
    far = add(parts[3][0], other[3], *others)
    first = swap(far[:half], "x")
    second = swap(far[half:], "y")
    along_y, along_x, here = (parts[r][0].astype(F32) + other[r].astype(F32) for r in (2, 1, 0))
    along_y = jnp.concatenate([along_y[:half] + first.astype(F32), along_y[half:]], axis=0).astype(BF)
    along_x = jnp.concatenate([along_x[:half], along_x[half:] + second.astype(F32)], axis=0).astype(BF)
    return (here, swap(along_x, "x"), swap(along_y, "y")), (along_x, along_y), far


def total(terms):
    here, got_x, got_y = terms
    return here + got_x.astype(F32) + got_y.astype(F32)


def direct_gather(block, count):
    return [block] + [
        lax.ppermute(block, "z", [(i, (i + k) % count) for i in range(count)])
        for k in range(1, count)
    ]


def padded(share):
    return share * HP // HD


def head_sheet_kernel(starts_ref, query_ref, key_ref, value_ref, gains_ref, out_ref):
    rows = query_ref.shape[0]
    spare = padded(rows) - rows
    same = lax.broadcasted_iota(jnp.int32, (rows, rows), 0) == lax.broadcasted_iota(
        jnp.int32, (rows, rows), 1
    )
    extra = [
        jnp.sum(
            jnp.where(same, jnp.broadcast_to(gains_ref[i : i + 1, :], (rows, rows)), 0.0),
            axis=1,
            keepdims=True,
        )
        for i in range(2)
    ]
    extra = extra + [jnp.full((rows, 1), starts_ref[0, 0], jnp.int32).astype(F32)]
    extra = jnp.concatenate(extra + [jnp.zeros((rows, HP - HD - 3), F32)], axis=1).astype(BF)
    for i, ref in enumerate((query_ref, key_ref, value_ref)):
        for h in range(H):
            pieces = []
            for a in range(HD // rows):
                pieces.append(ref[:, h * HD + a * rows : h * HD + (a + 1) * rows])
                if i == 0 and h % 2 == 0:
                    pieces.append(extra[:, a * spare : (a + 1) * spare])
                else:
                    pieces.append(jnp.zeros((rows, spare), BF))
            lo = (2 * i + h % 2) * HP
            out_ref[h // 2, :, lo : lo + HP] = jnp.concatenate(pieces, axis=1)


def head_sheet(query, key, value, gains, starts):
    whole = pl.BlockSpec(memory_space=pltpu.VMEM)
    return pl.pallas_call(
        head_sheet_kernel,
        in_specs=[pl.BlockSpec(memory_space=pltpu.SMEM)] + [whole] * 4,
        out_specs=whole,
        out_shape=jax.ShapeDtypeStruct((8, query.shape[0], 6 * HP), BF),
        cost_estimate=cost(2),
        compiler_params=pltpu.CompilerParams(vmem_limit_bytes=32 * 2**20),
    )(starts, query, key, value, gains)


def extra_column(j, share):
    spare = padded(share) - share
    return j // spare * padded(share) + share + j % spare


def attn_sheet_kernel(heads_ref, out_weight_ref, *refs):
    sheet_ref = refs[-1]
    count, rows, columns = heads_ref.shape
    size, tile = padded(rows), sheet_ref.shape[1] - columns
    heads = [heads_ref[p].astype(F32) for p in range(count)]
    sheet_ref[:, :columns] = jnp.concatenate(heads, axis=0).astype(BF)
    blank = jnp.zeros((size - rows, tile), F32)
    blocks = []
    for i in range(out_weight_ref.shape[1] // tile):
        blocks += [out_weight_ref[:, i * tile : (i + 1) * tile].astype(F32), blank]
    sheet_ref[:, columns:] = jnp.concatenate(blocks, axis=0).astype(BF)


def attn_sheet(heads, out_weight, *others):
    count, rows, columns = heads.shape
    return pl.pallas_call(
        attn_sheet_kernel,
        in_specs=[VMEM] * 2 + [ANY] * len(others),
        out_shape=jax.ShapeDtypeStruct((count * rows, columns + 256), BF),
        cost_estimate=cost(2),
        compiler_params=pltpu.CompilerParams(vmem_limit_bytes=32 * 2**20),
    )(heads, out_weight, *others)


def out_sheet_kernel(info_ref, *refs):
    *blocks, out_ref = refs
    layers, size, width = out_ref.shape
    tile = blocks[0].shape[1]
    count = width // tile
    for r, block in enumerate(blocks):

        @pl.when(pl.program_id(0) == r)
        def _():
            for z in range(layers):
                for i in range(count):
                    at = (z * count + i) * size
                    out_ref[z, :, i * tile : (i + 1) * tile] = block[at : at + size, :]


def out_sheet(blocks, info, layers):
    depth, tile = blocks[0].shape
    size, width = 2 * HP // layers, depth * tile * 8 // (16 * HP)
    place = lambda r, info: (0, 2 * ((r // 2) ^ info[0]) + ((r % 2) ^ info[1]), 0, 0)
    out = pl.pallas_call(
        out_sheet_kernel,
        grid_spec=pltpu.PrefetchScalarGridSpec(
            num_scalar_prefetch=1,
            grid=(8,),
            in_specs=[pl.BlockSpec((depth, tile), lambda r, info: (0, 0))] * 8,
            out_specs=pl.BlockSpec((layers, None, size, width), place),
        ),
        out_shape=pltpu.HBM((layers, 8, size, width), BF),
        cost_estimate=cost(6),
        compiler_params=pltpu.CompilerParams(vmem_limit_bytes=32 * 2**20),
    )(info, *blocks)
    return out.reshape(-1, width)


def unit_sheet_kernel(layers, part, gate_ref, up_ref, *refs):
    out_ref = refs[-1]
    units = out_ref.shape[2] // 2
    blank = jnp.zeros((gate_ref.shape[0], units // layers - part), BF)
    for w, ref in enumerate((gate_ref, up_ref)):
        for p in range(8):
            pieces = []
            for z in range(layers):
                pieces.append(ref[:, (8 * z + p) * part : (8 * z + p + 1) * part])
                pieces.append(blank)
            out_ref[p, :, w * units : (w + 1) * units] = jnp.concatenate(pieces, axis=1)


def unit_sheet(gate, up, layers, part, units, *others):
    return pl.pallas_call(
        functools.partial(unit_sheet_kernel, layers, part),
        in_specs=[pl.BlockSpec(memory_space=pltpu.VMEM)] * 2 + [ANY] * len(others),
        out_shape=jax.ShapeDtypeStruct((8, gate.shape[0], 2 * units), BF),
        cost_estimate=cost(2),
        compiler_params=pltpu.CompilerParams(vmem_limit_bytes=32 * 2**20),
    )(gate, up, *others)


def gain_row(products, gain):
    rows = products.shape[0]
    same = lax.broadcasted_iota(jnp.int32, (rows, rows), 0) == lax.broadcasted_iota(
        jnp.int32, (rows, rows), 1
    )
    row = jnp.sum(jnp.where(same, jnp.broadcast_to(products, (rows, rows)), 0.0), axis=0, keepdims=True)
    return row / gain


def head_owner_kernel(sheet_ref, *refs):
    weights, gain_ref, (*grads, gain_grad_ref) = refs[:3], refs[3], refs[4:]
    rows = weights[0].shape[0]
    products = jnp.zeros((rows, 1), F32)
    for i, ref in enumerate(grads):
        pieces = []
        for h in range(H):
            lo = (h % 2) * HP
            pieces += [
                sheet_ref[h // 2, i, :, lo + a * padded(rows) : lo + a * padded(rows) + rows]
                for a in range(HD // rows)
            ]
        grad = jnp.concatenate(pieces, axis=1).astype(F32)
        ref[...] = grad
        products += jnp.sum(grad * weights[i][...].astype(F32), axis=1, keepdims=True)
    gain_grad_ref[...] = gain_row(products, gain_ref[...])


def head_owner(sheet, weights, gain):
    share, width = weights[0].shape
    shape = jax.ShapeDtypeStruct((share, width), F32)
    return pl.pallas_call(
        head_owner_kernel,
        out_shape=[shape, shape, shape, jax.ShapeDtypeStruct((1, share), F32)],
        cost_estimate=cost(3),
        compiler_params=pltpu.CompilerParams(vmem_limit_bytes=32 * 2**20),
    )(sheet, *weights, gain)


def unit_owner_kernel(layers, part, sheet_ref, *refs):
    weights, gain_ref, (*grads, gain_grad_ref) = refs[:2], refs[2], refs[3:]
    _, columns, rows, tile = sheet_ref.shape
    units = columns * tile // 2
    owned = [
        jnp.concatenate([sheet_ref[p, b] for b in range(columns)], axis=1).astype(F32)
        for p in range(8)
    ]
    products = jnp.zeros((rows, 1), F32)
    for w, ref in enumerate(grads):
        for z in range(layers):
            lo = w * units + z * (units // layers)
            at = slice(8 * z * part, 8 * (z + 1) * part)
            grad = jnp.concatenate([value[:, lo : lo + part] for value in owned], axis=1)
            ref[:, at] = grad
            products += jnp.sum(grad * weights[w][:, at].astype(F32), axis=1, keepdims=True)
    gain_grad_ref[...] = gain_row(products, gain_ref[...])


def unit_owner(sheet, weights, gain, layers, part):
    share, columns = weights[0].shape
    shape = jax.ShapeDtypeStruct((share, columns), F32)
    return pl.pallas_call(
        functools.partial(unit_owner_kernel, layers, part),
        out_shape=[shape, shape, jax.ShapeDtypeStruct((1, share), F32)],
        cost_estimate=cost(3),
        compiler_params=pltpu.CompilerParams(vmem_limit_bytes=32 * 2**20),
    )(sheet, *weights, gain)


def enter_kernel(share, stream_ref, factor_ref, weight_ref, *refs):
    hidden_ref, qkv_ref, gains_ref = refs[-3:]

    @pl.when(pl.program_id(0) == 0)
    def _():
        row = lax.broadcasted_iota(jnp.int32, (8, HP), 0)
        col = lax.broadcasted_iota(jnp.int32, (8, HP), 1)
        pick = (row == 0) & (col == extra_column(0, share))
        pick = pick | ((row == 1) & (col == extra_column(1, share)))
        pick = pick.astype(F32).astype(BF)
        gains_ref[...] = dot(pick, weight_ref[:, :HP], NT)

    normed = stream_ref[...].astype(F32) * factor_ref[...]
    hidden = (normed * gains_ref[0:1, :]).astype(BF)
    hidden_ref[...] = hidden
    qkv_ref[...] = dot(hidden, weight_ref[...]).astype(BF)


def enter(stream, factor, weight, rows, share, *others):
    tokens, width = stream.shape
    whole = lambda i: (0, 0)
    tile = lambda columns: pl.BlockSpec((rows, columns), lambda i: (i, 0))
    return pl.pallas_call(
        functools.partial(enter_kernel, share),
        grid=(tokens // rows,),
        in_specs=[tile(width), tile(1), pl.BlockSpec((width, 6 * HP), whole)] + [ANY] * len(others),
        out_specs=[tile(width), tile(6 * HP), pl.BlockSpec((8, width), whole)],
        out_shape=[
            pltpu.HBM((tokens, width), BF),
            pltpu.HBM((tokens, 6 * HP), BF),
            jax.ShapeDtypeStruct((8, width), F32),
        ],
        cost_estimate=cost(12),
        compiler_params=pltpu.CompilerParams(vmem_limit_bytes=32 * 2**20),
    )(stream, factor, weight, *others)


def project_kernel(mixed_ref, weight_ref, input_ref, gain_ref, *refs):
    middle_ref, hidden_ref = refs[-2:]
    step = pl.program_id(0)

    @pl.when(step == 0)
    def _():
        middle_ref[...] = input_ref[...].astype(F32)

    middle_ref[...] += jnp.dot(mixed_ref[...], weight_ref[...], preferred_element_type=F32)

    @pl.when(step == pl.num_programs(0) - 1)
    def _():
        normed, _ = normalize(middle_ref[...])
        hidden_ref[...] = (normed * gain_ref[...]).astype(BF)


def project(mixed, weight, own, gain, *others):
    count, rows, depth = mixed.shape
    width = own.shape[1]
    whole = lambda p: (0, 0)
    return pl.pallas_call(
        project_kernel,
        grid=(count,),
        in_specs=[
            pl.BlockSpec((None, rows, depth), lambda p: (p, 0, 0)),
            pl.BlockSpec((depth, width), lambda p: (p, 0)),
            pl.BlockSpec((rows, width), whole),
            pl.BlockSpec((1, width), whole),
        ]
        + [ANY] * len(others),
        out_specs=[pl.BlockSpec((rows, width), whole), pl.BlockSpec((rows, width), whole)],
        out_shape=[
            jax.ShapeDtypeStruct((rows, width), F32),
            jax.ShapeDtypeStruct((rows, width), BF),
        ],
        cost_estimate=cost(7),
        compiler_params=pltpu.CompilerParams(vmem_limit_bytes=32 * 2**20),
    )(mixed, weight, own, gain, *others)


def unproject_kernel(
    here_ref, x_ref, y_ref, middle_ref, top_ref, gain_ref, weight_ref, *refs
):
    out_ref, grad_ref, branch_ref = refs[-3:]

    @pl.when(pl.program_id(0) == 0)
    def _():
        grad_hidden = here_ref[...] + x_ref[...].astype(F32) + y_ref[...].astype(F32)
        normed, factor = normalize(middle_ref[...])
        grad = top_ref[...].astype(F32) + norm_back(grad_hidden * gain_ref[...], normed, factor)
        grad_ref[...] = grad
        branch_ref[...] = grad.astype(BF)

    out_ref[...] = lax.dot_general(
        branch_ref[...], weight_ref[...], NT, preferred_element_type=F32
    ).astype(BF)


def unproject(terms, middle, top, gain, weight, *others):
    rows, width = middle.shape
    depth = weight.shape[0] // 8
    full = pl.BlockSpec((rows, width), lambda p: (0, 0))
    line = pl.BlockSpec((1, width), lambda p: (0, 0))
    return pl.pallas_call(
        unproject_kernel,
        grid=(8,),
        in_specs=[full] * 5
        + [line, pl.BlockSpec((depth, width), lambda p: (p, 0))]
        + [ANY] * len(others),
        out_specs=[pl.BlockSpec((None, rows, depth), lambda p: (p, 0, 0)), full, full],
        out_shape=[
            jax.ShapeDtypeStruct((8, rows, depth), BF),
            jax.ShapeDtypeStruct((rows, width), F32),
            jax.ShapeDtypeStruct((rows, width), BF),
        ],
        cost_estimate=cost(12),
        compiler_params=pltpu.CompilerParams(vmem_limit_bytes=48 * 2**20),
    )(*terms, middle, top, gain, weight, *others)


def ffn_kernel(count, kept, *refs):
    blocks, tops, refs = refs[:count], refs[count : 2 * count], refs[2 * count :]
    gate_up_ref, down_ref, refs = refs[0], refs[1], refs[2 + kept :]
    inner_ref, grads_ref, hidden_ref, top_ref = refs[:4]
    backs, (held_hidden, held_top, held_back, sems) = refs[4 : 4 + count], refs[4 + count :]
    rows = blocks[0].shape[0]
    step = pl.program_id(0)
    bring = [
        [
            pltpu.make_async_copy(source, place.at[j], sems.at[k, j])
            for j, source in enumerate(sources)
        ]
        for k, (sources, place) in enumerate(((blocks, held_hidden), (tops, held_top)))
    ]
    send = [
        pltpu.make_async_copy(
            held_back.at[j // 2, pl.ds(j % 2 * rows, rows)], backs[j], sems.at[2, j]
        )
        for j in range(count)
    ]

    @pl.when(step == 0)
    def _():
        for j in range(count):
            bring[0][j].start()
            bring[1][j].start()

    for j in range(0, count, 2):

        @pl.when(step == j // 2)
        def _():
            for k in range(2):
                bring[k][j].wait()
                bring[k][j + 1].wait()

    for half in range(2):
        at = slice(half * rows, (half + 1) * rows)
        hidden_ref[at, :] = held_hidden[2 * step + half]
        top_ref[at, :] = held_top[2 * step + half]
    units = down_ref.shape[0]
    both = dot(hidden_ref[...], gate_up_ref[...])
    grad_inner = dot(top_ref[...], down_ref[...], NT)
    gate, upper = both[:, :units], both[:, units:]
    sigma = jax.nn.sigmoid(gate)
    activ = gate * sigma
    inner_ref[...] = (activ * upper).astype(BF)
    grads_ref[:, units:] = (grad_inner * activ).astype(BF)
    grad_gate = grad_inner * upper * sigma * (1.0 + gate * (1.0 - sigma))
    grads_ref[:, :units] = grad_gate.astype(BF)
    held_back[step] = dot(grads_ref[...], gate_up_ref[...], NT).astype(BF)
    for j in range(0, count, 2):

        @pl.when(step == j // 2)
        def _():
            send[j].start()
            send[j + 1].start()

    @pl.when(step == count // 2 - 1)
    def _():
        for copy in send:
            copy.wait()


def ffn(blocks, tops, gate_up, down, first, carried=(), others=()):
    count = len(blocks)
    rows, width = blocks[0].shape
    units = down.shape[0]
    whole = lambda i: (0, 0)
    tile = lambda columns: pl.BlockSpec((2 * rows, columns), lambda i: (i + first, 0))
    once = lambda shape: pl.BlockSpec(shape, whole, pipeline_mode=pl.Buffered(1))
    stacked = lambda columns: jax.ShapeDtypeStruct((8 * rows, columns), BF)
    out = pl.pallas_call(
        functools.partial(ffn_kernel, count, len(carried) + len(others)),
        grid=(count // 2,),
        in_specs=[ANY] * (2 * count)
        + [once((width, 2 * units)), once((units, width))]
        + [ANY] * (len(carried) + len(others)),
        out_specs=[tile(units), tile(2 * units), tile(width), tile(width)] + [ANY] * count,
        out_shape=[stacked(units), stacked(2 * units), stacked(width), stacked(width)]
        + [jax.ShapeDtypeStruct((rows, width), BF)] * count,
        scratch_shapes=[
            pltpu.VMEM((count, rows, width), BF),
            pltpu.VMEM((count, rows, width), BF),
            pltpu.VMEM((count // 2, 2 * rows, width), BF),
            pltpu.SemaphoreType.DMA((3, count)),
        ],
        input_output_aliases={2 * count + 2 + i: i for i in range(len(carried))},
        cost_estimate=cost(4 * count + 2),
        compiler_params=pltpu.CompilerParams(vmem_limit_bytes=60 * 2**20),
    )(*blocks, *tops, gate_up, down, *carried, *others)
    return out[:4], out[4:]


def split_kernel(order, dims, left_ref, right_ref, *refs):
    rows = left_ref.shape[0] // 2
    both = dot(left_ref[...], right_ref[...], dims)
    outs = refs[-2 * len(order) :]
    both = both.astype(BF)
    for i in range(len(order)):

        @pl.when(pl.program_id(0) == i)
        def _():
            outs[2 * i][...] = both[:rows]
            outs[2 * i + 1][...] = both[rows:]


def split(left, right, dims, order, rows, others=()):
    width = right.shape[1 - dims[0][1][0]]

    def place(i):
        at = order[0]
        for n, r in enumerate(order):
            at = jnp.where(i == n, r, at)
        return at, 0

    used = (width, left.shape[1]) if dims == NT else (left.shape[1], width)
    out = pl.pallas_call(
        functools.partial(split_kernel, order, dims),
        grid=(len(order),),
        in_specs=[
            pl.BlockSpec((2 * rows, left.shape[1]), place),
            pl.BlockSpec(used, lambda i: (0, 0)),
        ]
        + [ANY] * len(others),
        out_specs=[pl.BlockSpec((rows, width), lambda i: (0, 0))] * (2 * len(order)),
        out_shape=[jax.ShapeDtypeStruct((rows, width), BF)] * (2 * len(order)),
        cost_estimate=cost(3 * len(order) + 2),
        compiler_params=pltpu.CompilerParams(vmem_limit_bytes=56 * 2**20),
    )(left, right, *others)
    return [tuple(out[2 * order.index(r) :][:2]) for r in range(len(order))]


def down_sums_kernel(inner_ref, top_ref, *refs):
    out_ref = refs[-1]
    count, size, _ = out_ref.shape
    found = dot(inner_ref[...], top_ref[...], TN).astype(BF)
    for z in range(count):
        out_ref[z] = found[z * size : (z + 1) * size]


def unit_sums_kernel(hidden_ref, grads_ref, *refs):
    out_ref = refs[-1]
    count, size, tile = out_ref.shape
    columns = grads_ref.shape[1] // tile
    depth = size // columns
    found = dot(hidden_ref[...], grads_ref[...], TN).astype(BF)
    for z in range(count):
        for b in range(columns):
            out_ref[z, b * depth : (b + 1) * depth, :] = found[
                z * depth : (z + 1) * depth, b * tile : (b + 1) * tile
            ]


def unit_sums(hidden, grads, layers, below, *others):
    tokens, width = hidden.shape
    tile = 256
    above = grads.shape[1] // tile * width // layers
    return pl.pallas_call(
        unit_sums_kernel,
        grid=(2,),
        in_specs=[
            pl.BlockSpec((tokens, width // 2), lambda i: (0, i)),
            pl.BlockSpec(grads.shape, lambda i: (0, 0)),
        ]
        + [ANY] * len(others),
        out_specs=pl.BlockSpec((layers // 2, above, tile), lambda i: (i, 0, 0)),
        out_shape=jax.ShapeDtypeStruct((layers, above + below, tile), BF),
        cost_estimate=cost(14),
        compiler_params=pltpu.CompilerParams(vmem_limit_bytes=56 * 2**20),
    )(hidden, grads, *others)


def down_sums(inner, tops, carried, *others):
    tokens, units = inner.shape
    width = tops.shape[1]
    layers, length, tile = carried.shape
    size = units // layers
    above = length - width // tile * size
    return pl.pallas_call(
        down_sums_kernel,
        grid=(width // tile,),
        in_specs=[
            pl.BlockSpec((tokens, units), lambda i: (0, 0)),
            pl.BlockSpec((tokens, tile), lambda i: (0, i)),
        ]
        + [ANY] * (1 + len(others)),
        out_specs=pl.BlockSpec((layers, size, tile), lambda i: (0, above // size + i, 0)),
        out_shape=jax.ShapeDtypeStruct(carried.shape, BF),
        input_output_aliases={2: 0},
        cost_estimate=cost(10),
        compiler_params=pltpu.CompilerParams(vmem_limit_bytes=56 * 2**20),
    )(inner, tops, carried, *others)


def part_sheet_kernel(sum_ref, *refs):
    heads_ref, out_ref = refs[-2:]
    owners, blocks, share, _ = heads_ref.shape
    depth = owners * share
    for b in range(blocks):
        block = sum_ref[b * depth : (b + 1) * depth].astype(F32)
        for p in range(owners):
            heads_ref[p, b] = block[p * share : (p + 1) * share].astype(BF)
    out_ref[...] = sum_ref[blocks * depth :]


def part_sheet(total_sum, share, *others):
    rows, tile = total_sum.shape
    blocks = 6 * HP // tile
    return pl.pallas_call(
        part_sheet_kernel,
        in_specs=[VMEM] + [ANY] * len(others),
        out_specs=[VMEM, VMEM],
        out_shape=[
            jax.ShapeDtypeStruct((8, blocks, share, tile), BF),
            jax.ShapeDtypeStruct((rows - blocks * 8 * share, tile), BF),
        ],
        cost_estimate=cost(2),
        compiler_params=pltpu.CompilerParams(vmem_limit_bytes=32 * 2**20),
    )(total_sum, *others)


def out_owner_kernel(piece_ref, out_ref):
    share, width = out_ref.shape
    size, tile = padded(share), piece_ref.shape[1]
    for i in range(width // tile):
        block = piece_ref[i * size : (i + 1) * size].astype(F32)
        out_ref[:, i * tile : (i + 1) * tile] = block[:share]


def out_owner(piece, share, width):
    return pl.pallas_call(
        out_owner_kernel,
        out_shape=jax.ShapeDtypeStruct((share, width), F32),
        cost_estimate=cost(2),
        compiler_params=pltpu.CompilerParams(vmem_limit_bytes=32 * 2**20),
    )(piece)


def out_sums_kernel(count, *refs):
    blocks, kept_ref, out_ref = refs[:count], refs[count], refs[-1]
    layers, size, _ = out_ref.shape
    found = [dot(kept_ref[i], ref[...], TN) for i, ref in enumerate(blocks)]
    found = functools.reduce(jnp.add, found).astype(BF)
    for z in range(layers):
        out_ref[z] = found[z * size : (z + 1) * size]


def head_sums_kernel(hidden_ref, grads_ref, rim_ref, lead_ref, *refs):
    out_ref = refs[-1]
    count, size, tile = out_ref.shape
    columns = grads_ref.shape[1] // tile
    depth = size // columns
    found = dot(hidden_ref[...], grads_ref[...], TN)
    more = dot(rim_ref[...], lead_ref[...], TN)
    skip = found.shape[1] - more.shape[1]
    found = jnp.concatenate([found[:, :skip], found[:, skip:] + more], axis=1).astype(BF)
    for z in range(count):
        for b in range(columns):
            out_ref[z, b * depth : (b + 1) * depth, :] = found[
                z * depth : (z + 1) * depth, b * tile : (b + 1) * tile
            ]


def head_sums(hidden, grad, rim, lead, layers, rows, *others):
    tokens, width = hidden.shape
    tile = 256
    above = grad.shape[1] // tile * width // layers
    whole = lambda i: (0, 0)
    return pl.pallas_call(
        head_sums_kernel,
        grid=(2,),
        in_specs=[
            pl.BlockSpec((tokens, width // 2), lambda i: (0, i)),
            pl.BlockSpec(grad.shape, whole),
            pl.BlockSpec((rim.shape[0], width // 2), lambda i: (0, i)),
            pl.BlockSpec(lead.shape, whole),
        ]
        + [ANY] * len(others),
        out_specs=pl.BlockSpec((layers // 2, above, tile), lambda i: (i, 0, 0)),
        out_shape=jax.ShapeDtypeStruct((layers, above + rows, tile), BF),
        cost_estimate=cost(11),
        compiler_params=pltpu.CompilerParams(vmem_limit_bytes=56 * 2**20),
    )(hidden, grad, rim, lead, *others)


def out_sums(blocks, kept, carried, *others):
    rows, width = blocks[0].shape
    count, _, depth = kept.shape
    layers, length, tile = carried.shape
    size = depth // layers
    above = length - width // tile * size
    return pl.pallas_call(
        functools.partial(out_sums_kernel, count),
        grid=(width // tile,),
        in_specs=[pl.BlockSpec((rows, tile), lambda i: (0, i))] * count
        + [pl.BlockSpec((count, rows, depth), lambda i: (0, 0, 0))]
        + [ANY] * (1 + len(others)),
        out_specs=pl.BlockSpec((layers, size, tile), lambda i: (0, above // size + i, 0)),
        out_shape=jax.ShapeDtypeStruct(carried.shape, BF),
        input_output_aliases={count + 1: 0},
        cost_estimate=cost(6),
        compiler_params=pltpu.CompilerParams(vmem_limit_bytes=32 * 2**20),
    )(*blocks, kept, carried, *others)


def leave_kernel(here_ref, x_ref, y_ref, own_ref, grad_ref, gain_ref, *refs):
    grad_hidden = here_ref[...] + x_ref[...].astype(F32) + y_ref[...].astype(F32)
    normed, factor = normalize(own_ref[...].astype(F32))
    refs[-1][...] = grad_ref[...] + norm_back(grad_hidden * gain_ref[...], normed, factor)


def leave(terms, own, grad_middle, gain, *others):
    return pl.pallas_call(
        leave_kernel,
        in_specs=[VMEM] * 6 + [ANY] * len(others),
        out_specs=VMEM,
        out_shape=jax.ShapeDtypeStruct(own.shape, F32),
        cost_estimate=cost(6),
        compiler_params=pltpu.CompilerParams(vmem_limit_bytes=32 * 2**20),
    )(*terms, own, grad_middle, gain, *others)


def mend_kernel(info_ref, tail_ref, back_ref, cur_ref, *refs):
    out_ref = refs[-1]
    out_ref[:, : 2 * HP] = cur_ref[:, : 2 * HP]
    out_ref[:, 2 * HP :] = (tail_ref[...] + back_ref[...].astype(F32)).astype(BF)


def mend(info, tail, back, grad_qkv, *others):
    rows, blocks = grad_qkv.shape[1], grad_qkv.shape[0] // 2
    side = pl.BlockSpec((None, WINDOW, 4 * HP), lambda s, info: (s, 0, 0))
    edge = pl.BlockSpec(
        (None, WINDOW, 6 * HP),
        lambda s, info: (2 * ((blocks - 1) ^ info[0]) + s, rows // WINDOW - 1, 0),
    )
    return pl.pallas_call(
        mend_kernel,
        grid_spec=pltpu.PrefetchScalarGridSpec(
            num_scalar_prefetch=1,
            grid=(2,),
            in_specs=[side, side, edge] + [ANY] * len(others),
            out_specs=edge,
        ),
        out_shape=jax.ShapeDtypeStruct(grad_qkv.shape, BF),
        cost_estimate=cost(2),
        input_output_aliases={3: 0},
    )(info, tail, back, grad_qkv, *others)


def first_key(at, rows):
    return min(at, rows + WINDOW - SPAN)


def shares_of(raws, cut, rows):
    row = lax.broadcasted_iota(jnp.int32, (SUB, SPAN), 0)
    col = lax.broadcasted_iota(jnp.int32, (SUB, SPAN), 1)
    seen = {}
    for at in range(0, rows, SUB):
        shift = at - first_key(at, rows)
        valid = (col > row + shift) & (col <= row + (shift + WINDOW))
        seen[at] = valid & (col >= cut) if at == 0 else valid
    scores = [jnp.where(seen[at], raw, MASKED) for at, raw in raws]
    peaks = [jnp.max(score, axis=-1, keepdims=True) for score in scores]
    powers = [jnp.exp((s - p) * (HD ** (-0.5))) for s, p in zip(scores, peaks)]
    totals = [jnp.sum(power, axis=-1, keepdims=True) for power in powers]
    return [power * (1.0 / total) for power, total in zip(powers, totals)]


def joined(prev_ref, halo_ref, cur_ref, at_first, lo):
    before = jnp.where(
        at_first, halo_ref[:, lo - 2 * HP : lo - HP], prev_ref[:, lo : lo + HP]
    )
    return jnp.concatenate([before, cur_ref[:, lo : lo + HP]], axis=0)


def tiles_of(rows):
    return [(h, at, first_key(at, rows)) for h in range(2) for at in range(0, rows, SUB)]


def attend_kernel(info_ref, cur_ref, prev_ref, halo_ref, *refs):
    flat_ref, kept_ref = refs[-2:]
    stream, block = pl.program_id(0), pl.program_id(1)
    at_first = block == 0
    cut = jnp.where(at_first & (info_ref[2 + stream] == 1), WINDOW, 0)
    rows = cur_ref.shape[0]
    tiles = tiles_of(rows)
    keys = [joined(prev_ref, halo_ref, cur_ref, at_first, (2 + h) * HP) for h in range(2)]
    values = [joined(prev_ref, halo_ref, cur_ref, at_first, (4 + h) * HP) for h in range(2)]
    raws = [
        (at, dot(cur_ref[at : at + SUB, h * HP : (h + 1) * HP], keys[h][lo : lo + SPAN], NT))
        for h, at, lo in tiles
    ]
    shares = [share.astype(BF) for share in shares_of(raws, cut, rows)]
    mixes = [dot(share, values[h][lo : lo + SPAN]) for share, (h, at, lo) in zip(shares, tiles)]
    for mixed, (h, at, lo) in zip(mixes, tiles):
        mixed = mixed.astype(BF)
        flat_ref[at : at + SUB, h * HP : (h + 1) * HP] = mixed
        kept_ref[at : at + SUB, h * HP : (h + 1) * HP] = mixed


def attend(qkv, halo, info, *others):
    rows, blocks = qkv.shape[1], qkv.shape[0] // 2
    mine = lambda s, b, info: (2 * (b ^ info[0]) + s, 0, 0)
    before = lambda s, b, info: (2 * (jnp.maximum(b - 1, 0) ^ info[0]) + s, rows // WINDOW - 1, 0)
    spec = pltpu.PrefetchScalarGridSpec(
        num_scalar_prefetch=1,
        grid=(2, blocks),
        in_specs=[
            pl.BlockSpec((None, rows, 6 * HP), mine),
            pl.BlockSpec((None, WINDOW, 6 * HP), before),
            pl.BlockSpec((None, WINDOW, 4 * HP), lambda s, b, info: (s, 0, 0)),
        ]
        + [ANY] * len(others),
        out_specs=[
            pl.BlockSpec((None, rows, 2 * HP), lambda s, b, info: (2 * b + (s ^ info[1]), 0, 0)),
            pl.BlockSpec((None, rows, 2 * HP), mine),
        ],
    )
    shape = jax.ShapeDtypeStruct((2 * blocks, rows, 2 * HP), BF)
    return pl.pallas_call(
        attend_kernel,
        grid_spec=spec,
        out_shape=[shape, pltpu.HBM(shape.shape, shape.dtype)],
        cost_estimate=cost(8),
        compiler_params=pltpu.CompilerParams(vmem_limit_bytes=32 * 2**20),
    )(info, qkv, qkv, halo, *others)


def attend_back_kernel(
    info_ref, cur_ref, prev_ref, halo_ref, top_ref, *refs
):
    out_ref, tail_ref, lead_ref, keep, acc = refs[-5:]
    stream, step = pl.program_id(0), pl.program_id(1)
    blocks = pl.num_programs(1)
    at_first = step == blocks - 1
    cut = jnp.where(at_first & (info_ref[2 + stream] == 1), WINDOW, 0)
    rows = cur_ref.shape[0]

    @pl.when(step == 0)
    def _():
        keep[...] = jnp.zeros_like(keep)

    acc[...] = jnp.zeros_like(acc)
    tiles = tiles_of(rows)
    keys = [joined(prev_ref, halo_ref, cur_ref, at_first, (2 + h) * HP) for h in range(2)]
    values = [joined(prev_ref, halo_ref, cur_ref, at_first, (4 + h) * HP) for h in range(2)]
    queries = [cur_ref[at : at + SUB, h * HP : (h + 1) * HP] for h, at, lo in tiles]
    tops = [top_ref[at : at + SUB, h * HP : (h + 1) * HP] for h, at, lo in tiles]
    raws = [
        (at, dot(query, keys[h][lo : lo + SPAN], NT)) for query, (h, at, lo) in zip(queries, tiles)
    ]
    grads = [dot(top, values[h][lo : lo + SPAN], NT) for top, (h, at, lo) in zip(tops, tiles)]
    shares = shares_of(raws, cut, rows)
    spent = [
        jnp.sum(share * grad, axis=-1, keepdims=True) for share, grad in zip(shares, grads)
    ]
    grads = [
        (share * ((grad - sum_) * (HD ** (-0.5)))).astype(BF)
        for share, grad, sum_ in zip(shares, grads, spent)
    ]
    shares = [share.astype(BF) for share in shares]
    for share, grad, query, top, (h, at, lo) in zip(shares, grads, queries, tops, tiles):
        left, right = h * HP, (h + 1) * HP
        out_ref[at : at + SUB, left:right] = dot(grad, keys[h][lo : lo + SPAN]).astype(BF)
        acc[lo : lo + SPAN, left:right] += dot(grad, query, TN)
        acc[lo : lo + SPAN, 2 * HP + left : 2 * HP + right] += dot(share, top, TN)
    last = acc[rows : rows + WINDOW, :] + keep[...]
    out_ref[: rows - WINDOW, 2 * HP :] = acc[WINDOW:rows, :].astype(BF)
    out_ref[rows - WINDOW :, 2 * HP :] = last.astype(BF)
    keep[...] = acc[:WINDOW, :]

    @pl.when(step == 0)
    def _():
        tail_ref[...] = last

    @pl.when(at_first)
    def _():
        lead_ref[...] = acc[:WINDOW, :].astype(BF)


def attend_back(qkv, halo, top, info, *others):
    rows, blocks = qkv.shape[1], qkv.shape[0] // 2
    at = lambda t: blocks - 1 - t
    mine = lambda s, t, info: (2 * (at(t) ^ info[0]) + s, 0, 0)
    before = lambda s, t, info: (
        2 * (jnp.maximum(at(t) - 1, 0) ^ info[0]) + s,
        rows // WINDOW - 1,
        0,
    )
    side = lambda s, t, info: (s, 0, 0)
    spec = pltpu.PrefetchScalarGridSpec(
        num_scalar_prefetch=1,
        grid=(2, blocks),
        in_specs=[
            pl.BlockSpec((None, rows, 6 * HP), mine),
            pl.BlockSpec((None, WINDOW, 6 * HP), before),
            pl.BlockSpec((None, WINDOW, 4 * HP), side),
            pl.BlockSpec(
                (None, rows, 2 * HP), lambda s, t, info: (2 * at(t) + (s ^ info[1]), 0, 0)
            ),
        ]
        + [ANY] * len(others),
        out_specs=[
            pl.BlockSpec((None, rows, 6 * HP), mine),
            pl.BlockSpec((None, WINDOW, 4 * HP), side),
            pl.BlockSpec((None, WINDOW, 4 * HP), side),
        ],
        scratch_shapes=[
            pltpu.VMEM((WINDOW, 4 * HP), F32),
            pltpu.VMEM((rows + WINDOW, 4 * HP), F32),
        ],
    )
    return pl.pallas_call(
        attend_back_kernel,
        grid_spec=spec,
        out_shape=[
            jax.ShapeDtypeStruct(qkv.shape, BF),
            jax.ShapeDtypeStruct(halo.shape, F32),
            jax.ShapeDtypeStruct(halo.shape, BF),
        ],
        cost_estimate=cost(17),
        compiler_params=pltpu.CompilerParams(vmem_limit_bytes=32 * 2**20),
    )(info, qkv, qkv, halo, top, *others)


def body(
    inputs,
    starts,
    attn_gain,
    query_weight,
    key_weight,
    value_weight,
    out_weight,
    ffn_gain,
    gate_weight,
    up_weight,
    down_weight,
    cotangent,
):
    rows, width = inputs.shape[1:]
    layers = lax.axis_size("z")
    devices = 8 * layers
    share = query_weight.shape[0]
    part = down_weight.shape[0]
    units = -(-part // 16) * 16 * layers
    me_z = lax.axis_index("z")
    me_block = 2 * lax.axis_index("y") + lax.axis_index("x")
    me_core = lax.axis_index("c")

    own = inputs[0]
    top = cotangent[0]
    own_gains = jnp.stack([attn_gain, ffn_gain]).astype(F32)
    heads = head_sheet(query_weight, key_weight, value_weight, own_gains, starts)
    down = jnp.pad(down_weight, ((0, units // layers - part), (0, 0)))
    down = lax.all_gather(down, "z", axis=0, tiled=True)
    heads = lax.all_to_all(heads, PLANE, 0, 0, tiled=True)
    opened = heads[:2, 0, extra_column(2, share)].astype(jnp.int32)
    opened = jnp.where(me_core == 0, opened, opened[::-1])
    info = jnp.concatenate([jnp.stack([me_block, me_core]), opened, me_z[None]]).astype(jnp.int32)
    ready = held(own, heads)
    from_x, from_y = neighbours(ready)
    streams = both_cores([own, from_x, from_y, across(ready)])
    top_ready = held(top, from_x, from_y)
    attn_weight = attn_sheet(heads, out_weight, down, from_x, from_y)
    attn_weight = lax.all_gather(attn_weight, "z", axis=0, tiled=True)
    stream = jnp.concatenate(streams, axis=0)
    factor = normalize(stream.astype(F32))[1]
    sheet = unit_sheet(gate_weight, up_weight, layers, part, units, heads)
    sheet = lax.all_to_all(sheet, PLANE, 0, 0, tiled=True).reshape(8 * share, 2 * units)
    gate_up = lax.all_gather(sheet, "z", axis=0, tiled=True)
    tops = both_cores([top, *neighbours(top_ready), across(top_ready)])

    hidden1, qkv, gains = enter(stream, factor, attn_weight, rows, share, *tops[2::2])
    gain_attn, gain_ffn = gains[0:1], gains[1:2]
    qkv = qkv.reshape(8, rows, 6 * HP)
    last = 2 * (3 ^ me_block)
    rim = lax.dynamic_slice(qkv, (last, rows - WINDOW, 2 * HP), (2, WINDOW, 4 * HP))
    halo = lax.ppermute(rim, "z", [(i, i + 1) for i in range(layers - 1)])
    own_out = attn_weight[:, 6 * HP :]
    from_x, from_y = neighbours(own_out)
    far = diagonal(from_x, from_y, halo)
    flat, kept = attend(qkv, halo, info)
    full_out = both_cores([own_out, from_x, from_y, join(*far, flat)])
    full_out = out_sheet(full_out, info, layers)
    rim = lax.dynamic_slice(
        hidden1.reshape(8, rows, width), (last, rows - WINDOW, 0), (2, WINDOW, width)
    )
    rim = lax.ppermute(rim, "z", [(i, i + 1) for i in range(layers - 1)])
    mixed = lax.all_to_all(flat, PLANE, 0, 0, tiled=True)
    middle, hidden2 = project(mixed, full_out, own, gain_ffn)

    blocks = both_cores([hidden2, *neighbours(hidden2)])
    far = across(hidden2)
    carried, near = ffn(blocks, tops[:6], gate_up, down, 0)
    far = held(far, carried[0])
    (inner, grads, hidden2, tops), far = ffn(
        both_cores([far]), tops[6:], gate_up, down, 3, carried
    )
    terms, sent, far = plane_sum([near[:2], near[2:4], near[4:], far])
    ffn_part = unit_sums(hidden2, grads, layers, width // 256 * units // layers, far, rim)
    ffn_part = down_sums(inner, tops, ffn_part, *sent)
    out_parts = split(inner, down, NN, (3, 2, 1, 0), rows, [ffn_part])
    ffn_sum = lax.psum_scatter(ffn_part, "z", scatter_dimension=0, tiled=True)[0]

    grad_mixed, grad_middle, grad_branch = unproject(
        terms, middle, top, gain_ffn, full_out, out_parts[3][0]
    )

    grad_mixed = lax.all_to_all(grad_mixed, PLANE, 0, 0, tiled=True)
    from_x, from_y = neighbours(grad_branch)
    grad_qkv, tail, lead = attend_back(qkv, halo, grad_mixed, info)
    back = lax.ppermute(lead, "z", [(i + 1, i) for i in range(layers - 1)])
    out_terms, sent, _ = plane_sum(out_parts, tail)
    attn_part = head_sums(
        hidden1,
        grad_qkv.reshape(8 * rows, 6 * HP),
        rim.reshape(2 * WINDOW, width),
        lead.reshape(2 * WINDOW, 4 * HP),
        layers,
        8 * share,
    )
    branches = join(*diagonal(from_x, from_y, attn_part))
    branches = both_cores([grad_branch, from_x, from_y, branches])
    grad_qkv = mend(info, tail, back, grad_qkv, attn_part).reshape(8 * rows, 6 * HP)
    attn_part = out_sums(branches, kept, attn_part, grad_qkv, *sent)
    attn_sum = lax.psum_scatter(attn_part, "z", scatter_dimension=0, tiled=True)[0]
    layer_out = (middle + total(out_terms)).astype(BF)
    above = 2 * units // 256 * 8 * share
    gate_up_sum = ffn_sum[:above].reshape(-1, 8, share, 256).swapaxes(0, 1)
    gate_up_sum = lax.all_to_all(gate_up_sum, PLANE, 0, 0, tiled=True)
    gate_grad, up_grad, ffn_gain_grad = unit_owner(
        gate_up_sum, (gate_weight, up_weight), own_gains[1:2], layers, part
    )
    down_grad = ffn_sum[above:].reshape(width // 256, -1, 256).swapaxes(0, 1)
    down_grad = down_grad[:part].reshape(part, width).astype(F32)
    parts = split(grad_qkv, attn_weight, NT, (3, 2, 1, 0), rows, [attn_part])
    terms, _, _ = plane_sum(parts, *out_terms[1:])
    input_grad = leave(terms, own, grad_middle, gain_attn)

    qkv_sum, out_sum = part_sheet(attn_sum, share, input_grad, gate_grad, layer_out)
    qkv_sum = lax.all_to_all(qkv_sum, PLANE, 0, 0, tiled=True)
    query_grad, key_grad, value_grad, attn_gain_grad = head_owner(
        qkv_sum, (query_weight, key_weight, value_weight), own_gains[0:1]
    )
    route = [(8 * z + p, layers * p + z) for z in range(layers) for p in range(8)]
    output_grad = out_owner(lax.ppermute(out_sum, ALL, route), share, width)
    return (
        layer_out[None],
        input_grad[None],
        attn_gain_grad[0],
        query_grad,
        key_grad,
        value_grad,
        output_grad,
        ffn_gain_grad[0],
        gate_grad,
        up_grad,
        down_grad,
    )


def solution(mesh):
    blocks = mesh.shape["seq"]
    fine = Mesh(mesh.devices.reshape(blocks // 4, 2, 2, 2), ALL)
    tokens = P("c", ("z", "y", "x"), None)
    weight = P(ALL, None)
    gain = P(ALL)
    in_specs = (
        tokens,
        P("c", ("z", "y", "x")),
        gain,
        weight,
        weight,
        weight,
        weight,
        gain,
        weight,
        weight,
        weight,
        tokens,
    )
    out_specs = (
        tokens,
        tokens,
        gain,
        weight,
        weight,
        weight,
        weight,
        gain,
        weight,
        weight,
        weight,
    )
    return jax.shard_map(body, mesh=fine, in_specs=in_specs, out_specs=out_specs, check_vma=False)
```
